32 devices in a mesh: dp: 8 (over y, x, core), ns: 4 (over z).
Axes of the slice: x: 2, y: 2, z: 4, core: 2. Of those that a mesh axis runs over, the one named last changes fastest.
Arguments:
- image_tokens: bfloat16 [128, 50, 768], P(('dp', 'ns')), may hold values from -6 to 6
- text_tokens: bfloat16 [256, 77, 512], P(('dp', 'ns')), may hold values from -6 to 6
- caption_image: int32 [256], replicated, may hold values from 0 to 127, as said below
- caption_length: int32 [256], P(('dp', 'ns')), may hold values from 2 to 77, as said below
- image_attention: float32 [2304, 768], P('ns'), may hold values from -0.21875 to 0.21875
- image_output: float32 [768, 768], P('ns'), may hold values from -0.5 to 0.5
- image_expand: float32 [3072, 768], P('ns'), may hold values from -0.21875 to 0.21875
- image_shrink: float32 [3072, 768], P('ns'), may hold values from -0.109375 to 0.109375
- image_embedding: float32 [768, 512], P('ns'), may hold values from -0.21875 to 0.21875
- text_attention: float32 [1536, 512], P('ns'), may hold values from -0.25 to 0.25
- text_output: float32 [512, 512], P('ns'), may hold values from -0.625 to 0.625
- text_expand: float32 [2048, 512], P('ns'), may hold values from -0.25 to 0.25
- text_shrink: float32 [2048, 512], P('ns'), may hold values from -0.125 to 0.125
- text_embedding: float32 [512, 512], P('ns'), may hold values from -0.25 to 0.25
- image_gains: float32 [3, 768], replicated, may hold values from 0.5 to 1.5
- text_gains: float32 [3, 512], replicated, may hold values from 0.5 to 1.5
- image_attention_momentum: float32 [2304, 768], P('ns'), may hold values from -2 to 2
- image_output_momentum: float32 [768, 768], P('ns'), may hold values from -2 to 2
- image_expand_momentum: float32 [3072, 768], P('ns'), may hold values from -2 to 2
- image_shrink_momentum: float32 [3072, 768], P('ns'), may hold values from -2 to 2
- image_embedding_momentum: float32 [768, 512], P('ns'), may hold values from -5 to 5
- text_attention_momentum: float32 [1536, 512], P('ns'), may hold values from -2 to 2
- text_output_momentum: float32 [512, 512], P('ns'), may hold values from -2 to 2
- text_expand_momentum: float32 [2048, 512], P('ns'), may hold values from -2 to 2
- text_shrink_momentum: float32 [2048, 512], P('ns'), may hold values from -2 to 2
- text_embedding_momentum: float32 [512, 512], P('ns'), may hold values from -5 to 5
- image_gains_momentum: float32 [3, 768], replicated, may hold values from -5 to 5
- text_gains_momentum: float32 [3, 512], replicated, may hold values from -5 to 5
Outputs:
- loss: float32 [1], replicated
- image_token_grad: bfloat16 [128, 50, 768], P(('dp', 'ns'))
- text_token_grad: bfloat16 [256, 77, 512], P(('dp', 'ns'))
- next_image_attention_momentum: float32 [2304, 768], P('ns')
- next_image_output_momentum: float32 [768, 768], P('ns')
- next_image_expand_momentum: float32 [3072, 768], P('ns')
- next_image_shrink_momentum: float32 [3072, 768], P('ns')
- next_image_embedding_momentum: float32 [768, 512], P('ns')
- next_text_attention_momentum: float32 [1536, 512], P('ns')
- next_text_output_momentum: float32 [512, 512], P('ns')
- next_text_expand_momentum: float32 [2048, 512], P('ns')
- next_text_shrink_momentum: float32 [2048, 512], P('ns')
- next_text_embedding_momentum: float32 [512, 512], P('ns')
- next_image_attention: float32 [2304, 768], P('ns')
- next_image_output: float32 [768, 768], P('ns')
- next_image_expand: float32 [3072, 768], P('ns')
- next_image_shrink: float32 [3072, 768], P('ns')
- next_image_embedding: float32 [768, 512], P('ns')
- next_text_attention: float32 [1536, 512], P('ns')
- next_text_output: float32 [512, 512], P('ns')
- next_text_expand: float32 [2048, 512], P('ns')
- next_text_shrink: float32 [2048, 512], P('ns')
- next_text_embedding: float32 [512, 512], P('ns')
- next_image_gains_momentum: float32 [3, 768], replicated
- next_text_gains_momentum: float32 [3, 512], replicated
- next_image_gains: float32 [3, 768], replicated
- next_text_gains: float32 [3, 512], replicated
The draws below stay inside these ranges and needn't reach their ends.
Inputs may be any that keep to these rules, and one draw needn't show every extreme that they name: `caption_image`: each image is named by 1 to 5 captions, some image by exactly 5; each aligned group of four images (0 to 3, 4 to 7, and so on) is named by 8 captions together. `caption_length`: in every draw some caption has length 77.
All inputs are finite; a program needn't handle non-finite values.
Results may differ from the reference program's by a relative error of at most 0.015.
Values may be sent and summed in bfloat16 or wider, within the bound.
No kernel may reach another device: no remote copies, remote signals or barrier semaphores. Data moves between devices by JAX's collectives and lax.ppermute only.
A program may use at most 256 MiB of HBM per device.

```python
import math
import jax
import jax.numpy as jnp
from jax import lax

DI = 768
HI = 12
FI = 3072
DT = 512
HT = 8
FT = 2048
PE = 512
PI = 50
PT = 77
IMG_DEV = 4
NS_ITERS = 3
IMAGES = 128
CAPTIONS = 256
N_DP = 8
N_NS = 4


def permute_four(subkey):
    return jax.random.permutation(subkey, 4)


def draw_caption_image(key, part):
    key = jax.random.fold_in(key, 5)
    pick_key, order_key, shuffle_key = jax.random.split(key, 3)
    groups = IMAGES // 4
    table = jnp.array([[5, 1, 1, 1], [2, 2, 2, 2], [3, 3, 1, 1], [4, 2, 1, 1], [3, 2, 2, 1]], jnp.int32)
    chosen = jax.random.randint(pick_key, (groups,), 0, 5)
    chosen = chosen.at[0].set(0)
    counted = table[chosen]
    orders = jax.vmap(permute_four)(jax.random.split(order_key, groups))
    counted = jnp.take_along_axis(counted, orders, 1)
    ending = jnp.cumsum(counted, 1)
    slots_all = jnp.arange(8, dtype=jnp.int32)
    within = jnp.sum((slots_all[None, :, None] >= ending[:, None, :]).astype(jnp.int32), 2)
    images = (4 * jnp.arange(groups, dtype=jnp.int32)[:, None] + within).reshape(-1)
    return images[jax.random.permutation(shuffle_key, 8 * groups)]


def draw_caption_length(key, part):
    key = jax.random.fold_in(key, 9)
    length_key, place_key = jax.random.split(key)
    lengths = jax.random.randint(length_key, (CAPTIONS,), 2, PT + 1)
    longest = jax.random.randint(place_key, (), 0, CAPTIONS)
    return jnp.where(jnp.arange(CAPTIONS, dtype=jnp.int32) == longest, PT, lengths).astype(jnp.int32)


def block_scale(own_key, dims, cuts, least, top_value):
    level = 1.0
    for axis_at, shards_of in cuts:
        draws = jax.random.uniform(jax.random.fold_in(jax.random.fold_in(own_key, 6), axis_at), (shards_of,), jnp.float32, least / len(cuts), top_value / len(cuts))
        level = level * jnp.repeat(jnp.exp(draws), dims[axis_at] // shards_of).reshape((-1,) + (1,) * (len(dims) - 1 - axis_at))
    return level


def centred(key, extent, scale, bound, cuts=(), kind=jnp.bfloat16):
    drawn = jax.random.normal(key, extent, jnp.float32) * scale
    if len(cuts) > 0:
        drawn = block_scale(key, extent, cuts, -0.22, 0.18) * drawn
    return jnp.clip(drawn, min=-bound, max=bound).astype(kind)


def setup_inputs(seed: int = 0) -> dict:
    streams_of = jax.random.split(jax.random.key(seed), 29)
    image_tokens = centred(streams_of[0], (IMAGES, PI, DI), 1.0, 6.0, ((0, 32),))
    text_tokens = centred(streams_of[1], (CAPTIONS, PT, DT), 1.0, 6.0, ((0, 32),))
    caption_image = draw_caption_image(jax.random.fold_in(streams_of[28], 71), 0)
    caption_length = draw_caption_length(jax.random.fold_in(streams_of[28], 71), 0)
    image_attention = centred(streams_of[4], (3 * DI, DI), DI ** -0.5, 0.21875, ((0, 4),), jnp.float32)
    image_output = centred(streams_of[5], (DI, DI), (DI // 7) ** -0.5, 0.5, ((0, 4),), jnp.float32)
    image_expand = centred(streams_of[6], (FI, DI), DI ** -0.5, 0.21875, ((0, 4),), jnp.float32)
    image_shrink = centred(streams_of[7], (FI, DI), FI ** -0.5, 0.109375, ((0, 4),), jnp.float32)
    image_embedding = centred(streams_of[8], (DI, PE), DI ** -0.5, 0.21875, ((0, 4),), jnp.float32)
    text_attention = centred(streams_of[9], (3 * DT, DT), DT ** -0.5, 0.25, ((0, 4),), jnp.float32)
    text_output = centred(streams_of[10], (DT, DT), (DT // 6) ** -0.5, 0.625, ((0, 4),), jnp.float32)
    text_expand = centred(streams_of[11], (FT, DT), DT ** -0.5, 0.25, ((0, 4),), jnp.float32)
    text_shrink = centred(streams_of[12], (FT, DT), FT ** -0.5, 0.125, ((0, 4),), jnp.float32)
    text_embedding = centred(streams_of[13], (DT, PE), DT ** -0.5, 0.25, ((0, 4),), jnp.float32)
    image_gains = jnp.clip(1.0 + 0.1 * jax.random.normal(streams_of[14], (3, DI), jnp.float32), 0.5, 1.5)
    text_gains = jnp.clip(1.0 + 0.1 * jax.random.normal(streams_of[15], (3, DT), jnp.float32), 0.5, 1.5)
    image_attention_momentum = centred(streams_of[16], (3 * DI, DI), (0.08 * (IMG_DEV * N_DP * N_NS) ** 0.5 * PI ** -0.5), 2.0, ((0, 4),), jnp.float32)
    image_output_momentum = centred(streams_of[17], (DI, DI), (0.08 * (IMG_DEV * N_DP * N_NS) ** 0.5 * PI ** -0.5), 2.0, ((0, 4),), jnp.float32)
    image_expand_momentum = centred(streams_of[18], (FI, DI), (0.08 * (IMG_DEV * N_DP * N_NS) ** 0.5 * PI ** -0.5), 2.0, ((0, 4),), jnp.float32)
    image_shrink_momentum = centred(streams_of[19], (FI, DI), (0.08 * (IMG_DEV * N_DP * N_NS) ** 0.5 * PI ** -0.5), 2.0, ((0, 4),), jnp.float32)
    image_embedding_momentum = centred(streams_of[20], (DI, PE), (0.2 * (IMG_DEV * N_DP * N_NS) ** 0.5 * PI ** -0.5), 5.0, ((0, 4),), jnp.float32)
    text_attention_momentum = centred(streams_of[21], (3 * DT, DT), (0.08 * (2 * IMG_DEV * N_DP * N_NS) ** 0.5 * PT ** -0.5), 2.0, ((0, 4),), jnp.float32)
    text_output_momentum = centred(streams_of[22], (DT, DT), (0.08 * (2 * IMG_DEV * N_DP * N_NS) ** 0.5 * PT ** -0.5), 2.0, ((0, 4),), jnp.float32)
    text_expand_momentum = centred(streams_of[23], (FT, DT), (0.08 * (2 * IMG_DEV * N_DP * N_NS) ** 0.5 * PT ** -0.5), 2.0, ((0, 4),), jnp.float32)
    text_shrink_momentum = centred(streams_of[24], (FT, DT), (0.08 * (2 * IMG_DEV * N_DP * N_NS) ** 0.5 * PT ** -0.5), 2.0, ((0, 4),), jnp.float32)
    text_embedding_momentum = centred(streams_of[25], (DT, PE), (0.2 * (2 * IMG_DEV * N_DP * N_NS) ** 0.5 * PT ** -0.5), 5.0, ((0, 4),), jnp.float32)
    image_gains_momentum = centred(streams_of[26], (3, DI), (0.03 * (IMG_DEV * N_DP * N_NS) ** 0.5), 5.0, (), jnp.float32)
    text_gains_momentum = centred(streams_of[27], (3, DT), (0.03 * (IMG_DEV * N_DP * N_NS) ** 0.5), 5.0, (), jnp.float32)
    return dict(image_tokens=image_tokens, text_tokens=text_tokens, caption_image=caption_image, caption_length=caption_length, image_attention=image_attention, image_output=image_output, image_expand=image_expand, image_shrink=image_shrink, image_embedding=image_embedding, text_attention=text_attention, text_output=text_output, text_expand=text_expand, text_shrink=text_shrink, text_embedding=text_embedding, image_gains=image_gains, text_gains=text_gains, image_attention_momentum=image_attention_momentum, image_output_momentum=image_output_momentum, image_expand_momentum=image_expand_momentum, image_shrink_momentum=image_shrink_momentum, image_embedding_momentum=image_embedding_momentum, text_attention_momentum=text_attention_momentum, text_output_momentum=text_output_momentum, text_expand_momentum=text_expand_momentum, text_shrink_momentum=text_shrink_momentum, text_embedding_momentum=text_embedding_momentum, image_gains_momentum=image_gains_momentum, text_gains_momentum=text_gains_momentum)


@jax.custom_vjp
def low(v):
    return lax.optimization_barrier(v.astype(jnp.bfloat16)).astype(jnp.float32)

@jax.custom_vjp
def low_back(v):
    return v

def low_keep(v):
    return (low(v), None)

def low_pass(kept, grad):
    return (grad,)

def back_keep(v):
    return (v, None)

def back_low(kept, grad):
    return (low(grad),)
low.defvjp(low_keep, low_pass)
low_back.defvjp(back_keep, back_low)
NORM_EPS = 1e-05
UNIT_EPS = 1e-06
SIM_SCALE = 30.0
MOMENTUM = 0.95
RATE = 0.5
GAIN_RATE = 0.5
COEF_A = 3.4445
COEF_B = -4.775
COEF_C = 2.0315
MASKED = -1000000000.0
HIGH = lax.Precision.HIGHEST

def both_ways(values):
    return low(low_back(values))

def layer_norm(values, gain):
    center = lax.optimization_barrier(jnp.mean(values, -1, keepdims=True))
    shifted = values - center
    spread = lax.optimization_barrier(jnp.mean(shifted * shifted, -1, keepdims=True))
    return shifted * lax.rsqrt(spread + NORM_EPS) * gain

def quick_gelu(values):
    return values * jax.nn.sigmoid(1.702 * values)

def times_t(left, right):
    return lax.dot_general(left, right, (((left.ndim - 1,), (1,)), ((), ())), precision=HIGH, preferred_element_type=jnp.float32)

def times(left, right):
    return lax.dot_general(left, right, (((left.ndim - 1,), (0,)), ((), ())), precision=HIGH, preferred_element_type=jnp.float32)

def tower(tokens, lengths, gains, weights, heads, causal):
    attention, output, expand, shrink, embedding = weights
    seq_count, seq_span, model_width = tokens.shape
    head_size = model_width // heads
    normed = low(layer_norm(tokens, gains[0]))
    packed = both_ways(times_t(normed, attention)).reshape(seq_count, seq_span, 3, heads, head_size)
    queries, keys_all, values_all = (packed[:, :, 0], packed[:, :, 1], packed[:, :, 2])
    scores = low_back(jnp.einsum('blhd,bmhd->bhlm', queries, keys_all, precision=HIGH) * head_size ** (-0.5))
    if causal:
        rows_at = lax.broadcasted_iota(jnp.int32, (seq_span, seq_span), 0)
        cols_at = lax.broadcasted_iota(jnp.int32, (seq_span, seq_span), 1)
        scores = jnp.where(cols_at <= rows_at, scores, MASKED)
    softmaxed = low(jax.nn.softmax(scores, axis=-1))
    attended = both_ways(jnp.einsum('bhlm,bmhd->blhd', softmaxed, values_all, precision=HIGH).reshape(seq_count, seq_span, model_width))
    first_sum = tokens + low_back(times_t(attended, output))
    second = low(layer_norm(first_sum, gains[1]))
    activated = low(quick_gelu(low_back(times_t(second, expand))))
    second_sum = first_sum + low_back(times(activated, shrink))
    valid_mask = (lax.broadcasted_iota(jnp.int32, (seq_count, seq_span), 1) < lengths[:, None]).astype(jnp.float32)
    pooled = lax.optimization_barrier(jnp.sum(second_sum * valid_mask[:, :, None], 1)) / lax.optimization_barrier(jnp.sum(valid_mask, 1))[:, None]
    final = low(layer_norm(pooled, gains[2]))
    embedded = low_back(times(final, embedding))
    return low(embedded * lax.rsqrt(lax.optimization_barrier(jnp.sum(embedded * embedded, -1, keepdims=True)) + UNIT_EPS))

def run_tower(tokens, lengths, gains, weights, heads, causal, group_size):
    row_total = tokens.shape[0]
    grouped = (tokens.reshape((row_total // group_size, group_size) + tokens.shape[1:]), lengths.reshape(row_total // group_size, group_size))

    def one_group(pieces):
        return tower(pieces[0], pieces[1], gains, weights, heads, causal)
    result = lax.map(jax.checkpoint(one_group), grouped)
    return result.reshape(row_total, result.shape[-1])

def objective(image_input, text_input, image_gain, text_gain, masters, caption_image, caption_length):
    lowered = [low(master) for master in masters]
    image_count = image_input.shape[0]
    caption_count = text_input.shape[0]
    image_lengths = jnp.full((image_count,), image_input.shape[1], jnp.int32)
    image_units = run_tower(image_input, image_lengths, image_gain, lowered[:5], HI, False, math.gcd(image_count, 64))
    text_units = run_tower(text_input, caption_length, text_gain, lowered[5:], HT, True, math.gcd(caption_count, 32))
    similar = times_t(image_units, text_units) * SIM_SCALE
    matches = (caption_image[None, :] == jnp.arange(image_count, dtype=jnp.int32)[:, None]).astype(jnp.float32)
    per_image = lax.optimization_barrier(jnp.sum(matches, 1))
    image_terms = jax.scipy.special.logsumexp(similar, axis=1) - lax.optimization_barrier(jnp.sum(similar * matches, 1)) / per_image
    caption_terms = jax.scipy.special.logsumexp(similar, axis=0) - lax.optimization_barrier(jnp.sum(similar * matches, 0))
    return 0.5 * jnp.sum(image_terms) + 0.5 * (image_count / caption_count) * jnp.sum(caption_terms)

def muon(master, moment, gradient):
    fresh = MOMENTUM * moment + gradient
    row_count, col_count = master.shape
    current = fresh / (jnp.sqrt(jnp.sum(fresh * fresh)) + 1e-07)
    for step_index in range(NS_ITERS):
        square = lax.dot_general(current, current, (((0,), (0,)), ((), ())), precision=HIGH, preferred_element_type=jnp.float32)
        poly = COEF_B * square + COEF_C * jnp.dot(square, square, precision=HIGH)
        current = COEF_A * current + jnp.dot(current, poly, precision=HIGH)
    return (fresh, master - RATE * math.sqrt(row_count / col_count) * current)

def reference(image_tokens, text_tokens, caption_image, caption_length, image_attention, image_output, image_expand, image_shrink, image_embedding, text_attention, text_output, text_expand, text_shrink, text_embedding, image_gains, text_gains, image_attention_momentum, image_output_momentum, image_expand_momentum, image_shrink_momentum, image_embedding_momentum, text_attention_momentum, text_output_momentum, text_expand_momentum, text_shrink_momentum, text_embedding_momentum, image_gains_momentum, text_gains_momentum):
    masters = (image_attention, image_output, image_expand, image_shrink, image_embedding, text_attention, text_output, text_expand, text_shrink, text_embedding)
    moments = (image_attention_momentum, image_output_momentum, image_expand_momentum, image_shrink_momentum, image_embedding_momentum, text_attention_momentum, text_output_momentum, text_expand_momentum, text_shrink_momentum, text_embedding_momentum)

    def loss_of(image_input, text_input, image_gain, text_gain, weights):
        return objective(image_input, text_input, image_gain, text_gain, weights, caption_image, caption_length)
    summed, pullback = jax.vjp(loss_of, image_tokens.astype(jnp.float32), text_tokens.astype(jnp.float32), image_gains, text_gains, masters)
    image_grad, text_grad, image_gain_grad, text_gain_grad, weight_grads = pullback(jnp.ones_like(summed))
    updates = [muon(master, moment, gradient) for master, moment, gradient in zip(masters, moments, weight_grads)]
    image_gain_next = MOMENTUM * image_gains_momentum + image_gain_grad
    text_gain_next = MOMENTUM * text_gains_momentum + text_gain_grad
    loss = jnp.reshape(summed / image_tokens.shape[0], (1,))
    return (loss, image_grad.astype(jnp.bfloat16), text_grad.astype(jnp.bfloat16), updates[0][0], updates[1][0], updates[2][0], updates[3][0], updates[4][0], updates[5][0], updates[6][0], updates[7][0], updates[8][0], updates[9][0], updates[0][1], updates[1][1], updates[2][1], updates[3][1], updates[4][1], updates[5][1], updates[6][1], updates[7][1], updates[8][1], updates[9][1], image_gain_next, text_gain_next, image_gains - GAIN_RATE * image_gain_next, text_gains - GAIN_RATE * text_gain_next)
```

```python
import math

import jax
import jax.numpy as jnp
import numpy as np
from jax import lax
from jax.experimental import pallas as pl
from jax.experimental.pallas import tpu as pltpu
from jax.sharding import PartitionSpec as P

HI = 12
HT = 8
NS_ITERS = 3


NORM_EPS = 1e-05
UNIT_EPS = 1e-06
SIM_SCALE = 30.0
MOMENTUM = 0.95
RATE = 0.5
GAIN_RATE = 0.5
COEF_A = 3.4445
COEF_B = -4.775
COEF_C = 2.0315
MASKED = -1000000000.0
HIGH = lax.Precision.HIGHEST


def layer_norm(values, gain):
    center = jnp.mean(values, -1, keepdims=True)
    shifted = values - center
    inverse = lax.rsqrt(jnp.mean(shifted * shifted, -1, keepdims=True) + NORM_EPS)
    unit_rows = shifted * inverse
    return (unit_rows * gain, unit_rows, inverse)


def norm_back(upstream, gain, unit_rows, inverse):
    scaled = upstream * gain
    inner = (
        scaled
        - jnp.mean(scaled, -1, keepdims=True)
        - unit_rows * jnp.mean(scaled * unit_rows, -1, keepdims=True)
    )
    gain_grad = jnp.sum((upstream * unit_rows).reshape(-1, unit_rows.shape[-1]), 0)
    return (inner * inverse, gain_grad)


def times_t(left, right):
    return lax.dot_general(
        left, right, (((left.ndim - 1,), (1,)), ((), ())), preferred_element_type=jnp.float32
    )


def times(left, right):
    return lax.dot_general(
        left, right, (((left.ndim - 1,), (0,)), ((), ())), preferred_element_type=jnp.float32
    )


def outer_sum(left, right):
    flat_left = left.reshape(-1, left.shape[-1])
    flat_right = right.reshape(-1, right.shape[-1])
    return lax.dot_general(
        flat_left, flat_right, (((0,), (0,)), ((), ())), preferred_element_type=jnp.float32
    )


def score_block(queries, keys_all, causal):
    head_size = queries.shape[-1]
    scores = jnp.einsum(
        "blhd,bmhd->bhlm", queries, keys_all, preferred_element_type=jnp.float32
    ) * head_size ** (-0.5)
    if causal:
        seq_span = queries.shape[1]
        rows_at = lax.broadcasted_iota(jnp.int32, (seq_span, seq_span), 0)
        cols_at = lax.broadcasted_iota(jnp.int32, (seq_span, seq_span), 1)
        scores = jnp.where(cols_at <= rows_at, scores, MASKED)
    return scores


def tower_forward(tokens, valid_mask, gains, weights, heads, causal):
    attention, output, expand, shrink, embedding = weights
    seq_count, seq_span, model_width = tokens.shape
    head_size = model_width // heads
    inputs = tokens.astype(jnp.float32)
    normed, normed_unit, normed_inverse = layer_norm(inputs, gains[0])
    normed_low = normed.astype(jnp.bfloat16)
    packed = (
        times_t(normed_low, attention)
        .astype(jnp.bfloat16)
        .reshape(seq_count, seq_span, 3, heads, head_size)
    )
    scores = score_block(packed[:, :, 0], packed[:, :, 1], causal)
    highest = jnp.max(scores, -1, keepdims=True)
    raised = jnp.exp(scores - highest)
    totals = jnp.sum(raised, -1, keepdims=True)
    softmaxed = (raised / totals).astype(jnp.bfloat16)
    log_total = highest + jnp.log(totals)
    attended = jnp.einsum(
        "bhlm,bmhd->blhd", softmaxed, packed[:, :, 2], preferred_element_type=jnp.float32
    )
    attended = attended.reshape(seq_count, seq_span, model_width).astype(jnp.bfloat16)
    first_sum = inputs + times_t(attended, output)
    second, second_unit, second_inverse = layer_norm(first_sum, gains[1])
    second_low = second.astype(jnp.bfloat16)
    hidden = times_t(second_low, expand)
    activated = (hidden * jax.nn.sigmoid(1.702 * hidden)).astype(jnp.bfloat16)
    second_sum = first_sum + times(activated, shrink)
    valid_counts = jnp.sum(valid_mask, 1)[:, None]
    pooled = jnp.sum(second_sum * valid_mask[:, :, None], 1) / valid_counts
    final, final_unit, final_inverse = layer_norm(pooled, gains[2])
    final_low = final.astype(jnp.bfloat16)
    embedded = times(final_low, embedding)
    inverse_norm = lax.rsqrt(jnp.sum(embedded * embedded, -1, keepdims=True) + UNIT_EPS)
    unit_embedded = embedded * inverse_norm
    cache = (
        normed_low,
        normed_unit,
        normed_inverse,
        packed,
        log_total,
        attended,
        second_low,
        second_unit,
        second_inverse,
        hidden,
        activated,
        valid_counts,
        final_low,
        final_unit,
        final_inverse,
        inverse_norm,
        unit_embedded,
    )
    return (unit_embedded, cache)


def tower_backward(unit_grad, valid_mask, gains, weights, heads, causal, cache):
    attention, output, expand, shrink, embedding = weights
    (
        normed_low,
        normed_unit,
        normed_inverse,
        packed,
        log_total,
        attended,
        second_low,
        second_unit,
        second_inverse,
        saved,
        activated,
        valid_counts,
        final_low,
        final_unit,
        final_inverse,
        inverse_norm,
        unit_embedded,
    ) = cache
    seq_count, seq_span = valid_mask.shape
    model_width = normed_low.shape[-1]
    head_size = model_width // heads
    along = jnp.sum(unit_grad * unit_embedded, -1, keepdims=True)
    embed_grad = (inverse_norm * (unit_grad - unit_embedded * along)).astype(jnp.bfloat16)
    grad_embedding = outer_sum(final_low, embed_grad)
    pooled_grad, gain_final = norm_back(
        times_t(embed_grad, embedding), gains[2], final_unit, final_inverse
    )
    branch_grad = valid_mask[:, :, None] * (pooled_grad / valid_counts)[:, None, :]
    branch_low = branch_grad.astype(jnp.bfloat16)
    grad_shrink = outer_sum(activated, branch_low)
    act_grad = times_t(branch_low, shrink)
    gate = jax.nn.sigmoid(1.702 * saved)
    hidden_grad = (act_grad * (gate + 1.702 * saved * gate * (1.0 - gate))).astype(jnp.bfloat16)
    grad_expand = outer_sum(hidden_grad, second_low)
    second_grad, gain_second = norm_back(
        times(hidden_grad, expand), gains[1], second_unit, second_inverse
    )
    first_grad = branch_grad + second_grad
    first_low = first_grad.astype(jnp.bfloat16)
    grad_output = outer_sum(first_low, attended)
    attended_grad = (
        times(first_low, output).astype(jnp.bfloat16).reshape(seq_count, seq_span, heads, head_size)
    )
    queries, keys_all, values_all = (packed[:, :, 0], packed[:, :, 1], packed[:, :, 2])
    probs_again = jnp.exp(score_block(queries, keys_all, causal) - log_total)
    prob_grad = jnp.einsum(
        "blhd,bmhd->bhlm", attended_grad, values_all, preferred_element_type=jnp.float32
    )
    score_grad = (
        probs_again * (prob_grad - jnp.sum(prob_grad * probs_again, -1, keepdims=True))
    ).astype(jnp.bfloat16)
    value_grad = jnp.einsum(
        "bhlm,blhd->bmhd",
        probs_again.astype(jnp.bfloat16),
        attended_grad,
        preferred_element_type=jnp.float32,
    )
    scale_factor = head_size ** (-0.5)
    query_grad = (
        jnp.einsum("bhlm,bmhd->blhd", score_grad, keys_all, preferred_element_type=jnp.float32)
        * scale_factor
    )
    key_grad = (
        jnp.einsum("bhlm,blhd->bmhd", score_grad, queries, preferred_element_type=jnp.float32)
        * scale_factor
    )
    packed_grad = (
        jnp.stack([query_grad, key_grad, value_grad], 2)
        .reshape(seq_count, seq_span, 3 * model_width)
        .astype(jnp.bfloat16)
    )
    grad_attention = outer_sum(packed_grad, normed_low)
    input_grad, gain_first = norm_back(
        times(packed_grad, attention), gains[0], normed_unit, normed_inverse
    )
    token_grad = (first_grad + input_grad).astype(jnp.bfloat16)
    return (
        token_grad,
        (grad_attention, grad_output, grad_expand, grad_shrink, grad_embedding),
        jnp.stack([gain_first, gain_second, gain_final]),
    )


TRI3 = ((0, 0), (0, 1), (0, 2), (1, 1), (1, 2), (2, 2))
TRI2 = ((0, 0), (0, 1), (1, 1))
BLOCK = 256


class Place:
    def __init__(self):
        self.n_dp = lax.axis_size("dp")
        self.n_ns = lax.axis_size("ns")
        self.dp = lax.axis_index("dp")
        self.ns = lax.axis_index("ns")
        self.core = self.dp & 1
        along_x = (self.dp >> 1) & 1
        along_y = (self.dp >> 2) & 1
        self.bit_one = jnp.where(self.core == 0, along_x, along_y)
        self.bit_two = jnp.where(self.core == 0, along_y, along_x)
        self.chip = (self.dp >> 1) & 3
        self.piece = self.core * 4 + self.bit_one * 2 + self.bit_two
        self.extra = [1 << bit for bit in range(3, self.n_dp.bit_length() - 1)]

    def over_dp(self, value, target):
        return lax.ppermute(value, "dp", [(i, target(i)) for i in range(self.n_dp)])

    def swap_mask(self, value, mask):
        return self.over_dp(value, lambda i: i ^ mask)

    def swap_core(self, value):
        return self.swap_mask(value, 1)

    def swap_one(self, value):
        return self.over_dp(value, lambda i: i ^ (2 if i % 2 == 0 else 4))

    def swap_two(self, value):
        return self.over_dp(value, lambda i: i ^ (4 if i % 2 == 0 else 2))

    def ring(self, value):
        count = self.n_ns
        return lax.ppermute(value, "ns", [(i, (i + 1) % count) for i in range(count)])

    def swap_ns(self, value, mask):
        return lax.ppermute(value, "ns", [(i, i ^ mask) for i in range(self.n_ns)])

    def spread(self, value):
        first = self.swap_one(value)
        own = [value, first, self.swap_two(value), self.swap_two(first)]
        return own + [self.swap_core(item) for item in own]

    def spread_pieces(self):
        own = [self.piece ^ ((k & 1) * 2) ^ (k >> 1) for k in range(4)]
        base = (1 - self.core) * 4 + self.bit_two * 2 + self.bit_one
        return own + [base ^ ((k & 1) * 2) ^ (k >> 1) for k in range(4)]

    def spread_owners(self):
        mask_one = jnp.where(self.core == 0, 1, 2)
        mask_two = 3 - mask_one
        own = [self.chip ^ ((k & 1) * mask_one) ^ ((k >> 1) * mask_two) for k in range(4)]
        far = [self.chip ^ ((k & 1) * mask_two) ^ ((k >> 1) * mask_one) for k in range(4)]
        return own + far


def pick(value, index, axis):
    return lax.dynamic_index_in_dim(value, index, axis, keepdims=False)


def assemble_kernel(units, splits, index_ref, own_ref, *refs):
    sources = refs[:8]
    outs = refs[8:]
    out_at = 0
    for unit in range(units):
        split = splits[unit]
        outs_of = outs[out_at : out_at + (1 if split is None else 2)]
        out_at += len(outs_of)
        here = index_ref[0]
        cuts = ((0, 8),) if split is None else ((0, split), (split, 8))
        for target, (low_at, high_at) in zip(outs_of, cuts):
            target[here] = own_ref[unit, low_at:high_at]
        for at, source in enumerate(sources):
            to_piece = index_ref[4 + at]
            for hop in range(3):
                to_block = index_ref[1 + hop]
                if split is None:
                    outs_of[0][to_block, to_piece] = source[hop, unit]
                    continue

                @pl.when(to_piece < split)
                def _():
                    outs_of[0][to_block, to_piece] = source[hop, unit]

                @pl.when(to_piece >= split)
                def _():
                    outs_of[1][to_block, to_piece - split] = source[hop, unit]


def gather_weights(place, groups):
    blocks = [jnp.concatenate(group, 0) if len(group) > 1 else group[0] for group in groups]
    rows, width = blocks[0].shape
    piece_rows = rows // 8
    own = jnp.stack(blocks).astype(jnp.bfloat16).reshape(len(blocks), 8, piece_rows, width)
    piece = pick(own, place.piece, 1)
    hop_one = place.ring(piece)
    hop_two = place.ring(hop_one)
    hop_three = place.ring(hop_two)
    sources = place.spread(jnp.stack([hop_one, hop_two, hop_three]))
    index = jnp.stack(
        [place.ns]
        + [(place.ns + place.n_ns - hop) % place.n_ns for hop in (1, 2, 3)]
        + place.spread_pieces()
    ).astype(jnp.int32)
    splits = []
    shapes = []
    for group in groups:
        counts = [item.shape[0] // piece_rows for item in group]
        splits.append(counts[0] if len(group) > 1 else None)
        shapes += [
            jax.ShapeDtypeStruct((place.n_ns, count, piece_rows, width), jnp.bfloat16)
            for count in counts
        ]
    whole = pl.pallas_call(
        lambda *refs: assemble_kernel(len(groups), splits, *refs),
        out_shape=shapes,
        in_specs=[pl.BlockSpec(memory_space=pltpu.SMEM)]
        + [pl.BlockSpec(memory_space=pltpu.VMEM)] * 9,
        out_specs=[pl.BlockSpec(memory_space=pltpu.VMEM)] * len(shapes),
        compiler_params=pltpu.CompilerParams(vmem_limit_bytes=32 << 20),
        name="place_weights",
    )(index, own, *sources)
    return [item.reshape(-1, width) for item in whole]


def sum_rows(place, gradient):
    for mask in place.extra:
        gradient = gradient + place.swap_mask(gradient, mask)
    count = place.n_ns
    rows, width = gradient.shape[0] // count, gradient.shape[1]
    halves = gradient.reshape(count, 2, rows // 2, width)
    far = place.swap_core(pick(halves, 1 - place.core, 1))
    near = pick(halves, place.core, 1)

    def halve(left, right, bit):
        shape = (count, 2, left.shape[1] // 2, width)
        left, right = left.reshape(shape), right.reshape(shape)
        kept = pick(left, bit, 1) + pick(right, bit, 1)
        sent = pick(left, 1 - bit, 1) + pick(right, 1 - bit, 1)
        return kept, sent

    kept, sent = halve(near, far, place.bit_one)
    kept, sent = halve(kept, place.swap_one(sent), place.bit_two)
    total = kept + place.swap_two(sent)
    wide = pick(total, place.ns, 0).astype(jnp.float32)
    for mask in range(1, count):
        wide = wide + place.swap_ns(pick(total, place.ns ^ mask, 0), mask).astype(jnp.float32)
    own = wide.astype(jnp.bfloat16)

    def join(value, other, bit):
        both = jnp.where(
            bit == 0, jnp.concatenate([value, other], 0), jnp.concatenate([other, value], 0)
        )
        return both

    own = join(own, place.swap_two(own), place.bit_two)
    own = join(own, place.swap_one(own), place.bit_one)
    return join(own, place.swap_core(own), place.core)


def sum_gram(place, part):
    count = place.n_ns
    shape = part.shape
    chunks = part.astype(jnp.bfloat16).reshape(count, -1, shape[-1])
    wide = pick(chunks, place.ns, 0).astype(jnp.float32)
    for mask in range(1, count):
        wide = wide + place.swap_ns(pick(chunks, place.ns ^ mask, 0), mask).astype(jnp.float32)
    own = wide.astype(jnp.bfloat16)
    relative = jnp.stack([own] + [place.swap_ns(own, mask) for mask in range(1, count)])
    swapped = jnp.stack([relative[at ^ 1] for at in range(count)])
    relative = jnp.where((place.ns & 1) != 0, swapped, relative)
    swapped = jnp.concatenate([relative[2:], relative[:2]])
    return jnp.where((place.ns & 2) != 0, swapped, relative).reshape(shape)


def upper_blocks(gram, pairs):
    return jnp.stack(
        [
            gram[i * BLOCK : (i + 1) * BLOCK, j * BLOCK : (j + 1) * BLOCK]
            for i, j in pairs
        ]
    )


def polynomial_kernel(side, pairs, gram_ref, out_ref):
    blocks = {pair: gram_ref[at].astype(jnp.float32) for at, pair in enumerate(pairs)}
    rows = [
        jnp.concatenate(
            [blocks[(i, j)] if i <= j else blocks[(j, i)].T for j in range(side)], 1
        )
        for i in range(side)
    ]
    square = jnp.concatenate(rows, 0)
    span = side * BLOCK
    same = lax.broadcasted_iota(jnp.int32, (span, span), 0) == lax.broadcasted_iota(
        jnp.int32, (span, span), 1
    )
    factor = 1.0 / (jnp.sqrt(jnp.sum(jnp.where(same, square, 0.0))) + 1e-07)
    square = square * (factor * factor)

    def mm(left, right):
        return jnp.dot(
            left.astype(jnp.bfloat16),
            right.astype(jnp.bfloat16),
            preferred_element_type=jnp.float32,
        )

    def terms(value):
        return COEF_B * value + COEF_C * mm(value, value)

    def following(value, term):
        half = COEF_A * value + mm(value, term)
        return COEF_A * half + mm(half, term)

    term_zero = terms(square)
    square = following(square, term_zero)
    term_one = terms(square)
    square = following(square, term_one)
    term_two = terms(square)
    both = COEF_A * (term_zero + term_one) + mm(term_zero, term_one)
    whole = COEF_A**2 * term_two + COEF_A * both + mm(both, term_two)
    whole = factor * (whole + jnp.where(same, COEF_A**3, 0.0))
    for at, (i, j) in enumerate(pairs):
        out_ref[at] = whole[
            i * BLOCK : (i + 1) * BLOCK, j * BLOCK : (j + 1) * BLOCK
        ].astype(jnp.bfloat16)


def polynomial(gram, side, pairs):
    span = side * BLOCK
    return pl.pallas_call(
        lambda *refs: polynomial_kernel(side, pairs, *refs),
        out_shape=jax.ShapeDtypeStruct(gram.shape, jnp.bfloat16),
        in_specs=[pl.BlockSpec(memory_space=pltpu.VMEM)],
        out_specs=pl.BlockSpec(memory_space=pltpu.VMEM),
        compiler_params=pltpu.CompilerParams(vmem_limit_bytes=48 << 20),
        cost_estimate=pl.CostEstimate(
            flops=18 * span**3, bytes_accessed=4 * span * span, transcendentals=0
        ),
        name="polynomial",
    )(gram)


def place_kernel(index_ref, *refs):
    out_ref = refs[8]
    for at, source in enumerate(refs[:8]):
        out_ref[index_ref[at], index_ref[8 + at]] = source[...]


def spread_polynomials(place, blocks):
    sources = place.spread(blocks)
    core = place.core
    index = jnp.stack(place.spread_owners() + [core] * 4 + [1 - core] * 4).astype(jnp.int32)
    return pl.pallas_call(
        place_kernel,
        out_shape=jax.ShapeDtypeStruct((4, 2) + blocks.shape, blocks.dtype),
        in_specs=[pl.BlockSpec(memory_space=pltpu.SMEM)]
        + [pl.BlockSpec(memory_space=pltpu.VMEM)] * 8,
        out_specs=pl.BlockSpec(memory_space=pltpu.VMEM),
        compiler_params=pltpu.CompilerParams(vmem_limit_bytes=32 << 20),
        name="place_polynomials",
    )(index, *sources)


def apply_kernel(side, pairs, scale, fresh_ref, poly_ref, master_ref, out_ref):
    fresh = fresh_ref[...].astype(jnp.bfloat16)
    at_of = {pair: at for at, pair in enumerate(pairs)}
    for j in range(side):
        total = None
        for i in range(side):
            left = fresh[:, i * BLOCK : (i + 1) * BLOCK]
            block = poly_ref[at_of[(min(i, j), max(i, j))]]
            term = lax.dot_general(
                left,
                block,
                (((1,), (0 if i <= j else 1,)), ((), ())),
                preferred_element_type=jnp.float32,
            )
            total = term if total is None else total + term
        columns = slice(j * BLOCK, (j + 1) * BLOCK)
        out_ref[:, columns] = master_ref[:, columns] - scale * total


def apply_polynomial(master, fresh, blocks, scale):
    rows, width = master.shape
    side = width // BLOCK
    pairs = TRI3 if side == 3 else TRI2
    tile = rows
    while tile > 256:
        tile = tile // 2 if tile % 512 == 0 or tile % 3 else tile // 3
    row_spec = pl.BlockSpec((tile, width), lambda i: (i, 0))
    return pl.pallas_call(
        lambda *refs: apply_kernel(side, pairs, scale, *refs),
        out_shape=jax.ShapeDtypeStruct(master.shape, jnp.float32),
        grid=(rows // tile,),
        in_specs=[row_spec, pl.BlockSpec(blocks.shape, lambda i: (0, 0, 0)), row_spec],
        out_specs=row_spec,
        compiler_params=pltpu.CompilerParams(vmem_limit_bytes=32 << 20),
        cost_estimate=pl.CostEstimate(
            flops=2 * rows * width * width, bytes_accessed=12 * rows * width, transcendentals=0
        ),
        name="apply_polynomial",
    )(fresh, blocks, master)


def outer_gram(rows):
    return lax.dot_general(
        rows, rows, (((0,), (0,)), ((), ())), preferred_element_type=jnp.float32
    )


def gather_units(place, units):
    masks = [(0, mask) for mask in range(place.n_ns)]
    held = jnp.stack(
        [units] + [place.swap_ns(units, mask) for mask in range(1, place.n_ns)]
    )
    for mask in [2, 4, 1] + place.extra:
        held = jnp.concatenate([held, place.swap_mask(held, mask)], 0)
        masks = masks + [(one ^ mask, two) for one, two in masks]
    over_dp = jnp.array([one for one, _ in masks], jnp.int32)
    over_ns = jnp.array([two for _, two in masks], jnp.int32)
    return held, (place.dp ^ over_dp) * place.n_ns + (place.ns ^ over_ns)


def contrast(place, image_unit, text_unit, caption_image):
    image_low = image_unit.astype(jnp.bfloat16)
    text_low = text_unit.astype(jnp.bfloat16)
    image_local, caption_local = image_low.shape[0], text_low.shape[0]
    held, numbers = gather_units(place, jnp.concatenate([image_low, text_low], 0))
    joint = held.shape[-1]
    every_image = held[:, :image_local].reshape(-1, joint)
    every_text = held[:, image_local:].reshape(-1, joint)
    image_total, caption_total = every_image.shape[0], every_text.shape[0]
    image_ids = (
        numbers[:, None] * image_local + jnp.arange(image_local, dtype=jnp.int32)
    ).reshape(-1)
    named = jnp.take(caption_image.reshape(-1, caption_local), numbers, axis=0).reshape(-1)
    match = (named[None, :] == image_ids[:, None]).astype(jnp.float32)
    counts = jnp.sum(match, 1, keepdims=True)
    sims = times_t(every_image, every_text) * SIM_SCALE
    row_log = jax.scipy.special.logsumexp(sims, axis=1, keepdims=True)
    col_log = jax.scipy.special.logsumexp(sims, axis=0, keepdims=True)
    side = 0.5 * image_total / caption_total
    image_terms = row_log - jnp.sum(sims * match, 1, keepdims=True) / counts
    caption_terms = col_log - jnp.sum(sims * match, 0, keepdims=True)
    loss_part = 0.5 * jnp.sum(image_terms[:image_local]) + side * jnp.sum(
        caption_terms[:, :caption_local]
    )
    sims_grad = 0.5 * (jnp.exp(sims - row_log) - match / counts) + side * (
        jnp.exp(sims - col_log) - match
    )
    image_unit_grad = SIM_SCALE * jnp.dot(
        sims_grad[:image_local], every_text.astype(jnp.float32), precision=HIGH
    )
    text_unit_grad = SIM_SCALE * lax.dot_general(
        sims_grad[:, :caption_local],
        every_image.astype(jnp.float32),
        (((0,), (0,)), ((), ())),
        precision=HIGH,
        preferred_element_type=jnp.float32,
    )
    return loss_part, image_unit_grad, text_unit_grad


def sum_small(place, loss_part, image_gain, text_gain):
    width = image_gain.shape[1]
    pad = width - text_gain.shape[1]
    packed = jnp.concatenate(
        [
            image_gain,
            jnp.pad(text_gain, ((0, 0), (0, pad))),
            jnp.broadcast_to(loss_part, (2, width)),
        ],
        0,
    )
    for mask in [1, 2, 4] + place.extra:
        packed = packed + place.swap_mask(packed, mask)
    for mask in (1, 2):
        packed = packed + place.swap_ns(packed, mask)
    return packed[6, 0], packed[:3], packed[3:6, : width - pad]


def joined(place, first, second, count):
    width = first.shape[1]
    return jnp.concatenate(
        [first.reshape(count, -1, width), second.reshape(count, -1, width)], 1
    ).reshape(-1, width)


def per_device(
    image_tokens,
    text_tokens,
    caption_image,
    caption_length,
    image_attention,
    image_output,
    image_expand,
    image_shrink,
    image_embedding,
    text_attention,
    text_output,
    text_expand,
    text_shrink,
    text_embedding,
    image_gains,
    text_gains,
    image_attention_momentum,
    image_output_momentum,
    image_expand_momentum,
    image_shrink_momentum,
    image_embedding_momentum,
    text_attention_momentum,
    text_output_momentum,
    text_expand_momentum,
    text_shrink_momentum,
    text_embedding_momentum,
    image_gains_momentum,
    text_gains_momentum,
):
    place = Place()
    masters = (
        image_attention,
        image_output,
        image_expand,
        image_shrink,
        image_embedding,
        text_attention,
        text_output,
        text_expand,
        text_shrink,
        text_embedding,
    )
    moments = (
        image_attention_momentum,
        image_output_momentum,
        image_expand_momentum,
        image_shrink_momentum,
        image_embedding_momentum,
        text_attention_momentum,
        text_output_momentum,
        text_expand_momentum,
        text_shrink_momentum,
        text_embedding_momentum,
    )
    ta_low, to_low = gather_weights(place, [(text_attention, text_output)])
    te_low, ts_low = gather_weights(place, [(text_expand,), (text_shrink,)])
    ia_low, io_low = gather_weights(place, [(image_attention, image_output)])
    (ie_low,) = gather_weights(place, [(image_expand,)])
    (is_low,) = gather_weights(place, [(image_shrink,)])
    em_rows, te_rows = image_embedding.shape[0], text_embedding.shape[0]
    padded = jnp.pad(text_embedding, ((0, em_rows - te_rows), (0, 0)))
    iem_low, tem_low = gather_weights(place, [(image_embedding, padded)])
    joint = text_embedding.shape[1]
    tem_low = tem_low.reshape(-1, em_rows, joint)[:, :te_rows].reshape(-1, joint)
    text_weights = (ta_low, to_low, te_low, ts_low, tem_low)
    image_weights = (ia_low, io_low, ie_low, is_low, iem_low)
    image_valid = jnp.ones(image_tokens.shape[:2], jnp.float32)
    slot_index = lax.broadcasted_iota(jnp.int32, text_tokens.shape[:2], 1)
    text_valid = (slot_index < caption_length[:, None]).astype(jnp.float32)
    text_unit, text_cache = tower_forward(
        text_tokens, text_valid, text_gains, text_weights, HT, True
    )
    image_unit, image_cache = tower_forward(
        image_tokens, image_valid, image_gains, image_weights, HI, False
    )
    loss_part, image_unit_grad, text_unit_grad = contrast(
        place, image_unit, text_unit, caption_image
    )
    image_total = image_tokens.shape[0] * place.n_dp * place.n_ns
    image_token_grad, image_grads, image_gain_grad = tower_backward(
        image_unit_grad, image_valid, image_gains, image_weights, HI, False, image_cache
    )
    text_token_grad, text_grads, text_gain_grad = tower_backward(
        text_unit_grad, text_valid, text_gains, text_weights, HT, True, text_cache
    )
    count = place.n_ns
    image_grads = [item.astype(jnp.bfloat16) for item in image_grads]
    text_grads = [item.astype(jnp.bfloat16) for item in text_grads]
    grad_embeds = sum_rows(place, joined(place, image_grads[4], text_grads[4], count))
    grad_is = sum_rows(place, image_grads[3])
    grad_ie = sum_rows(place, image_grads[2])
    grad_iao = sum_rows(place, joined(place, image_grads[0], image_grads[1], count))
    grad_ts = sum_rows(place, text_grads[3])
    grad_te = sum_rows(place, text_grads[2])
    grad_tao = sum_rows(place, joined(place, text_grads[0], text_grads[1], count))
    ia_rows, ta_rows = image_attention.shape[0], text_attention.shape[0]
    reduced = (
        grad_iao[:ia_rows],
        grad_iao[ia_rows:],
        grad_ie,
        grad_is,
        grad_embeds[:em_rows],
        grad_tao[:ta_rows],
        grad_tao[ta_rows:],
        grad_te,
        grad_ts,
        grad_embeds[em_rows:],
    )
    fresh = [
        MOMENTUM * moment + gradient.astype(jnp.float32)
        for moment, gradient in zip(moments, reduced)
    ]
    low = [item.astype(jnp.bfloat16) for item in fresh]

    rows_all = low[2].shape[0]
    row_at = lax.broadcasted_iota(jnp.int32, (rows_all, 1), 0)
    chip = place.chip
    iao = jnp.where((row_at < ia_rows) == (chip == 2), jnp.concatenate(low[:2], 0), 0)
    chosen = jnp.where(chip == 0, low[2], jnp.where(chip == 1, low[3], iao))
    blocks = upper_blocks(outer_gram(chosen), TRI3)
    half = sum_gram(place, pick(blocks.reshape(2, 3, BLOCK, BLOCK), place.core, 0))
    other = place.swap_core(half)
    whole = jnp.where(
        place.core == 0, jnp.concatenate([half, other]), jnp.concatenate([other, half])
    )
    image_poly = polynomial(whole, 3, TRI3).reshape(2, 3, BLOCK, BLOCK)
    image_poly = spread_polynomials(place, pick(image_poly, place.core, 0))
    image_poly = image_poly.reshape(4, 6, BLOCK, BLOCK)

    slot = place.chip * 2 + place.core
    rows_all = low[7].shape[0]
    row_at = lax.broadcasted_iota(jnp.int32, (rows_all, 1), 0)
    tao = jnp.where((row_at < ta_rows) == (slot == 2), jnp.concatenate(low[5:7], 0), 0)
    embeds = jnp.concatenate([low[4], low[9]], 0)
    embeds = jnp.pad(embeds, ((0, rows_all - embeds.shape[0]), (0, 0)))
    embeds = jnp.where((row_at < em_rows) == (slot == 4), embeds, 0)
    chosen = jnp.where(
        slot == 0,
        low[7],
        jnp.where(slot == 1, low[8], jnp.where(slot < 4, tao, embeds)),
    )
    blocks = upper_blocks(outer_gram(chosen), TRI2)
    text_poly = polynomial(sum_gram(place, blocks), 2, TRI2)
    text_poly = spread_polynomials(place, text_poly).reshape(8, 3, BLOCK, BLOCK)

    polys = (
        image_poly[2],
        image_poly[3],
        image_poly[0],
        image_poly[1],
        text_poly[4],
        text_poly[2],
        text_poly[3],
        text_poly[0],
        text_poly[1],
        text_poly[5],
    )
    next_weights = [
        apply_polynomial(
            master, item, blocks, RATE * math.sqrt(item.shape[0] * count / item.shape[1])
        )
        for master, item, blocks in zip(masters, fresh, polys)
    ]
    loss_total, image_gain_sum, text_gain_sum = sum_small(
        place, loss_part, image_gain_grad, text_gain_grad
    )
    image_gain_next = MOMENTUM * image_gains_momentum + image_gain_sum
    text_gain_next = MOMENTUM * text_gains_momentum + text_gain_sum
    loss = jnp.reshape(loss_total / image_total, (1,))
    return (
        loss,
        image_token_grad,
        text_token_grad,
        *fresh,
        *next_weights,
        image_gain_next,
        text_gain_next,
        image_gains - GAIN_RATE * image_gain_next,
        text_gains - GAIN_RATE * text_gain_next,
    )


def solution(mesh):
    placed = (
        P(("dp", "ns"), None, None),
        P(("dp", "ns"), None, None),
        P(),
        P(("dp", "ns")),
        P("ns", None),
        P("ns", None),
        P("ns", None),
        P("ns", None),
        P("ns", None),
        P("ns", None),
        P("ns", None),
        P("ns", None),
        P("ns", None),
        P("ns", None),
        P(),
        P(),
        P("ns", None),
        P("ns", None),
        P("ns", None),
        P("ns", None),
        P("ns", None),
        P("ns", None),
        P("ns", None),
        P("ns", None),
        P("ns", None),
        P("ns", None),
        P(),
        P(),
    )
    return jax.shard_map(
        per_device,
        mesh=mesh,
        in_specs=placed,
        out_specs=(
            P(),
            P(("dp", "ns"), None, None),
            P(("dp", "ns"), None, None),
            P("ns", None),
            P("ns", None),
            P("ns", None),
            P("ns", None),
            P("ns", None),
            P("ns", None),
            P("ns", None),
            P("ns", None),
            P("ns", None),
            P("ns", None),
            P("ns", None),
            P("ns", None),
            P("ns", None),
            P("ns", None),
            P("ns", None),
            P("ns", None),
            P("ns", None),
            P("ns", None),
            P("ns", None),
            P("ns", None),
            P(),
            P(),
            P(),
            P(),
        ),
        check_vma=False,
    )
```

```python
import math

import jax
import jax.numpy as jnp
from jax import lax
from jax.experimental import pallas as pl
from jax.experimental.pallas import tpu as pltpu
from jax.sharding import PartitionSpec as P

HI = 12
HT = 8
HEAD = 64

NORM_EPS = 1e-05
UNIT_EPS = 1e-06
SIM_SCALE = 30.0
MOMENTUM = 0.95
RATE = 0.5
GAIN_RATE = 0.5
COEF_A = 3.4445
COEF_B = -4.775
COEF_C = 2.0315
MASKED = -1000000000.0
HIGH = lax.Precision.HIGHEST
LOW = jnp.bfloat16
WIDE = jnp.float32

TRI3 = ((0, 0), (0, 1), (0, 2), (1, 1), (1, 2), (2, 2))
TRI2 = ((0, 0), (0, 1), (1, 1))
BLOCK = 256
IN_VMEM = pl.BlockSpec(memory_space=pltpu.VMEM)
IN_SMEM = pl.BlockSpec(memory_space=pltpu.SMEM)
IN_PLACE = pl.BlockSpec(memory_space=pl.ANY)


def call(body, out_shape, specs, micros, limit, scratch=(), name=None):
    outs = jax.tree.map(lambda _: IN_VMEM, out_shape)
    return pl.pallas_call(
        body,
        out_shape=out_shape,
        in_specs=specs,
        out_specs=outs,
        scratch_shapes=list(scratch),
        compiler_params=pltpu.CompilerParams(vmem_limit_bytes=limit << 20),
        cost_estimate=pl.CostEstimate(
            flops=int(1e4 * micros), bytes_accessed=16, transcendentals=0
        ),
        name=name,
    )


def after(value, *others):
    return lax.optimization_barrier((value,) + others)[0]


def shaped(shape, dtype=WIDE):
    return jax.ShapeDtypeStruct(shape, dtype)


class Place:
    def __init__(self):
        self.n_dp = lax.axis_size("dp")
        self.n_ns = lax.axis_size("ns")
        self.dp = lax.axis_index("dp")
        self.ns = lax.axis_index("ns")
        self.core = self.dp & 1
        along_x = (self.dp >> 1) & 1
        along_y = (self.dp >> 2) & 1
        self.bit_one = jnp.where(self.core == 0, along_x, along_y)
        self.bit_two = jnp.where(self.core == 0, along_y, along_x)
        self.chip = (self.dp >> 1) & 3
        self.piece = self.core * 4 + self.bit_one * 2 + self.bit_two
        self.extra = [1 << bit for bit in range(3, self.n_dp.bit_length() - 1)]
        self.core_at = self.core.astype(jnp.int32).reshape(1)
        self.blocks_at = jnp.stack([self.ns ^ mask for mask in range(self.n_ns)]).astype(jnp.int32)

    def over_dp(self, value, target):
        return lax.ppermute(value, "dp", [(i, target(i)) for i in range(self.n_dp)])

    def swap_mask(self, value, mask):
        return self.over_dp(value, lambda i: i ^ mask)

    def swap_core(self, value):
        return self.swap_mask(value, 1)

    def swap_one(self, value):
        return self.over_dp(value, lambda i: i ^ (2 if i % 2 == 0 else 4))

    def swap_two(self, value):
        return self.over_dp(value, lambda i: i ^ (4 if i % 2 == 0 else 2))

    def ring(self, value, steps=1):
        count = self.n_ns
        return lax.ppermute(value, "ns", [(i, (i + steps) % count) for i in range(count)])

    def swap_ns(self, value, mask):
        return lax.ppermute(value, "ns", [(i, i ^ mask) for i in range(self.n_ns)])

    def spread(self, value):
        first = self.swap_one(value)
        own = [value, first, self.swap_two(value), self.swap_two(first)]
        return own + [self.swap_core(item) for item in own]

    def spread_pieces(self):
        own = [self.piece ^ ((k & 1) * 2) ^ (k >> 1) for k in range(4)]
        base = (1 - self.core) * 4 + self.bit_two * 2 + self.bit_one
        return own + [base ^ ((k & 1) * 2) ^ (k >> 1) for k in range(4)]

    def spread_owners(self):
        mask_one = jnp.where(self.core == 0, 1, 2)
        mask_two = 3 - mask_one
        own = [self.chip ^ ((k & 1) * mask_one) ^ ((k >> 1) * mask_two) for k in range(4)]
        far = [self.chip ^ ((k & 1) * mask_two) ^ ((k >> 1) * mask_one) for k in range(4)]
        return own + far


class Spread:
    def __init__(self, place, value):
        self.place = place
        self.own = [value, place.swap_one(value), place.swap_two(value)]

    def flying(self):
        return self.own[1:]

    def landed(self, flown):
        self.own = [self.own[0]] + list(flown)

    def more(self):
        self.own.append(self.place.swap_two(self.own[1]))
        return self.own[3]

    def finish(self):
        return self.own + [self.place.swap_core(item) for item in self.own]


def pick(value, index, axis):
    return lax.dynamic_index_in_dim(value, index, axis, keepdims=False)


def unit_sizes(unit):
    rows = sum(item.shape[0] for item in unit) // 8
    width = unit[0].shape[1]
    split = unit[0].shape[0] // rows
    return rows, width, split


def cut_kernel(sizes, at_ref, *refs):
    count = sum(2 if split < 8 else 1 for unit in sizes for _, _, split in unit)
    units = [unit for bundle in sizes for unit in bundle]
    weights, outs = refs[:count], refs[count : count + len(sizes)]
    held, sems = refs[count + len(sizes) : -1], refs[-1]
    piece = at_ref[0]
    waits = []
    at = 0
    for number, (rows, _, split) in enumerate(units):
        low = pltpu.make_async_copy(
            weights[at].at[pl.ds(pl.multiple_of(jnp.minimum(piece, split - 1) * rows, 8), rows)],
            held[number],
            sems.at[number],
        )
        at += 1
        if split == 8:
            low.start()
            waits.append(((None, low),))
            continue
        high = pltpu.make_async_copy(
            weights[at].at[pl.ds(pl.multiple_of(jnp.maximum(piece - split, 0) * rows, 8), rows)],
            held[number],
            sems.at[number],
        )
        at += 1
        pl.when(piece < split)(low.start)
        pl.when(piece >= split)(high.start)
        waits.append(((piece < split, low), (piece >= split, high)))
    number = 0
    for bundle, out in zip(sizes, outs):
        row = 0
        for rows, width, _ in bundle:
            for condition, copy in waits[number]:
                if condition is None:
                    copy.wait()
                else:
                    pl.when(condition)(copy.wait)
            for column in range(0, width, BLOCK):
                out[row : row + rows] = held[number][:, column : column + BLOCK].astype(LOW)
                row += rows
            number += 1


def cut_pieces(place, bundles):
    sizes = [[unit_sizes(unit) for unit in bundle] for bundle in bundles]
    flat = [unit for bundle in sizes for unit in bundle]
    weights = [item for bundle in bundles for unit in bundle for item in unit]
    out_shape = [
        shaped((sum(rows * width // BLOCK for rows, width, _ in bundle), BLOCK), LOW)
        for bundle in sizes
    ]
    return call(
        lambda *refs: cut_kernel(sizes, *refs),
        out_shape,
        [IN_SMEM] + [IN_PLACE] * len(weights),
        1,
        56,
        [pltpu.VMEM((rows, width), WIDE) for rows, width, _ in flat]
        + [pltpu.SemaphoreType.DMA((len(flat),))],
        "cut_pieces",
    )(place.piece.astype(jnp.int32).reshape(1), *weights)


def lay_kernel(sizes, index_ref, *refs):
    count = sum(2 if split < 8 else 1 for _, _, split in sizes)
    weights, sources, outs = refs[:count], refs[count : count + 8], refs[count + 8 :]
    at = row = 0
    for rows, width, split in sizes:
        cuts = ((0, 8),) if split == 8 else ((0, split), (split, 8))
        for part, (low_at, high_at) in enumerate(cuts):
            own = weights[at + part][...].astype(LOW)
            outs[at + part][index_ref[0]] = own.reshape(high_at - low_at, rows, width)
        for number, source in enumerate(sources):
            to_piece = index_ref[4 + number]
            for hop in range(3):
                to_block = index_ref[1 + hop]

                def lay(target, to_row):
                    for slab in range(width // BLOCK):
                        target[to_block, to_row, :, slab * BLOCK : (slab + 1) * BLOCK] = source[
                            hop, row + slab * rows : row + (slab + 1) * rows
                        ]

                if split == 8:
                    lay(outs[at], to_piece)
                else:
                    pl.when(to_piece < split)(lambda: lay(outs[at], to_piece))
                    pl.when(to_piece >= split)(lambda: lay(outs[at + 1], to_piece - split))
        at += len(cuts)
        row += rows * width // BLOCK


class Bundle:
    def __init__(self, place, piece, bundle):
        self.place, self.bundle, self.piece = place, bundle, piece

    def hops_direct(self):
        place = self.place
        self.hops = [place.ring(self.piece, steps) for steps in (1, 2, 3)]

    def hops_ring(self):
        place = self.place
        self.hops = [place.ring(self.piece)]
        self.hops.append(place.ring(self.hops[0]))
        self.hops.append(place.ring(self.hops[1]))

    def first_links(self, *waits):
        place = self.place
        held = after(jnp.stack(self.hops), *waits)
        self.own = [held, place.swap_one(held), place.swap_two(held)]

    def second_link(self, *waits):
        place = self.place
        if waits:
            gated = lax.optimization_barrier(tuple(self.own) + waits)
            self.own = list(gated[:3])
        self.own.append(place.swap_two(self.own[1]))
        self.far = [place.swap_core(item) for item in self.own]

    def lay(self):
        place, bundle = self.place, self.bundle
        sizes = [unit_sizes(unit) for unit in bundle]
        weights = [item for unit in bundle for item in unit]
        index = jnp.stack(
            [place.ns]
            + [(place.ns + place.n_ns - hop) % place.n_ns for hop in (1, 2, 3)]
            + place.spread_pieces()
        ).astype(jnp.int32)
        out_shape = []
        for rows, width, split in sizes:
            for pieces in (8,) if split == 8 else (split, 8 - split):
                out_shape.append(shaped((place.n_ns, pieces, rows, width), LOW))
        whole = call(
            lambda *refs: lay_kernel(sizes, *refs),
            out_shape,
            [IN_SMEM] + [IN_VMEM] * (len(weights) + 8),
            5,
            48,
            name="lay_weights",
        )(index, *weights, *self.own, *self.far)
        return [item.reshape(-1, item.shape[-1]) for item in whole]


class RowSum:
    def __init__(self, place, near, far):
        for mask in place.extra:
            near = near + place.swap_mask(near, mask)
            far = far + place.swap_mask(far, mask)
        self.place, self.near = place, near
        self.got = place.swap_core(far)

    def halve(self, left, right, bit):
        count, rows, width = left.shape
        shape = (count, 2, rows // 2, width)
        left, right = left.reshape(shape), right.reshape(shape)
        self.kept = pick(left, bit, 1) + pick(right, bit, 1)
        self.sent = pick(left, 1 - bit, 1) + pick(right, 1 - bit, 1)

    def step_one(self):
        self.halve(self.near, self.got, self.place.bit_one)
        self.got = self.place.swap_one(self.sent)

    def step_two(self):
        self.halve(self.kept, self.got, self.place.bit_two)
        self.got = self.place.swap_two(self.sent)

    def step_three(self):
        place = self.place
        odd = place.ns & 1
        pairs = (2, 2) + self.kept.shape[1:]
        kept, got = self.kept.reshape(pairs), self.got.reshape(pairs)
        self.sent = pick(kept, 1 - odd, 1) + pick(got, 1 - odd, 1)
        self.kept = pick(kept, odd, 1) + pick(got, odd, 1)
        self.got = place.swap_ns(self.sent, 1)

    def step_four(self):
        high = (self.place.ns >> 1) & 1
        self.sent = pick(self.kept, 1 - high, 0) + pick(self.got, 1 - high, 0)
        self.kept = pick(self.kept, high, 0) + pick(self.got, high, 0)


def last_step(place, sums):
    kept = jnp.stack([item.kept for item in sums])
    return kept, place.swap_ns(jnp.stack([item.sent for item in sums]), 2)


def over_ns(place, parts):
    return [parts[0]] + [place.swap_ns(part, mask) for mask, part in enumerate(parts) if mask]


def total_of(place, parts):
    total = parts[0].astype(WIDE)
    for part in parts[1:]:
        total = total + part.astype(WIDE)
    return [total.astype(LOW)] * place.n_ns


def place_kernel(index_ref, *refs):
    out_ref = refs[8]
    for at, source in enumerate(refs[:8]):
        out_ref[index_ref[at], index_ref[8 + at]] = source[...]


def lay_spread(place, sources, name):
    core = place.core
    index = jnp.stack(place.spread_owners() + [core] * 4 + [1 - core] * 4).astype(jnp.int32)
    return call(
        place_kernel,
        shaped((4, 2) + sources[0].shape, sources[0].dtype),
        [IN_SMEM] + [IN_VMEM] * 8,
        1,
        32,
        name=name,
    )(index, *sources)


def spread_numbers(place):
    core = place.core
    chips = jnp.stack(place.spread_owners())
    cores = jnp.stack([core] * 4 + [1 - core] * 4)
    base = place.dp - (place.dp & 7)
    over_dp = base + chips * 2 + cores
    numbers = (over_dp[:, None] * place.n_ns + place.blocks_at[None, :]).reshape(-1)
    for mask in place.extra:
        numbers = jnp.concatenate([numbers, numbers ^ (mask * place.n_ns)])
    return numbers


def gather_units(place, units):
    parts = [units] + [place.swap_ns(units, mask) for mask in range(1, place.n_ns)]
    sources = place.spread(jnp.stack(parts))
    for mask in place.extra:
        sources = sources + [place.swap_mask(item, mask) for item in sources]
    return sources


def pack_small(loss_part, image_gain, text_gain):
    width = image_gain.shape[1]
    pad = width - text_gain.shape[1]
    return jnp.concatenate(
        [
            image_gain,
            jnp.pad(text_gain, ((0, 0), (0, pad))),
            jnp.broadcast_to(loss_part, (2, width)),
        ],
        0,
    )


def rows_by(left, right):
    return lax.dot_general(left, right, (((1,), (1,)), ((), ())), preferred_element_type=WIDE)


def product(left, right):
    return jnp.dot(left, right, preferred_element_type=WIDE)


def outer(left, right):
    return lax.dot_general(left, right, (((0,), (0,)), ((), ())), preferred_element_type=WIDE)


def normalize(values):
    shifted = values - jnp.mean(values, -1, keepdims=True)
    inverse = lax.rsqrt(jnp.mean(shifted * shifted, -1, keepdims=True) + NORM_EPS)
    return shifted * inverse, inverse


def norm_back(upstream, gain, unit_rows, inverse):
    scaled = upstream * gain
    inner = (
        scaled
        - jnp.mean(scaled, -1, keepdims=True)
        - unit_rows * jnp.mean(scaled * unit_rows, -1, keepdims=True)
    )
    return inner * inverse, jnp.sum(upstream * unit_rows, 0, keepdims=True)


def gate_of(hidden):
    return 0.5 * jnp.tanh(0.851 * hidden) + 0.5


class Tower:
    def __init__(self, count, span, width, hidden, heads, joint, causal):
        self.joint = joint
        self.count, self.span, self.width, self.hidden = count, span, width, hidden
        self.heads, self.causal = heads, causal
        self.padded = -(-span // 16) * 16
        self.rows = count * self.padded

    def valid(self, length_ref):
        at = lax.broadcasted_iota(jnp.int32, (self.padded, 1), 0)
        return jnp.concatenate(
            [(at < length_ref[number]).astype(WIDE) for number in range(self.count)], 0
        )

    def quarters(self):
        lane = lax.broadcasted_iota(jnp.int32, (1, BLOCK), 1)
        return [
            ((lane >= HEAD * at) & (lane < HEAD * (at + 1))).astype(WIDE).astype(LOW)
            for at in range(BLOCK // HEAD)
        ]

    def stacked(self, value, masks):
        return jnp.concatenate([value * mask for mask in masks], 0)

    def unstacked(self, value, masks):
        total = None
        for at, mask in enumerate(masks):
            part = value[at * self.padded : (at + 1) * self.padded] * mask.astype(WIDE)
            total = part if total is None else total + part
        return total

    def probabilities(self, left, right, over):
        scores = rows_by(left, right) * HEAD ** (-0.5)
        shape = scores.shape
        key = lax.broadcasted_iota(jnp.int32, shape, over)
        if self.causal:
            query = lax.broadcasted_iota(jnp.int32, shape, 1 - over)
            within = query - (query // self.padded) * self.padded
            scores = jnp.where(key <= within, scores, MASKED)
        elif self.padded != self.span:
            scores = jnp.where(key < self.span, scores, MASKED)
        raised = jnp.exp(scores - jnp.max(scores, over, keepdims=True))
        return raised * (1.0 / jnp.sum(raised, over, keepdims=True))

    def attend_kernel(
        self, x_ref, gains_ref, wa_ref, wo_ref, normed_ref, packed_ref, attended_ref, first_ref
    ):
        width = self.width
        unit_rows, _ = normalize(x_ref[...].astype(WIDE))
        normed_ref[...] = (unit_rows * gains_ref[0:1, :]).astype(LOW)
        for at in range(0, 3 * width, width):
            packed_ref[:, at : at + width] = rows_by(
                normed_ref[...], wa_ref[at : at + width, :]
            ).astype(LOW)
        masks = self.quarters()

        def one(number, carry):
            rows = pl.ds(pl.multiple_of(number * self.padded, 16), self.padded)
            for at in range(0, width, BLOCK):
                columns = slice(at, at + BLOCK)
                queries = self.stacked(packed_ref[rows, columns], masks)
                keys = packed_ref[rows, width + at : width + at + BLOCK]
                values = packed_ref[rows, 2 * width + at : 2 * width + at + BLOCK]
                probs = self.probabilities(queries, keys, 1).astype(LOW)
                attended_ref[rows, columns] = self.unstacked(product(probs, values), masks).astype(
                    LOW
                )
            return carry

        lax.fori_loop(0, self.count, one, 0, unroll=True)
        first_ref[...] = x_ref[...].astype(WIDE) + rows_by(attended_ref[...], wo_ref[...])

    def attend(self, x, gains, wa, wo):
        rows, width = self.rows, self.width
        return call(
            self.attend_kernel,
            [
                shaped((rows, width), LOW),
                shaped((rows, 3 * width), LOW),
                shaped((rows, width), LOW),
                shaped((rows, width)),
            ],
            [IN_VMEM] * 4,
            10,
            48,
            name="attend",
        )(x, gains, wa, wo)

    def feed_kernel(self, length_ref, first_ref, gains_ref, we_ref, sums_ref, pool_ref):
        valid = self.valid(length_ref)
        first = first_ref[...]
        unit_rows, _ = normalize(first)
        second = (unit_rows * gains_ref[1:2, :]).astype(LOW)

        def pooled(value):
            shape = (self.count, self.padded, value.shape[-1])
            return jnp.sum((value * valid).reshape(shape), 1)

        pool_ref[...] = pooled(first)
        step = self.hidden // 4
        for at in range(0, self.hidden, step):
            hidden = rows_by(second, we_ref[at : at + step, :])
            activated = (hidden * gate_of(hidden)).astype(LOW)
            sums_ref[:, at : at + step] = pooled(activated.astype(WIDE))

    def feed(self, lengths, first, gains, we):
        return call(
            self.feed_kernel,
            [shaped((self.count, self.hidden)), shaped((self.count, self.width))],
            [IN_SMEM] + [IN_VMEM] * 3,
            3,
            48,
            name="feed",
        )(lengths, first, gains, we)

    def head_kernel(
        self,
        sums_ref,
        pool_ref,
        counts_ref,
        ws_ref,
        gains_ref,
        wm_ref,
        pooled_ref,
        embedded_ref,
        unit_ref,
    ):
        sums = sums_ref[...]
        high = sums.astype(LOW)
        rest = (sums - high.astype(WIDE)).astype(LOW)
        total = pool_ref[...] + product(high, ws_ref[...]) + product(rest, ws_ref[...])
        pooled = total / counts_ref[...]
        unit_rows, _ = normalize(pooled)
        embedded = product((unit_rows * gains_ref[2:3, :]).astype(LOW), wm_ref[...])
        pooled_ref[...] = pooled
        embedded_ref[...] = embedded
        unit_ref[...] = embedded * lax.rsqrt(
            jnp.sum(embedded * embedded, -1, keepdims=True) + UNIT_EPS
        )

    def head(self, sums, pool, counts, ws, gains, wm):
        joint = wm.shape[1]
        return call(
            self.head_kernel,
            [
                shaped((self.count, self.width)),
                shaped((self.count, joint)),
                shaped((self.count, joint)),
            ],
            [IN_VMEM] * 6,
            1.5,
            32,
            name="head",
        )(sums, pool, counts, ws, gains, wm)

    def head_back_kernel(
        self,
        grad,
        pooled_ref,
        embedded_ref,
        counts_ref,
        ws_ref,
        gains_ref,
        wm_ref,
        embed_grad_ref,
        final_ref,
        branch_ref,
        pushed_ref,
        gain_ref,
    ):
        embedded = embedded_ref[...]
        inverse_norm = lax.rsqrt(jnp.sum(embedded * embedded, -1, keepdims=True) + UNIT_EPS)
        unit = embedded * inverse_norm
        along = jnp.sum(grad * unit, -1, keepdims=True)
        embed_grad = (inverse_norm * (grad - unit * along)).astype(LOW)
        embed_grad_ref[...] = embed_grad
        unit_rows, inverse = normalize(pooled_ref[...])
        gain = gains_ref[2:3, :]
        final_ref[...] = (unit_rows * gain).astype(LOW)
        pooled_grad, gain_grad = norm_back(
            rows_by(embed_grad, wm_ref[...]), gain, unit_rows, inverse
        )
        gain_ref[...] = gain_grad
        branch = pooled_grad / counts_ref[...]
        branch_ref[...] = branch
        pushed_ref[...] = rows_by(branch.astype(LOW), ws_ref[...])

    def head_back_shapes(self):
        count = self.count
        return [
            shaped((count, self.joint), LOW),
            shaped((count, self.width), LOW),
            shaped((count, self.width)),
            shaped((count, self.hidden)),
            shaped((1, self.width)),
        ]

    def head_back(self, grad, pooled, embedded, counts, ws, gains, wm):
        return call(
            lambda grad_ref, *refs: self.head_back_kernel(grad_ref[...], *refs),
            self.head_back_shapes(),
            [IN_VMEM] * 7,
            1.5,
            32,
            name="head_back",
        )(grad, pooled, embedded, counts, ws, gains, wm)

    def factor_cuts(self, blocks):
        cuts = [0]
        for size in (self.hidden // blocks, self.width, self.width // blocks, self.joint):
            cuts.append(cuts[-1] + size)
        return cuts

    def factor_rows(self, block, blocks, sums, branch, final, embed_grad):
        hidden, width = self.hidden // blocks, self.width // blocks
        return jnp.concatenate(
            [
                sums[:, block * hidden : (block + 1) * hidden],
                branch,
                final[:, block * width : (block + 1) * width].astype(WIDE),
                embed_grad.astype(WIDE),
            ],
            1,
        )

    def over_tokens(self, value):
        shape = (self.count, self.padded, value.shape[-1])
        return jnp.broadcast_to(value[:, None, :], shape).reshape(self.rows, shape[-1])

    def feed_back_kernel(self, length_ref, core_ref, *refs):
        for core in range(2):
            pl.when(core_ref[0] == core)(lambda: self.feed_back_body(core, length_ref, *refs))

    def feed_back_body(
        self,
        core,
        length_ref,
        first_ref,
        gains_ref,
        we_ref,
        pushed_ref,
        branch_ref,
        first_grad_ref,
        near_ref,
        far_ref,
        gain_ref,
    ):
        valid = self.valid(length_ref)
        gain = gains_ref[1:2, :]
        unit_rows, inverse = normalize(first_ref[...])
        second = (unit_rows * gain).astype(LOW)
        blocks, step, _ = near_ref.shape
        total = None
        for block in range(blocks):
            for half in range(2):
                rows = slice((2 * block + half) * step, (2 * block + half + 1) * step)
                expand = we_ref[rows, :]
                hidden = rows_by(second, expand)
                gate = gate_of(hidden)
                slope = gate + (1.702 * hidden) * (gate * (1.0 - gate))
                pushed = self.over_tokens(pushed_ref[:, rows]) * valid
                hidden_grad = (pushed * slope).astype(LOW)
                grads = outer(hidden_grad, second).astype(LOW)
                term = product(hidden_grad, expand)
                total = term if total is None else total + term
                (near_ref if half == core else far_ref)[block] = grads

        second_grad, gain_grad = norm_back(total, gain, unit_rows, inverse)
        gain_ref[...] = gain_grad
        first_grad_ref[...] = self.over_tokens(branch_ref[...]) * valid + second_grad

    def feed_back(self, blocks, lengths, core, first, gains, we, pushed, branch):
        part = (blocks, self.hidden // (2 * blocks), self.width)
        return call(
            self.feed_back_kernel,
            [
                shaped((self.rows, self.width)),
                shaped(part, LOW),
                shaped(part, LOW),
                shaped((1, self.width)),
            ],
            [IN_SMEM] * 2 + [IN_VMEM] * 5,
            13,
            56,
            name="feed_back",
        )(lengths, core, first, gains, we, pushed, branch)

    def attend_back_kernel(
        self,
        core_ref,
        first_grad_ref,
        x_ref,
        normed_ref,
        packed_ref,
        attended_ref,
        gains_ref,
        wa_ref,
        wo_ref,
        token_ref,
        near_ref,
        far_ref,
        gain_ref,
        packed_grad_ref,
        attended_grad_ref,
    ):
        width = self.width
        first_low = first_grad_ref[...].astype(LOW)
        attended_grad_ref[...] = product(first_low, wo_ref[...]).astype(LOW)
        masks = self.quarters()

        def one(number, carry):
            rows = pl.ds(pl.multiple_of(number * self.padded, 16), self.padded)
            for at in range(0, width, BLOCK):
                spots = [slice(at + part * width, at + part * width + BLOCK) for part in range(3)]
                queries = self.stacked(packed_ref[rows, spots[0]], masks)
                keys, values = packed_ref[rows, spots[1]], packed_ref[rows, spots[2]]
                upstream = self.stacked(attended_grad_ref[rows, spots[0]], masks)
                probs = self.probabilities(keys, queries, 0)
                prob_grad = rows_by(values, upstream)
                score_grad = (
                    probs * (prob_grad - jnp.sum(prob_grad * probs, 0, keepdims=True))
                ).astype(LOW)
                scale = HEAD ** (-0.5)
                query_grad = self.unstacked(outer(score_grad, keys), masks) * scale
                packed_grad_ref[rows, spots[0]] = query_grad.astype(LOW)
                packed_grad_ref[rows, spots[1]] = (product(score_grad, queries) * scale).astype(
                    LOW
                )
                packed_grad_ref[rows, spots[2]] = product(probs.astype(LOW), upstream).astype(LOW)
            return carry

        lax.fori_loop(0, self.count, one, 0, unroll=True)
        blocks, half_rows, _ = near_ref.shape
        main_rows = 3 * width // blocks
        rest_rows = width // blocks

        def weights(core):
            def put(block, half, at, value):
                (near_ref if half == core else far_ref)[block, at : at + value.shape[0]] = value

            for block in range(blocks):
                start = block * main_rows
                grads = outer(packed_grad_ref[:, start : start + main_rows], normed_ref[...])
                grads = grads.astype(LOW)
                put(block, 0, 0, grads[:half_rows])
                put(block, 1, 0, grads[half_rows:])
                start = block * rest_rows
                grads = outer(first_low[:, start : start + rest_rows], attended_ref[...])
                put(block, 1, half_rows - rest_rows, grads.astype(LOW))

        pl.when(core_ref[0] == 0)(lambda: weights(0))
        pl.when(core_ref[0] == 1)(lambda: weights(1))
        unit_rows, inverse = normalize(x_ref[...].astype(WIDE))
        input_grad, gain_grad = norm_back(
            product(packed_grad_ref[...], wa_ref[...]), gains_ref[0:1, :], unit_rows, inverse
        )
        gain_ref[...] = gain_grad
        token_ref[...] = (first_grad_ref[...] + input_grad).astype(LOW)

    def attend_back(
        self, blocks, core, first_grad, x, normed, packed, attended, gains, wa, wo
    ):
        rows, width = self.rows, self.width
        part = (blocks, 2 * width // blocks, width)
        return call(
            self.attend_back_kernel,
            [
                shaped((rows, width), LOW),
                shaped(part, LOW),
                shaped(part, LOW),
                shaped((1, width)),
            ],
            [IN_SMEM] + [IN_VMEM] * 8,
            18,
            56,
            [pltpu.VMEM((rows, 3 * width), LOW), pltpu.VMEM((rows, width), LOW)],
            "attend_back",
        )(core, first_grad, x, normed, packed, attended, gains, wa, wo)

    def pad(self, tokens):
        extra = self.padded - self.span
        return jnp.pad(tokens, ((0, 0), (0, extra), (0, 0))).reshape(self.rows, self.width)

    def unpad(self, rows):
        return rows.reshape(self.count, self.padded, self.width)[:, : self.span]


SLOTS = 16


def contrast_kernel(
    images, captions, side, image, row_ref, column_ref, *refs
):
    sources, refs = refs[:8], refs[8:]
    head_refs, outs, (ws_ref, wm_ref, sems) = refs[:6], refs[6:-3], refs[-3:]
    copies = [
        pltpu.make_async_copy(source, target, sems.at[at])
        for at, (source, target) in enumerate(((head_refs[3], ws_ref), (head_refs[5], wm_ref)))
    ]
    for copy in copies:
        copy.start()
    every = jnp.concatenate(
        [ref[...].reshape(-1, ref.shape[-1]) for ref in sources], 0
    )
    sims = rows_by(every, every) * SIM_SCALE
    row_label, column_label = row_ref[...], column_ref[...]
    valid = (row_label >= 0) & (column_label >= 0)
    match = jnp.where(valid & (row_label == column_label), 1.0, 0.0)
    counts = jnp.maximum(jnp.sum(match, 1, keepdims=True), 1.0)
    masked = jnp.where(valid, sims, -1e30)
    row_top = jnp.max(masked, 1, keepdims=True)
    row_raised = jnp.where(valid, jnp.exp(masked - row_top), 0.0)
    row_total = jnp.maximum(jnp.sum(row_raised, 1, keepdims=True), 1e-30)
    column_top = jnp.max(masked, 0, keepdims=True)
    column_raised = jnp.where(valid, jnp.exp(masked - column_top), 0.0)
    column_total = jnp.maximum(jnp.sum(column_raised, 0, keepdims=True), 1e-30)
    picked = sims * match
    image_terms = row_top + jnp.log(row_total) - jnp.sum(picked, 1, keepdims=True) / counts
    caption_terms = column_top + jnp.log(column_total) - jnp.sum(picked, 0, keepdims=True)
    row_at = lax.broadcasted_iota(jnp.int32, image_terms.shape, 0)
    column_at = lax.broadcasted_iota(jnp.int32, caption_terms.shape, 1)
    own_caption = (column_at >= images) & (column_at < images + captions)
    loss = 0.5 * jnp.sum(
        jnp.where(row_at < images, image_terms, 0.0), keepdims=True
    ) + side * jnp.sum(jnp.where(own_caption, caption_terms, 0.0), keepdims=True)
    outs[1][...] = jnp.broadcast_to(loss, outs[1].shape)
    grad = 0.5 * (row_raised / row_total - match / counts) + side * (
        column_raised / column_total - match
    )
    wide = every.astype(WIDE)
    image_grad = jnp.dot(
        grad[:SLOTS], wide, precision=HIGH, preferred_element_type=WIDE
    )
    text_grad = lax.dot_general(
        grad[:, :128],
        wide,
        (((0,), (0,)), ((), ())),
        precision=HIGH,
        preferred_element_type=WIDE,
    )
    outs[0][...] = SIM_SCALE * text_grad[images : images + captions]
    for copy in copies:
        copy.wait()
    pooled_ref, embedded_ref, counts_ref, _, gains_ref, _ = head_refs
    image.head_back_kernel(
        SIM_SCALE * image_grad[:images],
        pooled_ref,
        embedded_ref,
        counts_ref,
        ws_ref,
        gains_ref,
        wm_ref,
        *outs[2:],
    )


def contrast_whole(images, captions, side, row_label, column_label, sources):
    every = jnp.concatenate([item.reshape(-1, item.shape[-1]) for item in sources], 0)
    joint = every.shape[-1]
    slots = every.reshape(-1, SLOTS, joint)
    every_image = slots[:, :images].reshape(-1, joint)
    every_text = slots[:, images : images + captions].reshape(-1, joint)
    image_ids = row_label.reshape(-1, SLOTS)[:, :images].reshape(-1)
    named = column_label.reshape(-1, SLOTS)[:, images : images + captions].reshape(-1)
    match = (named[None, :] == image_ids[:, None]).astype(WIDE)
    counts = jnp.sum(match, 1, keepdims=True)
    sims = rows_by(every_image, every_text) * SIM_SCALE
    row_log = jax.scipy.special.logsumexp(sims, axis=1, keepdims=True)
    col_log = jax.scipy.special.logsumexp(sims, axis=0, keepdims=True)
    image_terms = row_log - jnp.sum(sims * match, 1, keepdims=True) / counts
    caption_terms = col_log - jnp.sum(sims * match, 0, keepdims=True)
    loss_part = 0.5 * jnp.sum(image_terms[:images]) + side * jnp.sum(caption_terms[:, :captions])
    grad = 0.5 * (jnp.exp(sims - row_log) - match / counts) + side * (
        jnp.exp(sims - col_log) - match
    )
    image_unit_grad = SIM_SCALE * jnp.dot(
        grad[:images], every_text.astype(WIDE), precision=HIGH
    )
    text_unit_grad = SIM_SCALE * lax.dot_general(
        grad[:, :captions],
        every_image.astype(WIDE),
        (((0,), (0,)), ((), ())),
        precision=HIGH,
        preferred_element_type=WIDE,
    )
    return image_unit_grad, text_unit_grad, jnp.broadcast_to(loss_part, (1, 128))


def contrast_labels(place, images, captions, caption_image):
    numbers = spread_numbers(place)
    at = jnp.arange(SLOTS, dtype=jnp.int32)[None, :]
    image_ids = jnp.where(at < images, numbers[:, None] * images + at, -1)
    named = jnp.take(caption_image.reshape(-1, captions), numbers, axis=0)
    named = jnp.pad(
        named, ((0, 0), (images, SLOTS - images - captions)), constant_values=-1
    )
    return image_ids.reshape(-1, 1), named.reshape(1, -1)


def contrast(place, image, head, image_unit, text_unit, row_label, column_label):
    images, captions, joint = image_unit.shape[0], text_unit.shape[0], text_unit.shape[1]
    blank = jnp.zeros((SLOTS - images - captions, joint), LOW)
    units = jnp.concatenate([image_unit.astype(LOW), text_unit.astype(LOW), blank], 0)
    sources = gather_units(place, units)
    side = 0.5 * images / captions
    if len(sources) > 8:
        image_grad, text_grad, loss_part = contrast_whole(
            images, captions, side, row_label, column_label, sources
        )
        return [text_grad, loss_part] + list(image.head_back(image_grad, *head))
    return call(
        lambda *refs: contrast_kernel(images, captions, side, image, *refs),
        [shaped((captions, joint)), shaped((1, 128))] + image.head_back_shapes(),
        [IN_VMEM] * 13 + [IN_PLACE, IN_VMEM, IN_PLACE],
        5,
        56,
        [
            pltpu.VMEM(head[3].shape, LOW),
            pltpu.VMEM(head[5].shape, LOW),
            pltpu.SemaphoreType.DMA((2,)),
        ],
        name="contrast",
    )(row_label, column_label, *sources, *head)


def together(*values):
    return lax.optimization_barrier(values)


class Factors:
    def __init__(self, place, packed, image, text):
        self.place, self.towers = place, (image, text)
        self.messages = [pick(packed, place.ns ^ mask, 0) for mask in range(place.n_ns)]

    def over_ns(self):
        place = self.place
        self.messages = [
            place.swap_ns(item, mask) if mask else item for mask, item in enumerate(self.messages)
        ]

    def stack(self):
        self.blocks = jnp.stack(self.messages)

    def every(self):
        place = self.place
        sources = self.own + [self.far[at] for at in range(4)]
        every = lay_spread(place, sources, "place_factors")
        every = every.reshape((-1,) + every.shape[3:])
        for mask in place.extra:
            other = place.swap_mask(every, mask)
            every = jnp.where(
                (place.dp & mask) == 0,
                jnp.concatenate([every, other], 0),
                jnp.concatenate([other, every], 0),
            )
        return every.reshape(-1, every.shape[-1])

    def products(self, every, dot):
        image, text = self.towers
        blocks = self.place.n_ns
        slot = lax.broadcasted_iota(jnp.int32, (every.shape[0], 1), 0) % SLOTS
        outs = []
        for tower, own in ((image, slot < image.count), (text, slot >= SLOTS - text.count)):
            cuts = tower.factor_cuts(blocks)
            held = every * jnp.where(own, 1.0, 0.0).astype(LOW)
            pieces = [held[:, low:high] for low, high in zip(cuts, cuts[1:])]
            outs += [dot(pieces[0], pieces[1]), dot(pieces[2], pieces[3])]
        return outs

    def kernel(self, index_ref, *refs):
        own_refs, far_ref, outs, every_ref = refs[:4], refs[4], refs[5:9], refs[9]
        rows = every_ref.shape[0] // 8
        for at in range(8):
            to = pl.ds(pl.multiple_of(index_ref[at] * rows, rows), rows)
            source = own_refs[at][...] if at < 4 else far_ref[at - 4]
            every_ref[to] = source.reshape(rows, source.shape[-1])
        for out_ref, value in zip(outs, self.products(every_ref[...], outer)):
            out_ref[...] = value

    def gradients(self):
        place = self.place
        if place.extra:
            return self.products(self.every(), outer)
        image, text = self.towers
        blocks, core = place.n_ns, place.core
        index = jnp.stack(
            [
                chip * 2 + (core if at < 4 else 1 - core)
                for at, chip in enumerate(place.spread_owners())
            ]
        ).astype(jnp.int32)
        columns = self.own[0].shape[-1]
        out_shape = []
        for tower in (image, text):
            out_shape.append(shaped((tower.hidden // blocks, tower.width)))
            out_shape.append(shaped((tower.width // blocks, tower.joint)))
        return call(
            self.kernel,
            out_shape,
            [IN_SMEM] + [IN_VMEM] * 5,
            4,
            48,
            [pltpu.VMEM((8 * blocks * SLOTS, columns), LOW)],
            name="factor_grads",
        )(index, *self.own, self.far)


def pack_factors(blocks, image, text, image_parts, text_parts):
    columns = max(image.factor_cuts(blocks)[-1], text.factor_cuts(blocks)[-1])

    def body(*refs):
        out_ref = refs[8]
        first, second = [ref[...] for ref in refs[:4]], [ref[...] for ref in refs[4:8]]
        out_ref[...] = jnp.zeros(out_ref.shape, LOW)
        for block in range(blocks):
            rows = image.factor_rows(block, blocks, *first)
            lower = jnp.zeros((SLOTS - text.count - image.count, rows.shape[1]), WIDE)
            rows = jnp.concatenate([rows, lower], 0)
            more = text.factor_rows(block, blocks, *second)
            blank = jnp.zeros((text.count, columns - more.shape[1]), WIDE)
            more = jnp.concatenate([more, blank], 1)
            out_ref[block] = jnp.concatenate([rows, more], 0).astype(LOW)

    return call(
        body,
        shaped((blocks, SLOTS, columns), LOW),
        [IN_VMEM] * 8,
        1,
        32,
        name="pack_factors",
    )(*image_parts, *text_parts)


class Fresh:
    def __init__(self, place, units, others, owners, per_chip):
        self.place, self.units, self.others = place, units, others
        self.owners, self.per_chip = owners, per_chip
        self.width = units[0][0].shape[1]
        self.rows = sum(item.shape[0] for item in units[0])
        self.pairs = TRI3 if per_chip else TRI2

    def body(self, info_ref, *refs):
        moments = [item for unit in self.units for item in unit]
        total = len(moments) + len(self.others)
        sources, refs = refs[:8], refs[8:]
        grads, refs = refs[: len(self.others)], refs[len(self.others) :]
        moment_refs, refs = refs[:total], refs[total:]
        fresh_refs, part_refs = refs[:total], refs[total:-2]
        chosen_ref, gram_ref = refs[-2:]
        size = self.rows // 8

        def freshen(at, rows, gradient):
            fresh_refs[at][rows] = MOMENTUM * moment_refs[at][rows] + gradient.astype(WIDE)

        for number, source in enumerate(sources):
            piece = info_ref[6 + number]
            at = 0
            for unit_at, unit in enumerate(self.units):
                split = unit[0].shape[0] // size

                def rows(first):
                    return pl.ds(pl.multiple_of((piece - first) * size, size), size)

                if split == 8:
                    freshen(at, rows(0), source[unit_at])
                else:
                    pl.when(piece < split)(
                        lambda: freshen(at, rows(0), source[unit_at])
                    )
                    pl.when(piece >= split)(
                        lambda: freshen(at + 1, rows(split), source[unit_at])
                    )
                at += len(unit)
        for number, grad in enumerate(grads):
            freshen(len(moments) + number, slice(None), grad[...])
        for owner, at in enumerate(self.owners):

            @pl.when(info_ref[0] == owner)
            def _():
                held = fresh_refs[at].shape[0]
                chosen_ref[:held] = fresh_refs[at][...].astype(LOW)
                if held < self.rows:
                    chosen_ref[held:] = jnp.zeros((self.rows - held, self.width), LOW)

        @pl.when(info_ref[0] >= len(self.owners))
        def _():
            chosen_ref[...] = jnp.zeros((self.rows, self.width), LOW)

        def blocks(pairs):
            for number, (i, j) in enumerate(pairs):
                left = chosen_ref[:, i * BLOCK : (i + 1) * BLOCK]
                right = chosen_ref[:, j * BLOCK : (j + 1) * BLOCK]
                gram_ref[number * BLOCK : (number + 1) * BLOCK] = outer(left, right).astype(LOW)

        if self.per_chip:
            pl.when(info_ref[1] == 0)(lambda: blocks(self.pairs[:3]))
            pl.when(info_ref[1] == 1)(lambda: blocks(self.pairs[3:]))
        else:
            blocks(self.pairs)
        size = gram_ref.shape[0] // len(part_refs)
        for number, part_ref in enumerate(part_refs):
            at = info_ref[2 + number]
            part_ref[...] = gram_ref[pl.ds(pl.multiple_of(at * size, size), size)]

    def make(self, sources, grads):
        place = self.place
        moments = [item for unit in self.units for item in unit] + list(self.others)
        owner = place.chip if self.per_chip else place.chip * 2 + place.core
        info = jnp.concatenate(
            [
                jnp.stack([owner, place.core]).astype(jnp.int32),
                place.blocks_at,
                jnp.stack(place.spread_pieces()).astype(jnp.int32),
            ]
        )
        part = shaped((3 * BLOCK // place.n_ns, BLOCK), LOW)
        out = call(
            self.body,
            [shaped(item.shape) for item in moments] + [part] * place.n_ns,
            [IN_SMEM] + [IN_VMEM] * (8 + len(grads) + len(moments)),
            5,
            56,
            [
                pltpu.VMEM((self.rows, self.width), LOW),
                pltpu.VMEM((3 * BLOCK, BLOCK), LOW),
            ],
            "freshen",
        )(info, *sources, *grads, *moments)
        return out[: len(moments)], out[len(moments) :]


def polynomial_kernel(side, pairs, info_ref, *refs):
    count = info_ref.shape[0] - 1
    parts, out_ref, gram_ref = refs[:-2], refs[-2], refs[-1]
    size = parts[0].shape[0]
    core = info_ref[count]
    for number, part in enumerate(parts):
        at = info_ref[number % count]
        half = 0 if side == 2 else (core if number < count else 1 - core)
        gram_ref[half, pl.ds(pl.multiple_of(at * size, size), size)] = part[...]
    blocks = {
        pair: gram_ref[at // 3, at % 3 * BLOCK : (at % 3 + 1) * BLOCK].astype(WIDE)
        for at, pair in enumerate(pairs)
    }
    rows = [
        jnp.concatenate(
            [blocks[(i, j)] if i <= j else blocks[(j, i)].T for j in range(side)], 1
        )
        for i in range(side)
    ]
    square = jnp.concatenate(rows, 0)
    span = side * BLOCK
    same = lax.broadcasted_iota(jnp.int32, (span, span), 0) == lax.broadcasted_iota(
        jnp.int32, (span, span), 1
    )
    factor = 1.0 / (jnp.sqrt(jnp.sum(jnp.where(same, square, 0.0))) + 1e-07)
    square = square * (factor * factor)

    def mm(left, right):
        return product(left.astype(LOW), right.astype(LOW))

    def terms(value):
        return COEF_B * value + COEF_C * mm(value, value)

    def following(value, term):
        half = COEF_A * value + mm(value, term)
        return COEF_A * half + mm(half, term)

    term_zero = terms(square)
    square = following(square, term_zero)
    term_one = terms(square)
    square = following(square, term_one)
    term_two = terms(square)
    both = COEF_A * (term_zero + term_one) + mm(term_zero, term_one)
    whole = COEF_A**2 * term_two + COEF_A * both + mm(both, term_two)
    whole = factor * (whole + jnp.where(same, COEF_A**3, 0.0))

    def give(chosen):
        for at, (i, j) in enumerate(chosen):
            out_ref[at] = whole[
                i * BLOCK : (i + 1) * BLOCK, j * BLOCK : (j + 1) * BLOCK
            ].astype(LOW)

    if side == 2:
        give(pairs)
    else:
        pl.when(core == 0)(lambda: give(pairs[:3]))
        pl.when(core == 1)(lambda: give(pairs[3:]))


def polynomial(place, parts, side, pairs):
    return call(
        lambda *refs: polynomial_kernel(side, pairs, *refs),
        shaped((3, BLOCK, BLOCK), LOW),
        [IN_SMEM] + [IN_VMEM] * len(parts),
        4 if side == 2 else 10,
        60,
        [pltpu.VMEM((len(pairs) // 3, 3 * BLOCK, BLOCK), LOW)],
        name="polynomial",
    )(jnp.concatenate([place.blocks_at, place.core_at]), *parts)


def apply_kernel(side, pairs, scale, fresh_ref, poly_ref, master_ref, out_ref):
    fresh = fresh_ref[...].astype(LOW)
    at_of = {pair: at for at, pair in enumerate(pairs)}
    for j in range(side):
        total = None
        for i in range(side):
            left = fresh[:, i * BLOCK : (i + 1) * BLOCK]
            block = poly_ref[at_of[(min(i, j), max(i, j))]]
            term = product(left, block) if i <= j else rows_by(left, block)
            total = term if total is None else total + term
        columns = slice(j * BLOCK, (j + 1) * BLOCK)
        out_ref[:, columns] = master_ref[:, columns] - scale * total


def apply_polynomial(master, fresh, blocks, scale):
    rows, width = master.shape
    side = width // BLOCK
    pairs = TRI3 if side == 3 else TRI2
    tile = rows
    while tile > 256:
        tile = tile // 2 if tile % 512 == 0 or tile % 3 else tile // 3
    row_spec = pl.BlockSpec((tile, width), lambda i: (i, 0))
    return pl.pallas_call(
        lambda *refs: apply_kernel(side, pairs, scale, *refs),
        out_shape=shaped(master.shape),
        grid=(rows // tile,),
        in_specs=[row_spec, pl.BlockSpec(blocks.shape, lambda i: (0, 0, 0)), row_spec],
        out_specs=row_spec,
        compiler_params=pltpu.CompilerParams(vmem_limit_bytes=32 << 20),
        cost_estimate=pl.CostEstimate(
            flops=2 * rows * width * width, bytes_accessed=12 * rows * width, transcendentals=0
        ),
        name="apply_polynomial",
    )(fresh, blocks, master)


def per_device(
    image_tokens,
    text_tokens,
    caption_image,
    caption_length,
    image_attention,
    image_output,
    image_expand,
    image_shrink,
    image_embedding,
    text_attention,
    text_output,
    text_expand,
    text_shrink,
    text_embedding,
    image_gains,
    text_gains,
    image_attention_momentum,
    image_output_momentum,
    image_expand_momentum,
    image_shrink_momentum,
    image_embedding_momentum,
    text_attention_momentum,
    text_output_momentum,
    text_expand_momentum,
    text_shrink_momentum,
    text_embedding_momentum,
    image_gains_momentum,
    text_gains_momentum,
):
    place = Place()
    count = place.n_ns
    em_rows, te_rows = image_embedding.shape[0], text_embedding.shape[0]
    joint = text_embedding.shape[1]
    embedding_padded = jnp.pad(text_embedding, ((0, em_rows - te_rows), (0, 0)))
    bundles = (
        ((text_attention, text_output),),
        ((text_expand,), (text_shrink,)),
        ((image_attention, image_output), (image_embedding, embedding_padded)),
        ((image_expand,), (image_shrink,)),
    )
    pieces = cut_pieces(place, bundles)
    one = Bundle(place, pieces[0], bundles[0])
    one.hops_direct()
    two = Bundle(place, after(pieces[1], *one.hops), bundles[1])
    two.hops_direct()
    three = Bundle(place, after(pieces[2], *one.hops), bundles[2])
    three.hops_ring()
    four = Bundle(place, after(pieces[3], three.hops[0]), bundles[3])
    four.hops_ring()
    one.first_links()
    one.second_link()
    two.first_links()
    three.first_links(*two.own[1:])
    four.first_links(*three.own[1:])

    images, image_span, image_width = image_tokens.shape
    captions, text_span, text_width = text_tokens.shape
    image = Tower(images, image_span, image_width, image_expand.shape[0] * count, HI, joint, False)
    text = Tower(captions, text_span, text_width, text_expand.shape[0] * count, HT, joint, True)
    image_lengths = jnp.full((images,), image_span, jnp.int32)
    image_counts = jnp.full((images, 1), image_span, WIDE)
    text_counts = caption_length.astype(WIDE).reshape(captions, 1)
    core = place.core.astype(jnp.int32).reshape(1)

    ta_low, to_low = one.lay()
    row_label, column_label = contrast_labels(place, images, captions, caption_image)
    tx = text.pad(text_tokens)
    t_normed, t_packed, t_attended, t_first = text.attend(
        after(tx, row_label, column_label), text_gains, ta_low, to_low
    )
    two.second_link(t_attended)
    te_low, ts_low = two.lay()
    t_sums, t_pool = text.feed(caption_length, t_first, text_gains, te_low)
    three.second_link(t_sums)
    ia_low, io_low, im_low, tm_low = three.lay()
    tm_low = tm_low.reshape(count, em_rows, joint)[:, :te_rows].reshape(-1, joint)
    t_pooled, t_embedded, t_unit = text.head(
        t_sums, t_pool, text_counts, ts_low, text_gains, tm_low
    )
    ix = image.pad(image_tokens)
    i_normed, i_packed, i_attended, i_first = image.attend(ix, image_gains, ia_low, io_low)
    four.second_link(i_attended)
    ie_low, is_low = four.lay()
    i_sums, i_pool = image.feed(image_lengths, i_first, image_gains, ie_low)
    i_pooled, i_embedded, i_unit = image.head(
        i_sums, i_pool, image_counts, is_low, image_gains, im_low
    )

    (
        text_unit_grad,
        loss_part,
        i_embed_grad,
        i_final,
        i_branch,
        i_pushed,
        i_gain_final,
    ) = contrast(
        place,
        image,
        (i_pooled, i_embedded, image_counts, is_low, image_gains, im_low),
        i_unit,
        t_unit,
        row_label,
        column_label,
    )
    i_first_grad, i_near, i_far, i_gain_second = image.feed_back(
        count, image_lengths, core, i_first, image_gains, ie_low, i_pushed, i_branch
    )
    sum_ie = RowSum(place, i_near, i_far)
    t_embed_grad, t_final, t_branch, t_pushed, t_gain_final = text.head_back(
        after(text_unit_grad, i_first_grad),
        t_pooled,
        t_embedded,
        text_counts,
        ts_low,
        text_gains,
        tm_low,
    )
    packed = pack_factors(
        count,
        image,
        text,
        (i_sums, i_branch, i_final, i_embed_grad),
        (t_sums, t_branch, t_final, t_embed_grad),
    )
    sum_ie.got, packed, t_pushed = together(sum_ie.got, packed, t_pushed)
    factors = Factors(place, packed, image, text)
    sum_ie.step_one()
    factors.over_ns()
    i_back = image.attend_back(
        count,
        core,
        after(i_first_grad, sum_ie.sent, packed),
        ix,
        i_normed,
        i_packed,
        i_attended,
        image_gains,
        ia_low,
        io_low,
    )
    i_back, sum_ie.got, factors.messages = together(i_back, sum_ie.got, factors.messages)
    i_token_grad, i_near, i_far, i_gain_first = i_back
    factors.stack()
    sum_iao = RowSum(place, i_near, i_far)
    sum_ie.step_two()
    factors.spread = Spread(place, factors.blocks)
    t_back = text.feed_back(
        count,
        caption_length,
        core,
        after(t_first, sum_ie.sent, i_far, factors.blocks),
        text_gains,
        te_low,
        t_pushed,
        t_branch,
    )
    t_back, sum_ie.got, sum_iao.got, flown = together(
        t_back, sum_ie.got, sum_iao.got, factors.spread.flying()
    )
    factors.spread.landed(flown)
    t_first_grad, t_near, t_far, t_gain_second = t_back
    sum_te = RowSum(place, t_near, t_far)
    sum_ie.step_three()
    sum_iao.step_one()
    factors.spread.more()
    t_back = text.attend_back(
        count,
        core,
        after(t_first_grad, sum_ie.sent, sum_iao.sent, t_far),
        tx,
        t_normed,
        t_packed,
        t_attended,
        text_gains,
        ta_low,
        to_low,
    )
    t_back, sum_ie.got, sum_iao.got, sum_te.got, factors.spread.own = together(
        t_back, sum_ie.got, sum_iao.got, sum_te.got, factors.spread.own
    )
    t_token_grad, t_near, t_far, t_gain_first = t_back

    sum_tao = RowSum(place, t_near, t_far)
    sum_iao.step_two()
    sum_te.step_one()
    far = place.swap_core(jnp.stack(factors.spread.own))
    sum_iao.got, sum_te.got, sum_tao.got, far = together(
        sum_iao.got, sum_te.got, sum_tao.got, far
    )
    factors.own, factors.far = factors.spread.own, far

    sum_tao.step_one()
    sum_iao.step_three()
    sum_te.step_two()
    grad_is, grad_im, grad_ts, grad_tm = factors.gradients()
    sum_iao.got, sum_te.got, sum_tao.got, grad_is, grad_im, grad_ts, grad_tm = together(
        sum_iao.got, sum_te.got, sum_tao.got, grad_is, grad_im, grad_ts, grad_tm
    )

    sum_ie.step_four()
    sum_iao.step_four()
    kept, got = last_step(place, (sum_ie, sum_iao))
    sum_tao.step_two()
    sum_te.step_three()
    kept, got, sum_te.got, sum_tao.got = together(kept, got, sum_te.got, sum_tao.got)

    image_spread = Spread(place, kept + got)
    sum_tao.step_three()
    flown, sum_tao.got = together(image_spread.flying(), sum_tao.got)
    image_spread.landed(flown)

    more = image_spread.more()
    sum_te.step_four()
    sum_tao.step_four()
    kept, got = last_step(place, (sum_te, sum_tao))
    image_spread.own[3], kept, got = together(more, kept, got)
    image_sources = image_spread.finish()

    fresh_image = Fresh(
        place,
        ((image_expand_momentum,), (image_attention_momentum, image_output_momentum)),
        (image_shrink_momentum,),
        (0, 3, 1, 2),
        True,
    )
    fresh_text = Fresh(
        place,
        ((text_expand_momentum,), (text_attention_momentum, text_output_momentum)),
        (text_shrink_momentum, image_embedding_momentum, text_embedding_momentum),
        (0, 3, 1, 2, 4, 5),
        False,
    )
    text_spread = Spread(place, kept + got)
    image_sources, held = together(image_sources, text_spread.own[0])
    made = fresh_image.make(image_sources, [grad_is])
    small = pack_small(
        loss_part[0, 0],
        jnp.concatenate([i_gain_first, i_gain_second, i_gain_final], 0),
        jnp.concatenate([t_gain_first, t_gain_second, t_gain_final], 0),
    )
    other = place.swap_mask(after(small, held), 1)
    made, flown, other = together(made, text_spread.flying(), other)
    small = small + other
    text_spread.landed(flown)
    (fresh_ie, fresh_ia, fresh_io, fresh_is), parts = made

    parts = over_ns(place, parts)
    more = text_spread.more()
    parts, text_spread.own[3] = together(parts, more)
    text_sources = text_spread.finish()

    parts = total_of(place, parts)
    text_sources, parts = together(text_sources, parts)
    made = fresh_text.make(text_sources, [grad_ts, grad_im, grad_tm])
    parts = over_ns(place, parts)
    other = place.swap_mask(after(small, text_sources[0]), 2)
    made, parts, other = together(made, parts, other)
    small = small + other
    (fresh_te, fresh_ta, fresh_to, fresh_ts, fresh_im, fresh_tm), text_parts = made

    parts, text_parts = together(
        parts + [place.swap_core(part) for part in parts], text_parts
    )
    image_poly = polynomial(place, parts, 3, TRI3)
    text_parts = over_ns(place, text_parts)
    other = place.swap_mask(after(small, parts[0]), 4)
    image_poly, text_parts, other = together(image_poly, text_parts, other)
    small = small + other

    image_spread = Spread(place, image_poly)
    text_parts = over_ns(place, total_of(place, text_parts))
    flown, text_parts = together(image_spread.flying(), text_parts)
    image_spread.landed(flown)

    text_poly = polynomial(place, text_parts, 2, TRI2)
    more = image_spread.more()
    other = place.swap_ns(after(small, text_parts[0]), 1)
    text_poly, image_spread.own[3], other = together(text_poly, more, other)
    small = small + other
    image_sources = image_spread.finish()

    text_spread = Spread(place, text_poly)
    image_poly = lay_spread(place, image_sources, "place_polynomials")
    image_poly = image_poly.reshape(4, 6, BLOCK, BLOCK)
    other = place.swap_ns(after(small, text_poly), 2)

    def updated(master, fresh, blocks):
        rows, width = master.shape
        return apply_polynomial(master, fresh, blocks, RATE * math.sqrt(rows * count / width))

    image_weights = [
        updated(image_expand, fresh_ie, image_poly[0]),
        updated(image_shrink, fresh_is, image_poly[1]),
        updated(image_attention, fresh_ia, image_poly[2]),
        updated(image_output, fresh_io, image_poly[3]),
    ]
    image_weights, flown, other = together(image_weights, text_spread.flying(), other)
    small = small + other
    for mask in place.extra:
        small = small + place.swap_mask(small, mask)
    next_ie, next_is, next_ia, next_io = image_weights
    text_spread.landed(flown)
    text_spread.more()
    text_poly = lay_spread(place, text_spread.finish(), "place_polynomials")
    text_poly = text_poly.reshape(8, 3, BLOCK, BLOCK)
    loss_total, image_gain_sum = small[6, 0], small[:3]
    text_gain_sum = small[3:6, : text_gains.shape[1]]
    image_gain_next = MOMENTUM * image_gains_momentum + image_gain_sum
    text_gain_next = MOMENTUM * text_gains_momentum + text_gain_sum
    loss = jnp.reshape(loss_total / (images * place.n_dp * count), (1,))
    return (
        loss,
        image.unpad(i_token_grad),
        text.unpad(t_token_grad),
        fresh_ia,
        fresh_io,
        fresh_ie,
        fresh_is,
        fresh_im,
        fresh_ta,
        fresh_to,
        fresh_te,
        fresh_ts,
        fresh_tm,
        next_ia,
        next_io,
        next_ie,
        next_is,
        updated(image_embedding, fresh_im, text_poly[4]),
        updated(text_attention, fresh_ta, text_poly[2]),
        updated(text_output, fresh_to, text_poly[3]),
        updated(text_expand, fresh_te, text_poly[0]),
        updated(text_shrink, fresh_ts, text_poly[1]),
        updated(text_embedding, fresh_tm, text_poly[5]),
        image_gain_next,
        text_gain_next,
        image_gains - GAIN_RATE * image_gain_next,
        text_gains - GAIN_RATE * text_gain_next,
    )


def solution(mesh):
    placed = (
        P(("dp", "ns"), None, None),
        P(("dp", "ns"), None, None),
        P(),
        P(("dp", "ns")),
        P("ns", None),
        P("ns", None),
        P("ns", None),
        P("ns", None),
        P("ns", None),
        P("ns", None),
        P("ns", None),
        P("ns", None),
        P("ns", None),
        P("ns", None),
        P(),
        P(),
        P("ns", None),
        P("ns", None),
        P("ns", None),
        P("ns", None),
        P("ns", None),
        P("ns", None),
        P("ns", None),
        P("ns", None),
        P("ns", None),
        P("ns", None),
        P(),
        P(),
    )
    return jax.shard_map(
        per_device,
        mesh=mesh,
        in_specs=placed,
        out_specs=(
            P(),
            P(("dp", "ns"), None, None),
            P(("dp", "ns"), None, None),
            P("ns", None),
            P("ns", None),
            P("ns", None),
            P("ns", None),
            P("ns", None),
            P("ns", None),
            P("ns", None),
            P("ns", None),
            P("ns", None),
            P("ns", None),
            P("ns", None),
            P("ns", None),
            P("ns", None),
            P("ns", None),
            P("ns", None),
            P("ns", None),
            P("ns", None),
            P("ns", None),
            P("ns", None),
            P("ns", None),
            P(),
            P(),
            P(),
            P(),
        ),
        check_vma=False,
    )
```

```python
import math

import jax
import jax.numpy as jnp
from jax import lax
from jax.experimental import pallas as pl
from jax.experimental.pallas import tpu as pltpu
from jax.sharding import PartitionSpec as P

HI = 12
HT = 8
HEAD = 64

NORM_EPS = 1e-05
UNIT_EPS = 1e-06
SIM_SCALE = 30.0
MOMENTUM = 0.95
RATE = 0.5
GAIN_RATE = 0.5
COEF_A = 3.4445
COEF_B = -4.775
COEF_C = 2.0315
MASKED = -1000000000.0
HIGH = lax.Precision.HIGHEST
LOW = jnp.bfloat16
WIDE = jnp.float32

TRI3 = ((0, 0), (0, 1), (0, 2), (1, 1), (1, 2), (2, 2))
TRI2 = ((0, 0), (0, 1), (1, 1))
BLOCK = 256
IN_VMEM = pl.BlockSpec(memory_space=pltpu.VMEM)
IN_SMEM = pl.BlockSpec(memory_space=pltpu.SMEM)
IN_PLACE = pl.BlockSpec(memory_space=pl.ANY)


def call(body, out_shape, specs, micros, limit, scratch=(), name=None):
    outs = jax.tree.map(lambda _: IN_VMEM, out_shape)
    return pl.pallas_call(
        body,
        out_shape=out_shape,
        in_specs=specs,
        out_specs=outs,
        scratch_shapes=list(scratch),
        compiler_params=pltpu.CompilerParams(vmem_limit_bytes=limit << 20),
        cost_estimate=pl.CostEstimate(
            flops=int(1e4 * micros), bytes_accessed=16, transcendentals=0
        ),
        name=name,
    )


def after(value, *others):
    return lax.optimization_barrier((value,) + others)[0]


def shaped(shape, dtype=WIDE):
    return jax.ShapeDtypeStruct(shape, dtype)


class Place:
    def __init__(self):
        self.n_dp = lax.axis_size("dp")
        self.n_ns = lax.axis_size("ns")
        self.dp = lax.axis_index("dp")
        self.ns = lax.axis_index("ns")
        self.core = self.dp & 1
        along_x = (self.dp >> 1) & 1
        along_y = (self.dp >> 2) & 1
        self.bit_one = jnp.where(self.core == 0, along_x, along_y)
        self.bit_two = jnp.where(self.core == 0, along_y, along_x)
        self.chip = (self.dp >> 1) & 3
        self.piece = self.core * 4 + self.bit_one * 2 + self.bit_two
        self.extra = [1 << bit for bit in range(3, self.n_dp.bit_length() - 1)]
        self.core_at = self.core.astype(jnp.int32).reshape(1)
        self.blocks_at = jnp.stack([self.ns ^ mask for mask in range(self.n_ns)]).astype(jnp.int32)

    def over_dp(self, value, target):
        return lax.ppermute(value, "dp", [(i, target(i)) for i in range(self.n_dp)])

    def swap_mask(self, value, mask):
        return self.over_dp(value, lambda i: i ^ mask)

    def swap_core(self, value):
        return self.swap_mask(value, 1)

    def swap_one(self, value):
        return self.over_dp(value, lambda i: i ^ (2 if i % 2 == 0 else 4))

    def swap_two(self, value):
        return self.over_dp(value, lambda i: i ^ (4 if i % 2 == 0 else 2))

    def ring(self, value, steps=1):
        count = self.n_ns
        return lax.ppermute(value, "ns", [(i, (i + steps) % count) for i in range(count)])

    def swap_ns(self, value, mask):
        return lax.ppermute(value, "ns", [(i, i ^ mask) for i in range(self.n_ns)])

    def spread(self, value):
        first = self.swap_one(value)
        own = [value, first, self.swap_two(value), self.swap_two(first)]
        return own + [self.swap_core(item) for item in own]

    def spread_pieces(self):
        own = [self.piece ^ ((k & 1) * 2) ^ (k >> 1) for k in range(4)]
        base = (1 - self.core) * 4 + self.bit_two * 2 + self.bit_one
        return own + [base ^ ((k & 1) * 2) ^ (k >> 1) for k in range(4)]

    def spread_owners(self):
        mask_one = jnp.where(self.core == 0, 1, 2)
        mask_two = 3 - mask_one
        own = [self.chip ^ ((k & 1) * mask_one) ^ ((k >> 1) * mask_two) for k in range(4)]
        far = [self.chip ^ ((k & 1) * mask_two) ^ ((k >> 1) * mask_one) for k in range(4)]
        return own + far


class Spread:
    def __init__(self, place, value):
        self.place = place
        self.own = [value, place.swap_one(value), place.swap_two(value)]

    def flying(self):
        return self.own[1:]

    def landed(self, flown):
        self.own = [self.own[0]] + list(flown)

    def more(self):
        self.own.append(self.place.swap_two(self.own[1]))
        return self.own[3]

    def finish(self):
        return self.own + [self.place.swap_core(item) for item in self.own]


def pick(value, index, axis):
    return lax.dynamic_index_in_dim(value, index, axis, keepdims=False)


def unit_sizes(unit):
    rows, width = unit[0].shape
    if len(unit) == 1:
        return rows // 8, width, 8, 0
    rest = unit[1].shape[0]
    split = 6 if rest * 6 <= rows * 2 else 4
    return rows // split, width, split, rest // (8 - split)


def cut_kernel(sizes, at_ref, *refs):
    count = sum(2 if unit[2] < 8 else 1 for bundle in sizes for unit in bundle)
    units = [unit for bundle in sizes for unit in bundle]
    weights, outs = refs[:count], refs[count : count + len(sizes)]
    held, sems = refs[count + len(sizes) : -1], refs[-1]
    piece = at_ref[0]
    waits = []
    at = 0
    for number, (rows, _, split, rest) in enumerate(units):
        low = pltpu.make_async_copy(
            weights[at].at[pl.ds(pl.multiple_of(jnp.minimum(piece, split - 1) * rows, 8), rows)],
            held[number],
            sems.at[number],
        )
        at += 1
        if split == 8:
            low.start()
            waits.append(((None, low),))
            continue
        high = pltpu.make_async_copy(
            weights[at].at[pl.ds(pl.multiple_of(jnp.maximum(piece - split, 0) * rest, 8), rest)],
            held[number].at[:rest],
            sems.at[number],
        )
        at += 1
        if rest < rows:
            held[number][rest:] = jnp.zeros((rows - rest, held[number].shape[1]), WIDE)
        pl.when(piece < split)(low.start)
        pl.when(piece >= split)(high.start)
        waits.append(((piece < split, low), (piece >= split, high)))
    number = 0
    for bundle, out in zip(sizes, outs):
        row = 0
        for rows, width, _, _ in bundle:
            for condition, copy in waits[number]:
                if condition is None:
                    copy.wait()
                else:
                    pl.when(condition)(copy.wait)
            for column in range(0, width, BLOCK):
                out[row : row + rows] = held[number][:, column : column + BLOCK].astype(LOW)
                row += rows
            number += 1


def cut_pieces(place, bundles):
    sizes = [[unit_sizes(unit) for unit in bundle] for bundle in bundles]
    flat = [unit for bundle in sizes for unit in bundle]
    weights = [item for bundle in bundles for unit in bundle for item in unit]
    out_shape = [
        shaped((sum(unit[0] * unit[1] // BLOCK for unit in bundle), BLOCK), LOW)
        for bundle in sizes
    ]
    return call(
        lambda *refs: cut_kernel(sizes, *refs),
        out_shape,
        [IN_SMEM] + [IN_PLACE] * len(weights),
        1,
        56,
        [pltpu.VMEM(unit[:2], WIDE) for unit in flat]
        + [pltpu.SemaphoreType.DMA((len(flat),))],
        "cut_pieces",
    )(place.piece.astype(jnp.int32).reshape(1), *weights)


def lay_kernel(sizes, index_ref, *refs):
    count = sum(2 if unit[2] < 8 else 1 for unit in sizes)
    weights, sources, outs = refs[:count], refs[count : count + 8], refs[count + 8 :]
    at = row = 0
    for rows, width, split, rest in sizes:
        parts = ((8, rows),) if split == 8 else ((split, rows), (8 - split, rest))
        for part, (pieces, size) in enumerate(parts):
            own = weights[at + part][...].astype(LOW)
            outs[at + part][index_ref[0]] = own.reshape(pieces, size, width)
        for number, source in enumerate(sources):
            to_piece = index_ref[4 + number]
            for hop in range(3):
                to_block = index_ref[1 + hop]

                def lay(target, to_row, size):
                    for slab in range(width // BLOCK):
                        start = row + slab * rows
                        target[to_block, to_row, :, slab * BLOCK : (slab + 1) * BLOCK] = source[
                            hop, start : start + size
                        ]

                if split == 8:
                    lay(outs[at], to_piece, rows)
                else:
                    pl.when(to_piece < split)(lambda: lay(outs[at], to_piece, rows))
                    pl.when(to_piece >= split)(
                        lambda: lay(outs[at + 1], to_piece - split, rest)
                    )
        at += len(parts)
        row += rows * width // BLOCK


class Bundle:
    def __init__(self, place, piece, bundle):
        self.place, self.bundle, self.piece = place, bundle, piece

    def hops_direct(self):
        place = self.place
        self.hops = [place.ring(self.piece, steps) for steps in (1, 2, 3)]

    def hops_ring(self):
        place = self.place
        self.hops = [place.ring(self.piece)]
        self.hops.append(place.ring(self.hops[0]))
        self.hops.append(place.ring(self.hops[1]))

    def first_links(self, *waits):
        place = self.place
        held = after(jnp.stack(self.hops), *waits)
        self.own = [held, place.swap_one(held), place.swap_two(held)]

    def second_link(self, *waits):
        place = self.place
        if waits:
            gated = lax.optimization_barrier(tuple(self.own) + waits)
            self.own = list(gated[:3])
        self.own.append(place.swap_two(self.own[1]))

    def cores(self):
        self.far = [self.place.swap_core(item) for item in self.own]

    def lay(self):
        place, bundle = self.place, self.bundle
        sizes = [unit_sizes(unit) for unit in bundle]
        weights = [item for unit in bundle for item in unit]
        index = jnp.stack(
            [place.ns]
            + [(place.ns + place.n_ns - hop) % place.n_ns for hop in (1, 2, 3)]
            + place.spread_pieces()
        ).astype(jnp.int32)
        out_shape = []
        for rows, width, split, rest in sizes:
            out_shape.append(shaped((place.n_ns, split, rows, width), LOW))
            if split < 8:
                out_shape.append(shaped((place.n_ns, 8 - split, rest, width), LOW))
        whole = call(
            lambda *refs: lay_kernel(sizes, *refs),
            out_shape,
            [IN_SMEM] + [IN_VMEM] * (len(weights) + 8),
            5,
            60,
            name="lay_weights",
        )(index, *weights, *self.own, *self.far)
        return [item.reshape(-1, item.shape[-1]) for item in whole]


class RowSum:
    def __init__(self, place, near, far):
        for mask in place.extra:
            near = near + place.swap_mask(near, mask)
            far = far + place.swap_mask(far, mask)
        self.place, self.near = place, near
        self.got = place.swap_core(far)

    def halve(self, left, right, bit):
        count, rows, width = left.shape
        shape = (count, 2, rows // 2, width)
        left, right = left.reshape(shape), right.reshape(shape)
        self.kept = pick(left, bit, 1) + pick(right, bit, 1)
        self.sent = pick(left, 1 - bit, 1) + pick(right, 1 - bit, 1)

    def step_one(self, send=True):
        self.halve(self.near, self.got, self.place.bit_one)
        if send:
            self.got = self.place.swap_one(self.sent)

    def step_two(self, send=True):
        self.halve(self.kept, self.got, self.place.bit_two)
        if send:
            self.got = self.place.swap_two(self.sent)

    def step_three(self, send=True):
        place = self.place
        odd = place.ns & 1
        pairs = (2, 2) + self.kept.shape[1:]
        kept, got = self.kept.reshape(pairs), self.got.reshape(pairs)
        self.sent = pick(kept, 1 - odd, 1) + pick(got, 1 - odd, 1)
        self.kept = pick(kept, odd, 1) + pick(got, odd, 1)
        if send:
            self.got = place.swap_ns(self.sent, 1)

    def step_four(self):
        high = (self.place.ns >> 1) & 1
        self.sent = pick(self.kept, 1 - high, 0) + pick(self.got, 1 - high, 0)
        self.kept = pick(self.kept, high, 0) + pick(self.got, high, 0)


def in_step(swap, sums):
    got = swap(jnp.stack([item.sent for item in sums]))
    for at, item in enumerate(sums):
        item.got = got[at]
    return got


def last_step(place, sums):
    kept = jnp.stack([item.kept for item in sums])
    return kept, place.swap_ns(jnp.stack([item.sent for item in sums]), 2)


def over_ns(place, parts):
    return [parts[0]] + [place.swap_ns(part, mask) for mask, part in enumerate(parts) if mask]


def total_of(place, parts):
    total = parts[0].astype(WIDE)
    for part in parts[1:]:
        total = total + part.astype(WIDE)
    return [total.astype(LOW)] * place.n_ns


def place_kernel(index_ref, *refs):
    out_ref = refs[8]
    for at, source in enumerate(refs[:8]):
        out_ref[index_ref[at], index_ref[8 + at]] = source[...]


def lay_spread(place, sources, name):
    core = place.core
    index = jnp.stack(place.spread_owners() + [core] * 4 + [1 - core] * 4).astype(jnp.int32)
    return call(
        place_kernel,
        shaped((4, 2) + sources[0].shape, sources[0].dtype),
        [IN_SMEM] + [IN_VMEM] * 8,
        1,
        32,
        name=name,
    )(index, *sources)


def spread_numbers(place):
    core = place.core
    chips = place.chip ^ jnp.array([0, 1, 2, 3] * 2, jnp.int32)
    cores = jnp.stack([core] * 4 + [1 - core] * 4)
    base = place.dp - (place.dp & 7)
    over_dp = base + chips * 2 + cores
    numbers = (over_dp[:, None] * place.n_ns + place.blocks_at[None, :]).reshape(-1)
    for mask in place.extra:
        numbers = jnp.concatenate([numbers, numbers ^ (mask * place.n_ns)])
    return numbers


def gather_units(place, units):
    parts = [units] + [place.swap_ns(units, mask) for mask in range(1, place.n_ns)]
    held = jnp.stack(parts)
    sources = [held] + [place.swap_mask(held, mask) for mask in (2, 4, 6)]
    sources = sources + [place.swap_core(item) for item in sources]
    for mask in place.extra:
        sources = sources + [place.swap_mask(item, mask) for item in sources]
    return sources


def pack_small(loss_part, image_gain, text_gain):
    width = image_gain.shape[1]
    pad = width - text_gain.shape[1]
    return jnp.concatenate(
        [
            image_gain,
            jnp.pad(text_gain, ((0, 0), (0, pad))),
            jnp.broadcast_to(loss_part, (2, width)),
        ],
        0,
    )


def rows_by(left, right):
    return lax.dot_general(left, right, (((1,), (1,)), ((), ())), preferred_element_type=WIDE)


def product(left, right):
    return jnp.dot(left, right, preferred_element_type=WIDE)


def outer(left, right):
    return lax.dot_general(left, right, (((0,), (0,)), ((), ())), preferred_element_type=WIDE)


def normalize(values):
    shifted = values - jnp.mean(values, -1, keepdims=True)
    inverse = lax.rsqrt(jnp.mean(shifted * shifted, -1, keepdims=True) + NORM_EPS)
    return shifted * inverse, inverse


def norm_back(upstream, gain, unit_rows, inverse):
    scaled = upstream * gain
    inner = (
        scaled
        - jnp.mean(scaled, -1, keepdims=True)
        - unit_rows * jnp.mean(scaled * unit_rows, -1, keepdims=True)
    )
    return inner * inverse, jnp.sum(upstream * unit_rows, 0, keepdims=True)


def gate_of(hidden):
    return 0.5 * jnp.tanh(0.851 * hidden) + 0.5


class Tower:
    def __init__(self, count, span, width, hidden, heads, joint, causal):
        self.joint = joint
        self.count, self.span, self.width, self.hidden = count, span, width, hidden
        self.heads, self.causal = heads, causal
        self.padded = -(-span // 16) * 16
        self.rows = count * self.padded

    def valid(self, length_ref):
        at = lax.broadcasted_iota(jnp.int32, (self.padded, 1), 0)
        return jnp.concatenate(
            [(at < length_ref[number]).astype(WIDE) for number in range(self.count)], 0
        )

    def quarters(self):
        lane = lax.broadcasted_iota(jnp.int32, (1, BLOCK), 1)
        return [
            ((lane >= HEAD * at) & (lane < HEAD * (at + 1))).astype(WIDE).astype(LOW)
            for at in range(BLOCK // HEAD)
        ]

    def stacked(self, value, masks):
        return jnp.concatenate([value * mask for mask in masks], 0)

    def unstacked(self, value, masks):
        total = None
        for at, mask in enumerate(masks):
            part = value[at * self.padded : (at + 1) * self.padded] * mask.astype(WIDE)
            total = part if total is None else total + part
        return total

    def probabilities(self, left, right, over):
        scores = rows_by(left, right) * HEAD ** (-0.5)
        shape = scores.shape
        key = lax.broadcasted_iota(jnp.int32, shape, over)
        if self.causal:
            query = lax.broadcasted_iota(jnp.int32, shape, 1 - over)
            within = query - (query // self.padded) * self.padded
            scores = jnp.where(key <= within, scores, MASKED)
        elif self.padded != self.span:
            scores = jnp.where(key < self.span, scores, MASKED)
        raised = jnp.exp(scores - jnp.max(scores, over, keepdims=True))
        return raised * (1.0 / jnp.sum(raised, over, keepdims=True))

    def attend_kernel(
        self, x_ref, gains_ref, wa_ref, wo_ref, normed_ref, packed_ref, attended_ref, first_ref
    ):
        width = self.width
        unit_rows, _ = normalize(x_ref[...].astype(WIDE))
        normed_ref[...] = (unit_rows * gains_ref[0:1, :]).astype(LOW)
        for at in range(0, 3 * width, width):
            packed_ref[:, at : at + width] = rows_by(
                normed_ref[...], wa_ref[at : at + width, :]
            ).astype(LOW)
        masks = self.quarters()

        def one(number, carry):
            rows = pl.ds(pl.multiple_of(number * self.padded, 16), self.padded)
            for at in range(0, width, BLOCK):
                columns = slice(at, at + BLOCK)
                queries = self.stacked(packed_ref[rows, columns], masks)
                keys = packed_ref[rows, width + at : width + at + BLOCK]
                values = packed_ref[rows, 2 * width + at : 2 * width + at + BLOCK]
                probs = self.probabilities(queries, keys, 1).astype(LOW)
                attended_ref[rows, columns] = self.unstacked(product(probs, values), masks).astype(
                    LOW
                )
            return carry

        lax.fori_loop(0, self.count, one, 0, unroll=True)
        first_ref[...] = x_ref[...].astype(WIDE) + rows_by(attended_ref[...], wo_ref[...])

    def attend(self, x, gains, wa, wo):
        rows, width = self.rows, self.width
        return call(
            self.attend_kernel,
            [
                shaped((rows, width), LOW),
                shaped((rows, 3 * width), LOW),
                shaped((rows, width), LOW),
                shaped((rows, width)),
            ],
            [IN_VMEM] * 4,
            10,
            48,
            name="attend",
        )(x, gains, wa, wo)

    def feed_kernel(self, length_ref, first_ref, gains_ref, we_ref, sums_ref, pool_ref):
        valid = self.valid(length_ref)
        first = first_ref[...]
        unit_rows, _ = normalize(first)
        second = (unit_rows * gains_ref[1:2, :]).astype(LOW)

        def pooled(value):
            shape = (self.count, self.padded, value.shape[-1])
            return jnp.sum((value * valid).reshape(shape), 1)

        pool_ref[...] = pooled(first)
        step = self.hidden // 4
        for at in range(0, self.hidden, step):
            hidden = rows_by(second, we_ref[at : at + step, :])
            activated = (hidden * gate_of(hidden)).astype(LOW)
            sums_ref[:, at : at + step] = pooled(activated.astype(WIDE))

    def feed(self, lengths, first, gains, we):
        return call(
            self.feed_kernel,
            [shaped((self.count, self.hidden)), shaped((self.count, self.width))],
            [IN_SMEM] + [IN_VMEM] * 3,
            3,
            48,
            name="feed",
        )(lengths, first, gains, we)

    def head_kernel(
        self,
        sums_ref,
        pool_ref,
        counts_ref,
        ws_ref,
        gains_ref,
        wm_ref,
        pooled_ref,
        embedded_ref,
        unit_ref,
    ):
        sums = sums_ref[...]
        high = sums.astype(LOW)
        rest = (sums - high.astype(WIDE)).astype(LOW)
        total = pool_ref[...] + product(high, ws_ref[...]) + product(rest, ws_ref[...])
        pooled = total / counts_ref[...]
        unit_rows, _ = normalize(pooled)
        embedded = product((unit_rows * gains_ref[2:3, :]).astype(LOW), wm_ref[...])
        pooled_ref[...] = pooled
        embedded_ref[...] = embedded
        unit_ref[...] = embedded * lax.rsqrt(
            jnp.sum(embedded * embedded, -1, keepdims=True) + UNIT_EPS
        )

    def head(self, sums, pool, counts, ws, gains, wm):
        joint = wm.shape[1]
        return call(
            self.head_kernel,
            [
                shaped((self.count, self.width)),
                shaped((self.count, joint)),
                shaped((self.count, joint)),
            ],
            [IN_VMEM] * 6,
            1.5,
            32,
            name="head",
        )(sums, pool, counts, ws, gains, wm)

    def head_back_kernel(
        self,
        grad,
        pooled_ref,
        embedded_ref,
        counts_ref,
        ws_ref,
        gains_ref,
        wm_ref,
        embed_grad_ref,
        final_ref,
        branch_ref,
        pushed_ref,
        gain_ref,
    ):
        embedded = embedded_ref[...]
        inverse_norm = lax.rsqrt(jnp.sum(embedded * embedded, -1, keepdims=True) + UNIT_EPS)
        unit = embedded * inverse_norm
        along = jnp.sum(grad * unit, -1, keepdims=True)
        embed_grad = (inverse_norm * (grad - unit * along)).astype(LOW)
        embed_grad_ref[...] = embed_grad
        unit_rows, inverse = normalize(pooled_ref[...])
        gain = gains_ref[2:3, :]
        final_ref[...] = (unit_rows * gain).astype(LOW)
        pooled_grad, gain_grad = norm_back(
            rows_by(embed_grad, wm_ref[...]), gain, unit_rows, inverse
        )
        gain_ref[...] = gain_grad
        branch = pooled_grad / counts_ref[...]
        branch_ref[...] = branch
        pushed_ref[...] = rows_by(branch.astype(LOW), ws_ref[...])

    def head_back_shapes(self):
        count = self.count
        return [
            shaped((count, self.joint), LOW),
            shaped((count, self.width), LOW),
            shaped((count, self.width)),
            shaped((count, self.hidden)),
            shaped((1, self.width)),
        ]

    def head_back(self, grad, pooled, embedded, counts, ws, gains, wm):
        return call(
            lambda grad_ref, *refs: self.head_back_kernel(grad_ref[...], *refs),
            self.head_back_shapes(),
            [IN_VMEM] * 7,
            1.5,
            32,
            name="head_back",
        )(grad, pooled, embedded, counts, ws, gains, wm)

    def factor_cuts(self, blocks):
        cuts = [0]
        for size in (self.hidden // blocks, self.width, self.width // blocks, self.joint):
            cuts.append(cuts[-1] + size)
        return cuts

    def factor_rows(self, block, blocks, sums, branch, final, embed_grad):
        hidden, width = self.hidden // blocks, self.width // blocks
        return jnp.concatenate(
            [
                sums[:, block * hidden : (block + 1) * hidden],
                branch,
                final[:, block * width : (block + 1) * width].astype(WIDE),
                embed_grad.astype(WIDE),
            ],
            1,
        )

    def over_tokens(self, value):
        shape = (self.count, self.padded, value.shape[-1])
        return jnp.broadcast_to(value[:, None, :], shape).reshape(self.rows, shape[-1])

    def feed_back_kernel(self, length_ref, core_ref, *refs):
        for core in range(2):
            pl.when(core_ref[0] == core)(lambda: self.feed_back_body(core, length_ref, *refs))

    def feed_back_body(
        self,
        core,
        length_ref,
        first_ref,
        gains_ref,
        we_ref,
        pushed_ref,
        branch_ref,
        first_grad_ref,
        near_ref,
        far_ref,
        gain_ref,
    ):
        valid = self.valid(length_ref)
        gain = gains_ref[1:2, :]
        unit_rows, inverse = normalize(first_ref[...])
        second = (unit_rows * gain).astype(LOW)
        blocks, step, _ = near_ref.shape
        total = None
        for block in range(blocks):
            rows = slice(2 * block * step, 2 * (block + 1) * step)
            expand = we_ref[rows, :]
            hidden = rows_by(second, expand)
            gate = gate_of(hidden)
            slope = gate + (1.702 * hidden) * (gate * (1.0 - gate))
            pushed = self.over_tokens(pushed_ref[:, rows]) * valid
            hidden_grad = (pushed * slope).astype(LOW)
            grads = outer(hidden_grad, second).astype(LOW)
            term = product(hidden_grad, expand)
            total = term if total is None else total + term
            halves = (grads[:step], grads[step:])
            near_ref[block] = halves[core]
            far_ref[block] = halves[1 - core]

        second_grad, gain_grad = norm_back(total, gain, unit_rows, inverse)
        gain_ref[...] = gain_grad
        first_grad_ref[...] = self.over_tokens(branch_ref[...]) * valid + second_grad

    def feed_back(self, blocks, lengths, core, first, gains, we, pushed, branch):
        part = (blocks, self.hidden // (2 * blocks), self.width)
        return call(
            self.feed_back_kernel,
            [
                shaped((self.rows, self.width)),
                shaped(part, LOW),
                shaped(part, LOW),
                shaped((1, self.width)),
            ],
            [IN_SMEM] * 2 + [IN_VMEM] * 5,
            13,
            56,
            name="feed_back",
        )(lengths, core, first, gains, we, pushed, branch)

    def attend_back_kernel(
        self,
        core_ref,
        first_grad_ref,
        x_ref,
        normed_ref,
        packed_ref,
        attended_ref,
        gains_ref,
        wa_ref,
        wo_ref,
        token_ref,
        near_ref,
        far_ref,
        gain_ref,
        packed_grad_ref,
        attended_grad_ref,
    ):
        width = self.width
        first_low = first_grad_ref[...].astype(LOW)
        attended_grad_ref[...] = product(first_low, wo_ref[...]).astype(LOW)
        masks = self.quarters()

        def one(number, carry):
            rows = pl.ds(pl.multiple_of(number * self.padded, 16), self.padded)
            for at in range(0, width, BLOCK):
                spots = [slice(at + part * width, at + part * width + BLOCK) for part in range(3)]
                queries = self.stacked(packed_ref[rows, spots[0]], masks)
                keys, values = packed_ref[rows, spots[1]], packed_ref[rows, spots[2]]
                upstream = self.stacked(attended_grad_ref[rows, spots[0]], masks)
                probs = self.probabilities(keys, queries, 0)
                prob_grad = rows_by(values, upstream)
                score_grad = (
                    probs * (prob_grad - jnp.sum(prob_grad * probs, 0, keepdims=True))
                ).astype(LOW)
                scale = HEAD ** (-0.5)
                query_grad = self.unstacked(outer(score_grad, keys), masks) * scale
                packed_grad_ref[rows, spots[0]] = query_grad.astype(LOW)
                packed_grad_ref[rows, spots[1]] = (product(score_grad, queries) * scale).astype(
                    LOW
                )
                packed_grad_ref[rows, spots[2]] = product(probs.astype(LOW), upstream).astype(LOW)
            return carry

        lax.fori_loop(0, self.count, one, 0, unroll=True)
        blocks, half_rows, _ = near_ref.shape
        main_rows = 3 * width // blocks
        rest_rows = width // blocks

        def weights(core):
            def put(block, half, at, value):
                (near_ref if half == core else far_ref)[block, at : at + value.shape[0]] = value

            for block in range(blocks):
                start = block * main_rows
                grads = outer(packed_grad_ref[:, start : start + main_rows], normed_ref[...])
                grads = grads.astype(LOW)
                put(block, 0, 0, grads[:half_rows])
                put(block, 1, 0, grads[half_rows:])
                start = block * rest_rows
                grads = outer(first_low[:, start : start + rest_rows], attended_ref[...])
                put(block, 1, half_rows - rest_rows, grads.astype(LOW))

        pl.when(core_ref[0] == 0)(lambda: weights(0))
        pl.when(core_ref[0] == 1)(lambda: weights(1))
        unit_rows, inverse = normalize(x_ref[...].astype(WIDE))
        input_grad, gain_grad = norm_back(
            product(packed_grad_ref[...], wa_ref[...]), gains_ref[0:1, :], unit_rows, inverse
        )
        gain_ref[...] = gain_grad
        token_ref[...] = (first_grad_ref[...] + input_grad).astype(LOW)

    def attend_back(
        self, blocks, core, first_grad, x, normed, packed, attended, gains, wa, wo
    ):
        rows, width = self.rows, self.width
        part = (blocks, 2 * width // blocks, width)
        return call(
            self.attend_back_kernel,
            [
                shaped((rows, width), LOW),
                shaped(part, LOW),
                shaped(part, LOW),
                shaped((1, width)),
            ],
            [IN_SMEM] + [IN_VMEM] * 8,
            18,
            56,
            [pltpu.VMEM((rows, 3 * width), LOW), pltpu.VMEM((rows, width), LOW)],
            "attend_back",
        )(core, first_grad, x, normed, packed, attended, gains, wa, wo)

    def pad(self, tokens):
        extra = self.padded - self.span
        return jnp.pad(tokens, ((0, 0), (0, extra), (0, 0))).reshape(self.rows, self.width)

    def unpad(self, rows):
        return rows.reshape(self.count, self.padded, self.width)[:, : self.span]


SLOTS = 16


def contrast_kernel(
    images, captions, side, image, row_ref, column_ref, *refs
):
    sources, refs = refs[:8], refs[8:]
    head_refs, outs, (ws_ref, wm_ref, sems) = refs[:6], refs[6:-3], refs[-3:]
    copies = [
        pltpu.make_async_copy(source, target, sems.at[at])
        for at, (source, target) in enumerate(((head_refs[3], ws_ref), (head_refs[5], wm_ref)))
    ]
    for copy in copies:
        copy.start()
    every = jnp.concatenate(
        [ref[...].reshape(-1, ref.shape[-1]) for ref in sources], 0
    )
    sims = rows_by(every, every) * SIM_SCALE
    row_label, column_label = row_ref[...], column_ref[...]
    valid = (row_label >= 0) & (column_label >= 0)
    match = jnp.where(valid & (row_label == column_label), 1.0, 0.0)
    counts = jnp.maximum(jnp.sum(match, 1, keepdims=True), 1.0)
    masked = jnp.where(valid, sims, -1e30)
    row_top = jnp.max(masked, 1, keepdims=True)
    row_raised = jnp.where(valid, jnp.exp(masked - row_top), 0.0)
    row_total = jnp.maximum(jnp.sum(row_raised, 1, keepdims=True), 1e-30)
    column_top = jnp.max(masked, 0, keepdims=True)
    column_raised = jnp.where(valid, jnp.exp(masked - column_top), 0.0)
    column_total = jnp.maximum(jnp.sum(column_raised, 0, keepdims=True), 1e-30)
    picked = sims * match
    image_terms = row_top + jnp.log(row_total) - jnp.sum(picked, 1, keepdims=True) / counts
    caption_terms = column_top + jnp.log(column_total) - jnp.sum(picked, 0, keepdims=True)
    row_at = lax.broadcasted_iota(jnp.int32, image_terms.shape, 0)
    column_at = lax.broadcasted_iota(jnp.int32, caption_terms.shape, 1)
    own_caption = (column_at >= images) & (column_at < images + captions)
    loss = 0.5 * jnp.sum(
        jnp.where(row_at < images, image_terms, 0.0), keepdims=True
    ) + side * jnp.sum(jnp.where(own_caption, caption_terms, 0.0), keepdims=True)
    outs[1][...] = jnp.broadcast_to(loss, outs[1].shape)
    grad = 0.5 * (row_raised / row_total - match / counts) + side * (
        column_raised / column_total - match
    )
    wide = every.astype(WIDE)
    image_grad = jnp.dot(
        grad[:SLOTS], wide, precision=HIGH, preferred_element_type=WIDE
    )
    text_grad = lax.dot_general(
        grad[:, :128],
        wide,
        (((0,), (0,)), ((), ())),
        precision=HIGH,
        preferred_element_type=WIDE,
    )
    outs[0][...] = SIM_SCALE * text_grad[images : images + captions]
    for copy in copies:
        copy.wait()
    pooled_ref, embedded_ref, counts_ref, _, gains_ref, _ = head_refs
    image.head_back_kernel(
        SIM_SCALE * image_grad[:images],
        pooled_ref,
        embedded_ref,
        counts_ref,
        ws_ref,
        gains_ref,
        wm_ref,
        *outs[2:],
    )


def contrast_whole(images, captions, side, row_label, column_label, sources):
    every = jnp.concatenate([item.reshape(-1, item.shape[-1]) for item in sources], 0)
    joint = every.shape[-1]
    slots = every.reshape(-1, SLOTS, joint)
    every_image = slots[:, :images].reshape(-1, joint)
    every_text = slots[:, images : images + captions].reshape(-1, joint)
    image_ids = row_label.reshape(-1, SLOTS)[:, :images].reshape(-1)
    named = column_label.reshape(-1, SLOTS)[:, images : images + captions].reshape(-1)
    match = (named[None, :] == image_ids[:, None]).astype(WIDE)
    counts = jnp.sum(match, 1, keepdims=True)
    sims = rows_by(every_image, every_text) * SIM_SCALE
    row_log = jax.scipy.special.logsumexp(sims, axis=1, keepdims=True)
    col_log = jax.scipy.special.logsumexp(sims, axis=0, keepdims=True)
    image_terms = row_log - jnp.sum(sims * match, 1, keepdims=True) / counts
    caption_terms = col_log - jnp.sum(sims * match, 0, keepdims=True)
    loss_part = 0.5 * jnp.sum(image_terms[:images]) + side * jnp.sum(caption_terms[:, :captions])
    grad = 0.5 * (jnp.exp(sims - row_log) - match / counts) + side * (
        jnp.exp(sims - col_log) - match
    )
    image_unit_grad = SIM_SCALE * jnp.dot(
        grad[:images], every_text.astype(WIDE), precision=HIGH
    )
    text_unit_grad = SIM_SCALE * lax.dot_general(
        grad[:, :captions],
        every_image.astype(WIDE),
        (((0,), (0,)), ((), ())),
        precision=HIGH,
        preferred_element_type=WIDE,
    )
    return image_unit_grad, text_unit_grad, jnp.broadcast_to(loss_part, (1, 128))


def contrast_labels(place, images, captions, caption_image):
    numbers = spread_numbers(place)
    at = jnp.arange(SLOTS, dtype=jnp.int32)[None, :]
    image_ids = jnp.where(at < images, numbers[:, None] * images + at, -1)
    named = jnp.take(caption_image.reshape(-1, captions), numbers, axis=0)
    named = jnp.pad(
        named, ((0, 0), (images, SLOTS - images - captions)), constant_values=-1
    )
    return image_ids.reshape(-1, 1), named.reshape(1, -1)


def contrast(place, image, head, image_unit, text_unit, row_label, column_label):
    images, captions, joint = image_unit.shape[0], text_unit.shape[0], text_unit.shape[1]
    blank = jnp.zeros((SLOTS - images - captions, joint), LOW)
    units = jnp.concatenate([image_unit.astype(LOW), text_unit.astype(LOW), blank], 0)
    sources = gather_units(place, units)
    side = 0.5 * images / captions
    if len(sources) > 8:
        image_grad, text_grad, loss_part = contrast_whole(
            images, captions, side, row_label, column_label, sources
        )
        return [text_grad, loss_part] + list(image.head_back(image_grad, *head))
    return call(
        lambda *refs: contrast_kernel(images, captions, side, image, *refs),
        [shaped((captions, joint)), shaped((1, 128))] + image.head_back_shapes(),
        [IN_VMEM] * 13 + [IN_PLACE, IN_VMEM, IN_PLACE],
        5,
        56,
        [
            pltpu.VMEM(head[3].shape, LOW),
            pltpu.VMEM(head[5].shape, LOW),
            pltpu.SemaphoreType.DMA((2,)),
        ],
        name="contrast",
    )(row_label, column_label, *sources, *head)


def together(*values):
    return lax.optimization_barrier(values)


class Factors:
    def __init__(self, place, packed, image, text):
        self.place, self.towers = place, (image, text)
        self.messages = [pick(packed, place.ns ^ mask, 0) for mask in range(place.n_ns)]

    def over_ns(self):
        place = self.place
        self.messages = [
            place.swap_ns(item, mask) if mask else item for mask, item in enumerate(self.messages)
        ]

    def stack(self):
        self.blocks = jnp.stack(self.messages)

    def every(self):
        place = self.place
        sources = self.own + [self.far[at] for at in range(4)]
        every = lay_spread(place, sources, "place_factors")
        every = every.reshape((-1,) + every.shape[3:])
        for mask in place.extra:
            other = place.swap_mask(every, mask)
            every = jnp.where(
                (place.dp & mask) == 0,
                jnp.concatenate([every, other], 0),
                jnp.concatenate([other, every], 0),
            )
        return every.reshape(-1, every.shape[-1])

    def products(self, every, dot):
        image, text = self.towers
        blocks = self.place.n_ns
        slot = lax.broadcasted_iota(jnp.int32, (every.shape[0], 1), 0) % SLOTS
        outs = []
        for tower, own in ((image, slot < image.count), (text, slot >= SLOTS - text.count)):
            cuts = tower.factor_cuts(blocks)
            held = every * jnp.where(own, 1.0, 0.0).astype(LOW)
            pieces = [held[:, low:high] for low, high in zip(cuts, cuts[1:])]
            outs += [dot(pieces[0], pieces[1]), dot(pieces[2], pieces[3])]
        return outs

    def kernel(self, index_ref, *refs):
        own_refs, far_ref, outs, every_ref = refs[:4], refs[4], refs[5:9], refs[9]
        rows = every_ref.shape[0] // 8
        for at in range(8):
            to = pl.ds(pl.multiple_of(index_ref[at] * rows, rows), rows)
            source = own_refs[at][...] if at < 4 else far_ref[at - 4]
            every_ref[to] = source.reshape(rows, source.shape[-1])
        for out_ref, value in zip(outs, self.products(every_ref[...], outer)):
            out_ref[...] = value

    def gradients(self):
        place = self.place
        if place.extra:
            return self.products(self.every(), outer)
        image, text = self.towers
        blocks, core = place.n_ns, place.core
        index = jnp.stack(
            [
                chip * 2 + (core if at < 4 else 1 - core)
                for at, chip in enumerate(place.spread_owners())
            ]
        ).astype(jnp.int32)
        columns = self.own[0].shape[-1]
        out_shape = []
        for tower in (image, text):
            out_shape.append(shaped((tower.hidden // blocks, tower.width)))
            out_shape.append(shaped((tower.width // blocks, tower.joint)))
        return call(
            self.kernel,
            out_shape,
            [IN_SMEM] + [IN_VMEM] * 5,
            4,
            48,
            [pltpu.VMEM((8 * blocks * SLOTS, columns), LOW)],
            name="factor_grads",
        )(index, *self.own, self.far)


def pack_factors(blocks, image, text, image_parts, text_parts):
    columns = max(image.factor_cuts(blocks)[-1], text.factor_cuts(blocks)[-1])

    def body(*refs):
        out_ref = refs[8]
        first, second = [ref[...] for ref in refs[:4]], [ref[...] for ref in refs[4:8]]
        out_ref[...] = jnp.zeros(out_ref.shape, LOW)
        for block in range(blocks):
            rows = image.factor_rows(block, blocks, *first)
            lower = jnp.zeros((SLOTS - text.count - image.count, rows.shape[1]), WIDE)
            rows = jnp.concatenate([rows, lower], 0)
            more = text.factor_rows(block, blocks, *second)
            blank = jnp.zeros((text.count, columns - more.shape[1]), WIDE)
            more = jnp.concatenate([more, blank], 1)
            out_ref[block] = jnp.concatenate([rows, more], 0).astype(LOW)

    return call(
        body,
        shaped((blocks, SLOTS, columns), LOW),
        [IN_VMEM] * 8,
        1,
        32,
        name="pack_factors",
    )(*image_parts, *text_parts)


class Fresh:
    def __init__(self, place, units, others, owners, per_chip):
        self.place, self.units, self.others = place, units, others
        self.owners, self.per_chip = owners, per_chip
        self.width = units[0][0].shape[1]
        self.rows = sum(item.shape[0] for item in units[0])
        self.pairs = TRI3 if per_chip else TRI2

        self.moments = [item for unit in units for item in unit] + list(others)
        owner = place.chip if per_chip else place.chip * 2 + place.core
        self.info = jnp.concatenate(
            [
                jnp.stack([owner, place.core]).astype(jnp.int32),
                place.blocks_at,
                jnp.stack(place.spread_pieces()).astype(jnp.int32),
            ]
        )

    def spots(self):
        out = []
        for unit_at, unit in enumerate(self.units):
            split = unit[0].shape[0] * 8 // self.rows
            out.append((unit_at, 0, split))
            if len(unit) > 1:
                out.append((unit_at, split, 8))
        return out

    def lay(self, info_ref, sources, at, put):
        unit_at, low, high = self.spots()[at]
        size = self.rows // 8
        for number, source in enumerate(sources):
            piece = info_ref[6 + number]

            def one():
                put(pl.ds(pl.multiple_of((piece - low) * size, size), size), source[unit_at])

            if (low, high) == (0, 8):
                one()
            else:
                pl.when((piece >= low) & (piece < high))(one)

    def gram_kernel(self, info_ref, *refs):
        gathered = len(self.spots())
        sources, refs = refs[:8], refs[8:]
        grads, refs = refs[: len(self.others)], refs[len(self.others) :]
        moments, refs = refs[: len(self.moments)], refs[len(self.moments) :]
        part_refs, (moment_ref, grad_ref, chosen_ref, gram_ref, sems) = refs[:-5], refs[-5:]
        for owner, at in enumerate(self.owners):

            @pl.when(info_ref[0] == owner)
            def _():
                rows = self.moments[at].shape[0]
                copies = [
                    pltpu.make_async_copy(moments[at], moment_ref.at[:rows], sems.at[0])
                ]
                if at >= gathered:
                    copies.append(
                        pltpu.make_async_copy(
                            grads[at - gathered], grad_ref.at[:rows], sems.at[1]
                        )
                    )
                for copy in copies:
                    copy.start()
                if rows < self.rows:
                    chosen_ref[rows:] = jnp.zeros((self.rows - rows, self.width), LOW)
                for copy in copies:
                    copy.wait()

                def put(where, gradient):
                    chosen_ref[where] = (
                        MOMENTUM * moment_ref[where] + gradient.astype(WIDE)
                    ).astype(LOW)

                if at < gathered:
                    self.lay(info_ref, sources, at, put)
                else:
                    put(slice(0, rows), grad_ref[:rows])

        @pl.when(info_ref[0] >= len(self.owners))
        def _():
            chosen_ref[...] = jnp.zeros((self.rows, self.width), LOW)

        def blocks(pairs):
            for number, (i, j) in enumerate(pairs):
                left = chosen_ref[:, i * BLOCK : (i + 1) * BLOCK]
                right = chosen_ref[:, j * BLOCK : (j + 1) * BLOCK]
                gram_ref[number * BLOCK : (number + 1) * BLOCK] = outer(left, right).astype(LOW)

        if self.per_chip:
            pl.when(info_ref[1] == 0)(lambda: blocks(self.pairs[:3]))
            pl.when(info_ref[1] == 1)(lambda: blocks(self.pairs[3:]))
        else:
            blocks(self.pairs)
        size = gram_ref.shape[0] // len(part_refs)
        for number, part_ref in enumerate(part_refs):
            at = info_ref[2 + number]
            part_ref[...] = gram_ref[pl.ds(pl.multiple_of(at * size, size), size)]

    def gram(self, sources, grads):
        count = self.place.n_ns
        return call(
            self.gram_kernel,
            [shaped((3 * BLOCK // count, BLOCK), LOW)] * count,
            [IN_SMEM] + [IN_VMEM] * 8 + [IN_PLACE] * (len(grads) + len(self.moments)),
            3,
            56,
            [
                pltpu.VMEM((self.rows, self.width), WIDE),
                pltpu.VMEM((self.rows, self.width), WIDE),
                pltpu.VMEM((self.rows, self.width), LOW),
                pltpu.VMEM((3 * BLOCK, BLOCK), LOW),
                pltpu.SemaphoreType.DMA((2,)),
            ],
            "gram",
        )(self.info, *sources, *grads, *self.moments)

    def fresh_kernel(self, info_ref, *refs):
        gathered, total = len(self.spots()), len(self.moments)
        sources, refs = refs[:8], refs[8:]
        grads, refs = refs[: len(self.others)], refs[len(self.others) :]
        moments, fresh = refs[:total], refs[total:]
        for at in range(total):

            def put(where, gradient):
                fresh[at][where] = MOMENTUM * moments[at][where] + gradient.astype(WIDE)

            if at < gathered:
                self.lay(info_ref, sources, at, put)
            else:
                put(slice(None), grads[at - gathered][...])

    def make(self, sources, grads):
        return call(
            self.fresh_kernel,
            [shaped(item.shape) for item in self.moments],
            [IN_SMEM] + [IN_VMEM] * (8 + len(grads) + len(self.moments)),
            5,
            60,
            name="freshen",
        )(self.info, *sources, *grads, *self.moments)


def polynomial_kernel(side, pairs, info_ref, *refs):
    count = info_ref.shape[0] - 1
    parts, out_ref, gram_ref = refs[:-2], refs[-2], refs[-1]
    size = parts[0].shape[0]
    core = info_ref[count]
    for number, part in enumerate(parts):
        at = info_ref[number % count]
        half = 0 if side == 2 else (core if number < count else 1 - core)
        gram_ref[half, pl.ds(pl.multiple_of(at * size, size), size)] = part[...]
    blocks = {
        pair: gram_ref[at // 3, at % 3 * BLOCK : (at % 3 + 1) * BLOCK].astype(WIDE)
        for at, pair in enumerate(pairs)
    }
    rows = [
        jnp.concatenate(
            [blocks[(i, j)] if i <= j else blocks[(j, i)].T for j in range(side)], 1
        )
        for i in range(side)
    ]
    square = jnp.concatenate(rows, 0)
    span = side * BLOCK
    same = lax.broadcasted_iota(jnp.int32, (span, span), 0) == lax.broadcasted_iota(
        jnp.int32, (span, span), 1
    )
    factor = 1.0 / (jnp.sqrt(jnp.sum(jnp.where(same, square, 0.0))) + 1e-07)
    square = square * (factor * factor)

    def mm(left, right):
        return product(left.astype(LOW), right.astype(LOW))

    def terms(value):
        return COEF_B * value + COEF_C * mm(value, value)

    def following(value, term):
        half = COEF_A * value + mm(value, term)
        return COEF_A * half + mm(half, term)

    term_zero = terms(square)
    square = following(square, term_zero)
    term_one = terms(square)
    square = following(square, term_one)
    term_two = terms(square)
    both = COEF_A * (term_zero + term_one) + mm(term_zero, term_one)
    whole = COEF_A**2 * term_two + COEF_A * both + mm(both, term_two)
    whole = factor * (whole + jnp.where(same, COEF_A**3, 0.0))

    def give(chosen):
        for at, (i, j) in enumerate(chosen):
            out_ref[at] = whole[
                i * BLOCK : (i + 1) * BLOCK, j * BLOCK : (j + 1) * BLOCK
            ].astype(LOW)

    if side == 2:
        give(pairs)
    else:
        pl.when(core == 0)(lambda: give(pairs[:3]))
        pl.when(core == 1)(lambda: give(pairs[3:]))


def polynomial(place, parts, side, pairs):
    return call(
        lambda *refs: polynomial_kernel(side, pairs, *refs),
        shaped((3, BLOCK, BLOCK), LOW),
        [IN_SMEM] + [IN_VMEM] * len(parts),
        4 if side == 2 else 10,
        60,
        [pltpu.VMEM((len(pairs) // 3, 3 * BLOCK, BLOCK), LOW)],
        name="polynomial",
    )(jnp.concatenate([place.blocks_at, place.core_at]), *parts)


def apply_kernel(weights, per_chip, info_ref, *refs):
    count = len(weights)
    sources, refs, held_ref = refs[:8], refs[8:-1], refs[-1]
    masters, fresh, outs = refs[:count], refs[count : 2 * count], refs[2 * count :]
    for at, source in enumerate(sources):
        held_ref[info_ref[at]] = source[...]
    for at, (owner, scale) in enumerate(weights):
        rows, width = outs[at].shape
        side = width // BLOCK
        pairs = TRI3 if per_chip else TRI2

        def block(i, j):
            number = pairs.index((min(i, j), max(i, j)))
            if per_chip:
                return held_ref[2 * owner + number // 3, number % 3]
            return held_ref[owner, number]

        for start in range(0, rows, BLOCK):
            spot = slice(start, min(start + BLOCK, rows))
            left = fresh[at][spot].astype(LOW)
            for j in range(side):
                total = None
                for i in range(side):
                    part = left[:, i * BLOCK : (i + 1) * BLOCK]
                    term = product(part, block(i, j)) if i <= j else rows_by(part, block(i, j))
                    total = term if total is None else total + term
                columns = slice(j * BLOCK, (j + 1) * BLOCK)
                outs[at][spot, columns] = masters[at][spot, columns] - scale * total


def apply_polynomials(place, sources, masters, fresh, owners, per_chip):
    core = place.core
    info = jnp.stack(
        [
            chip * 2 + (core if at < 4 else 1 - core)
            for at, chip in enumerate(place.spread_owners())
        ]
    ).astype(jnp.int32)
    weights = [
        (owner, RATE * math.sqrt(item.shape[0] * place.n_ns / item.shape[1]))
        for owner, item in zip(owners, masters)
    ]
    return call(
        lambda *refs: apply_kernel(weights, per_chip, *refs),
        [shaped(item.shape) for item in masters],
        [IN_SMEM] + [IN_VMEM] * (8 + 2 * len(masters)),
        6,
        60 if per_chip else 40,
        [pltpu.VMEM((8,) + sources[0].shape, LOW)],
        "apply_polynomials",
    )(info, *sources, *masters, *fresh)


def per_device(
    image_tokens,
    text_tokens,
    caption_image,
    caption_length,
    image_attention,
    image_output,
    image_expand,
    image_shrink,
    image_embedding,
    text_attention,
    text_output,
    text_expand,
    text_shrink,
    text_embedding,
    image_gains,
    text_gains,
    image_attention_momentum,
    image_output_momentum,
    image_expand_momentum,
    image_shrink_momentum,
    image_embedding_momentum,
    text_attention_momentum,
    text_output_momentum,
    text_expand_momentum,
    text_shrink_momentum,
    text_embedding_momentum,
    image_gains_momentum,
    text_gains_momentum,
):
    place = Place()
    count = place.n_ns
    joint = text_embedding.shape[1]
    bundles = (
        ((text_attention, text_output),),
        ((text_expand,), (text_shrink,)),
        ((image_attention, image_output), (image_embedding, text_embedding)),
        ((image_expand,), (image_shrink,)),
    )
    pieces = cut_pieces(place, bundles)
    one = Bundle(place, pieces[0], bundles[0])
    one.hops_direct()
    two = Bundle(place, after(pieces[1], *one.hops), bundles[1])
    two.hops_direct()
    three = Bundle(place, after(pieces[2], *two.hops), bundles[2])
    three.hops_direct()
    one.first_links()
    one.second_link()
    one.cores()
    two.first_links()
    three.first_links(*two.own[1:])

    images, image_span, image_width = image_tokens.shape
    captions, text_span, text_width = text_tokens.shape
    image = Tower(images, image_span, image_width, image_expand.shape[0] * count, HI, joint, False)
    text = Tower(captions, text_span, text_width, text_expand.shape[0] * count, HT, joint, True)
    image_lengths = jnp.full((images,), image_span, jnp.int32)
    image_counts = jnp.full((images, 1), image_span, WIDE)
    text_counts = caption_length.astype(WIDE).reshape(captions, 1)
    core = place.core.astype(jnp.int32).reshape(1)

    ta_low, to_low = one.lay()
    row_label, column_label = contrast_labels(place, images, captions, caption_image)
    tx = text.pad(text_tokens)
    t_normed, t_packed, t_attended, t_first = text.attend(
        after(tx, row_label, column_label), text_gains, ta_low, to_low
    )
    four = Bundle(place, after(pieces[3], t_attended), bundles[3])
    four.hops_ring()
    four.first_links(*three.own[1:])
    two.second_link(t_attended)
    two.cores()
    te_low, ts_low = two.lay()
    t_sums, t_pool = text.feed(caption_length, t_first, text_gains, te_low)
    three.second_link(t_sums)
    three.cores()
    ia_low, io_low, im_low, tm_low = three.lay()
    t_pooled, t_embedded, t_unit = text.head(
        t_sums, t_pool, text_counts, ts_low, text_gains, tm_low
    )
    ix = image.pad(image_tokens)
    i_normed, i_packed, i_attended, i_first = image.attend(ix, image_gains, ia_low, io_low)
    four.second_link(i_attended)
    four.own[3], t_pooled, t_embedded, t_unit = together(
        four.own[3], t_pooled, t_embedded, t_unit
    )
    four.cores()
    ie_low, is_low = four.lay()
    i_sums, i_pool = image.feed(image_lengths, i_first, image_gains, ie_low)
    i_pooled, i_embedded, i_unit = image.head(
        i_sums, i_pool, image_counts, is_low, image_gains, im_low
    )

    (
        text_unit_grad,
        loss_part,
        i_embed_grad,
        i_final,
        i_branch,
        i_pushed,
        i_gain_final,
    ) = contrast(
        place,
        image,
        (i_pooled, i_embedded, image_counts, is_low, image_gains, im_low),
        i_unit,
        t_unit,
        row_label,
        column_label,
    )
    i_first_grad, i_near, i_far, i_gain_second = image.feed_back(
        count, image_lengths, core, i_first, image_gains, ie_low, i_pushed, i_branch
    )
    sum_ie = RowSum(place, i_near, i_far)
    t_embed_grad, t_final, t_branch, t_pushed, t_gain_final = text.head_back(
        after(text_unit_grad, i_first_grad),
        t_pooled,
        t_embedded,
        text_counts,
        ts_low,
        text_gains,
        tm_low,
    )
    packed = pack_factors(
        count,
        image,
        text,
        (i_sums, i_branch, i_final, i_embed_grad),
        (t_sums, t_branch, t_final, t_embed_grad),
    )
    sum_ie.got, packed, t_pushed = together(sum_ie.got, packed, t_pushed)
    factors = Factors(place, packed, image, text)
    sum_ie.step_one()
    factors.over_ns()
    i_back = image.attend_back(
        count,
        core,
        after(i_first_grad, sum_ie.sent, packed),
        ix,
        i_normed,
        i_packed,
        i_attended,
        image_gains,
        ia_low,
        io_low,
    )
    i_back, sum_ie.got, factors.messages = together(i_back, sum_ie.got, factors.messages)
    i_token_grad, i_near, i_far, i_gain_first = i_back
    factors.stack()
    sum_iao = RowSum(place, i_near, i_far)
    sum_ie.step_two()
    factors.spread = Spread(place, factors.blocks)
    t_back = text.feed_back(
        count,
        caption_length,
        core,
        after(t_first, sum_ie.sent, i_far, factors.blocks),
        text_gains,
        te_low,
        t_pushed,
        t_branch,
    )
    t_back, sum_ie.got, sum_iao.got, flown = together(
        t_back, sum_ie.got, sum_iao.got, factors.spread.flying()
    )
    factors.spread.landed(flown)
    t_first_grad, t_near, t_far, t_gain_second = t_back
    sum_te = RowSum(place, t_near, t_far)
    sum_ie.step_three()
    sum_iao.step_one()
    factors.spread.more()
    t_back = text.attend_back(
        count,
        core,
        after(t_first_grad, sum_ie.sent, sum_iao.sent, t_far),
        tx,
        t_normed,
        t_packed,
        t_attended,
        text_gains,
        ta_low,
        to_low,
    )
    t_back, sum_ie.got, sum_iao.got, sum_te.got, factors.spread.own = together(
        t_back, sum_ie.got, sum_iao.got, sum_te.got, factors.spread.own
    )
    t_token_grad, t_near, t_far, t_gain_first = t_back

    sum_tao = RowSum(place, t_near, t_far)
    sum_iao.step_two()
    far = place.swap_core(jnp.stack(factors.spread.own))
    sum_iao.got, sum_tao.got, far = together(sum_iao.got, sum_tao.got, far)
    factors.own, factors.far = factors.spread.own, far

    text_sums = (sum_te, sum_tao)
    for item in text_sums:
        item.step_one(False)
    in_step(place.swap_one, text_sums)
    sum_iao.step_three()
    grad_is, grad_im, grad_ts, grad_tm = factors.gradients()
    sum_iao.got, sum_te.got, sum_tao.got, grad_is, grad_im, grad_ts, grad_tm = together(
        sum_iao.got, sum_te.got, sum_tao.got, grad_is, grad_im, grad_ts, grad_tm
    )

    sum_ie.step_four()
    sum_iao.step_four()
    kept, got = last_step(place, (sum_ie, sum_iao))
    for item in text_sums:
        item.step_two(False)
    in_step(place.swap_two, text_sums)
    kept, got, sum_te.got, sum_tao.got = together(kept, got, sum_te.got, sum_tao.got)

    image_spread = Spread(place, kept + got)
    for item in text_sums:
        item.step_three(False)
    in_step(lambda value: place.swap_ns(value, 1), text_sums)
    flown, sum_te.got, sum_tao.got = together(
        image_spread.flying(), sum_te.got, sum_tao.got
    )
    image_spread.landed(flown)

    more = image_spread.more()
    sum_te.step_four()
    sum_tao.step_four()
    kept, got = last_step(place, (sum_te, sum_tao))
    image_spread.own[3], kept, got, image_token_grad, text_token_grad = together(
        more, kept, got, image.unpad(i_token_grad), text.unpad(t_token_grad)
    )
    image_sources = image_spread.finish()

    fresh_image = Fresh(
        place,
        ((image_expand_momentum,), (image_attention_momentum, image_output_momentum)),
        (image_shrink_momentum,),
        (0, 3, 1, 2),
        True,
    )
    fresh_text = Fresh(
        place,
        ((text_expand_momentum,), (text_attention_momentum, text_output_momentum)),
        (text_shrink_momentum, image_embedding_momentum, text_embedding_momentum),
        (0, 3, 1, 2, 4, 5),
        False,
    )
    text_spread = Spread(place, kept + got)
    image_sources, held = together(image_sources, text_spread.own[0])
    parts = fresh_image.gram(image_sources, [grad_is])
    small = pack_small(
        loss_part[0, 0],
        jnp.concatenate([i_gain_first, i_gain_second, i_gain_final], 0),
        jnp.concatenate([t_gain_first, t_gain_second, t_gain_final], 0),
    )
    other = place.swap_mask(after(small, held), 1)
    parts, flown, other = together(parts, text_spread.flying(), other)
    small = small + other
    text_spread.landed(flown)

    made = fresh_image.make([after(image_sources[0], parts[0])] + image_sources[1:], [grad_is])
    parts = over_ns(place, parts)
    more = text_spread.more()
    parts, text_spread.own[3], made = together(parts, more, made)
    fresh_ie, fresh_ia, fresh_io, fresh_is = made
    text_sources = text_spread.finish()

    parts = total_of(place, parts)
    text_sources, parts = together(text_sources, parts)
    text_parts = fresh_text.gram(text_sources, [grad_ts, grad_im, grad_tm])
    parts = over_ns(place, parts)
    other = place.swap_mask(after(small, text_sources[0]), 2)
    text_parts, parts, other = together(text_parts, parts, other)
    small = small + other

    parts, text_parts = together(
        parts + [place.swap_core(part) for part in parts], text_parts
    )
    image_poly = polynomial(place, parts, 3, TRI3)
    text_parts = over_ns(place, text_parts)
    other = place.swap_mask(after(small, parts[0]), 4)
    image_poly, text_parts, other = together(image_poly, text_parts, other)
    small = small + other

    image_spread = Spread(place, image_poly)
    text_parts = over_ns(place, total_of(place, text_parts))
    made = fresh_text.make(
        [after(text_sources[0], text_parts[0])] + text_sources[1:], [grad_ts, grad_im, grad_tm]
    )
    flown, text_parts, made = together(image_spread.flying(), text_parts, made)
    fresh_te, fresh_ta, fresh_to, fresh_ts, fresh_im, fresh_tm = made
    image_spread.landed(flown)

    text_poly = polynomial(place, text_parts, 2, TRI2)
    more = image_spread.more()
    text_poly, image_spread.own[3] = together(text_poly, more)
    image_sources = image_spread.finish()

    text_spread = Spread(place, text_poly)
    other = place.swap_ns(after(small, text_poly), 1)

    image_weights = apply_polynomials(
        place,
        image_sources,
        (image_expand, image_shrink, image_attention, image_output),
        (fresh_ie, fresh_is, fresh_ia, fresh_io),
        (0, 1, 2, 3),
        True,
    )
    image_weights, flown, other = together(image_weights, text_spread.flying(), other)
    small = small + other
    small = small + place.swap_ns(small, 2)
    for mask in place.extra:
        small = small + place.swap_mask(small, mask)
    next_ie, next_is, next_ia, next_io = image_weights
    text_spread.landed(flown)
    text_spread.more()
    next_te, next_ts, next_ta, next_to, next_im, next_tm = apply_polynomials(
        place,
        text_spread.finish(),
        (
            text_expand,
            text_shrink,
            text_attention,
            text_output,
            image_embedding,
            text_embedding,
        ),
        (fresh_te, fresh_ts, fresh_ta, fresh_to, fresh_im, fresh_tm),
        (0, 1, 2, 3, 4, 5),
        False,
    )
    loss_total, image_gain_sum = small[6, 0], small[:3]
    text_gain_sum = small[3:6, : text_gains.shape[1]]
    image_gain_next = MOMENTUM * image_gains_momentum + image_gain_sum
    text_gain_next = MOMENTUM * text_gains_momentum + text_gain_sum
    loss = jnp.reshape(loss_total / (images * place.n_dp * count), (1,))
    return (
        loss,
        image_token_grad,
        text_token_grad,
        fresh_ia,
        fresh_io,
        fresh_ie,
        fresh_is,
        fresh_im,
        fresh_ta,
        fresh_to,
        fresh_te,
        fresh_ts,
        fresh_tm,
        next_ia,
        next_io,
        next_ie,
        next_is,
        next_im,
        next_ta,
        next_to,
        next_te,
        next_ts,
        next_tm,
        image_gain_next,
        text_gain_next,
        image_gains - GAIN_RATE * image_gain_next,
        text_gains - GAIN_RATE * text_gain_next,
    )


def solution(mesh):
    placed = (
        P(("dp", "ns"), None, None),
        P(("dp", "ns"), None, None),
        P(),
        P(("dp", "ns")),
        P("ns", None),
        P("ns", None),
        P("ns", None),
        P("ns", None),
        P("ns", None),
        P("ns", None),
        P("ns", None),
        P("ns", None),
        P("ns", None),
        P("ns", None),
        P(),
        P(),
        P("ns", None),
        P("ns", None),
        P("ns", None),
        P("ns", None),
        P("ns", None),
        P("ns", None),
        P("ns", None),
        P("ns", None),
        P("ns", None),
        P("ns", None),
        P(),
        P(),
    )
    return jax.shard_map(
        per_device,
        mesh=mesh,
        in_specs=placed,
        out_specs=(
            P(),
            P(("dp", "ns"), None, None),
            P(("dp", "ns"), None, None),
            P("ns", None),
            P("ns", None),
            P("ns", None),
            P("ns", None),
            P("ns", None),
            P("ns", None),
            P("ns", None),
            P("ns", None),
            P("ns", None),
            P("ns", None),
            P("ns", None),
            P("ns", None),
            P("ns", None),
            P("ns", None),
            P("ns", None),
            P("ns", None),
            P("ns", None),
            P("ns", None),
            P("ns", None),
            P("ns", None),
            P(),
            P(),
            P(),
            P(),
        ),
        check_vma=False,
    )
```

```python
import math

import jax
import jax.numpy as jnp
from jax import lax
from jax.experimental import pallas as pl
from jax.experimental.pallas import tpu as pltpu
from jax.sharding import PartitionSpec as P

HI = 12
HT = 8
HEAD = 64

NORM_EPS = 1e-05
UNIT_EPS = 1e-06
SIM_SCALE = 30.0
MOMENTUM = 0.95
RATE = 0.5
GAIN_RATE = 0.5
COEF_A = 3.4445
COEF_B = -4.775
COEF_C = 2.0315
MASKED = -1000000000.0
HIGH = lax.Precision.HIGHEST
LOW = jnp.bfloat16
WIDE = jnp.float32

TRI3 = ((0, 0), (0, 1), (0, 2), (1, 1), (1, 2), (2, 2))
TRI2 = ((0, 0), (0, 1), (1, 1))
BLOCK = 256
IN_VMEM = pl.BlockSpec(memory_space=pltpu.VMEM)
IN_SMEM = pl.BlockSpec(memory_space=pltpu.SMEM)
IN_PLACE = pl.BlockSpec(memory_space=pl.ANY)


def call(body, out_shape, specs, micros, limit, scratch=(), name=None):
    outs = jax.tree.map(lambda _: IN_VMEM, out_shape)
    return pl.pallas_call(
        body,
        out_shape=out_shape,
        in_specs=specs,
        out_specs=outs,
        scratch_shapes=list(scratch),
        compiler_params=pltpu.CompilerParams(vmem_limit_bytes=limit << 20),
        cost_estimate=pl.CostEstimate(
            flops=int(1e4 * micros), bytes_accessed=16, transcendentals=0
        ),
        name=name,
    )


def after(value, *others):
    return lax.optimization_barrier((value,) + others)[0]


def shaped(shape, dtype=WIDE):
    return jax.ShapeDtypeStruct(shape, dtype)


class Place:
    def __init__(self):
        self.n_dp = lax.axis_size("dp")
        self.n_ns = lax.axis_size("ns")
        self.dp = lax.axis_index("dp")
        self.ns = lax.axis_index("ns")
        self.core = self.dp & 1
        along_x = (self.dp >> 1) & 1
        along_y = (self.dp >> 2) & 1
        self.bit_one = jnp.where(self.core == 0, along_x, along_y)
        self.bit_two = jnp.where(self.core == 0, along_y, along_x)
        self.chip = (self.dp >> 1) & 3
        self.piece = self.core * 4 + self.bit_one * 2 + self.bit_two
        self.extra = [1 << bit for bit in range(3, self.n_dp.bit_length() - 1)]
        self.core_at = self.core.astype(jnp.int32).reshape(1)
        self.blocks_at = jnp.stack([self.ns ^ mask for mask in range(self.n_ns)]).astype(jnp.int32)

    def over_dp(self, value, target):
        return lax.ppermute(value, "dp", [(i, target(i)) for i in range(self.n_dp)])

    def swap_mask(self, value, mask):
        return self.over_dp(value, lambda i: i ^ mask)

    def swap_core(self, value):
        return self.swap_mask(value, 1)

    def swap_one(self, value):
        return self.over_dp(value, lambda i: i ^ (2 if i % 2 == 0 else 4))

    def swap_two(self, value):
        return self.over_dp(value, lambda i: i ^ (4 if i % 2 == 0 else 2))

    def ring(self, value, steps=1):
        count = self.n_ns
        return lax.ppermute(value, "ns", [(i, (i + steps) % count) for i in range(count)])

    def swap_ns(self, value, mask):
        return lax.ppermute(value, "ns", [(i, i ^ mask) for i in range(self.n_ns)])

    def spread(self, value):
        first = self.swap_one(value)
        own = [value, first, self.swap_two(value), self.swap_two(first)]
        return own + [self.swap_core(item) for item in own]

    def spread_pieces(self):
        own = [self.piece ^ ((k & 1) * 2) ^ (k >> 1) for k in range(4)]
        base = (1 - self.core) * 4 + self.bit_two * 2 + self.bit_one
        return own + [base ^ ((k & 1) * 2) ^ (k >> 1) for k in range(4)]

    def spread_owners(self):
        mask_one = jnp.where(self.core == 0, 1, 2)
        mask_two = 3 - mask_one
        own = [self.chip ^ ((k & 1) * mask_one) ^ ((k >> 1) * mask_two) for k in range(4)]
        far = [self.chip ^ ((k & 1) * mask_two) ^ ((k >> 1) * mask_one) for k in range(4)]
        return own + far


class Spread:
    def __init__(self, place, value):
        self.place = place
        self.own = [value, place.swap_one(value), place.swap_two(value)]

    def flying(self):
        return self.own[1:]

    def landed(self, flown):
        self.own = [self.own[0]] + list(flown)

    def more(self):
        self.own.append(self.place.swap_two(self.own[1]))
        return self.own[3]

    def finish(self):
        return self.own + [self.place.swap_core(item) for item in self.own]


def pick(value, index, axis):
    return lax.dynamic_index_in_dim(value, index, axis, keepdims=False)


def unit_sizes(unit):
    rows, width = unit[0].shape
    if len(unit) == 1:
        return rows // 8, width, 8, 0
    rest = unit[1].shape[0]
    split = 6 if rest * 6 <= rows * 2 else 4
    return rows // split, width, split, rest // (8 - split)


def cut_kernel(sizes, at_ref, *refs):
    count = sum(2 if unit[2] < 8 else 1 for bundle in sizes for unit in bundle)
    units = [unit for bundle in sizes for unit in bundle]
    weights, outs = refs[:count], refs[count : count + len(sizes)]
    held, sems = refs[count + len(sizes) : -1], refs[-1]
    piece = at_ref[0]
    waits = []
    at = 0
    for number, (rows, _, split, rest) in enumerate(units):
        low = pltpu.make_async_copy(
            weights[at].at[pl.ds(pl.multiple_of(jnp.minimum(piece, split - 1) * rows, 8), rows)],
            held[number],
            sems.at[number],
        )
        at += 1
        if split == 8:
            low.start()
            waits.append(((None, low),))
            continue
        high = pltpu.make_async_copy(
            weights[at].at[pl.ds(pl.multiple_of(jnp.maximum(piece - split, 0) * rest, 8), rest)],
            held[number].at[:rest],
            sems.at[number],
        )
        at += 1
        if rest < rows:
            held[number][rest:] = jnp.zeros((rows - rest, held[number].shape[1]), WIDE)
        pl.when(piece < split)(low.start)
        pl.when(piece >= split)(high.start)
        waits.append(((piece < split, low), (piece >= split, high)))
    number = 0
    for bundle, out in zip(sizes, outs):
        row = 0
        for rows, width, _, _ in bundle:
            for condition, copy in waits[number]:
                if condition is None:
                    copy.wait()
                else:
                    pl.when(condition)(copy.wait)
            for column in range(0, width, BLOCK):
                out[row : row + rows] = held[number][:, column : column + BLOCK].astype(LOW)
                row += rows
            number += 1


def cut_pieces(place, bundles):
    sizes = [[unit_sizes(unit) for unit in bundle] for bundle in bundles]
    flat = [unit for bundle in sizes for unit in bundle]
    weights = [item for bundle in bundles for unit in bundle for item in unit]
    out_shape = [
        shaped((sum(unit[0] * unit[1] // BLOCK for unit in bundle), BLOCK), LOW)
        for bundle in sizes
    ]
    return call(
        lambda *refs: cut_kernel(sizes, *refs),
        out_shape,
        [IN_SMEM] + [IN_PLACE] * len(weights),
        1,
        56,
        [pltpu.VMEM(unit[:2], WIDE) for unit in flat]
        + [pltpu.SemaphoreType.DMA((len(flat),))],
        "cut_pieces",
    )(place.piece.astype(jnp.int32).reshape(1), *weights)


def lay_kernel(sizes, index_ref, *refs):
    count = sum(2 if unit[2] < 8 else 1 for unit in sizes)
    weights, sources, outs = refs[:count], refs[count : count + 8], refs[count + 8 :]
    at = row = 0
    for rows, width, split, rest in sizes:
        parts = ((8, rows),) if split == 8 else ((split, rows), (8 - split, rest))
        for part, (pieces, size) in enumerate(parts):
            own = weights[at + part][...].astype(LOW)
            outs[at + part][index_ref[0]] = own.reshape(pieces, size, width)
        for number, source in enumerate(sources):
            to_piece = index_ref[4 + number]
            for hop in range(3):
                to_block = index_ref[1 + hop]

                def lay(target, to_row, size):
                    for slab in range(width // BLOCK):
                        start = row + slab * rows
                        target[to_block, to_row, :, slab * BLOCK : (slab + 1) * BLOCK] = source[
                            hop, start : start + size
                        ]

                if split == 8:
                    lay(outs[at], to_piece, rows)
                else:
                    pl.when(to_piece < split)(lambda: lay(outs[at], to_piece, rows))
                    pl.when(to_piece >= split)(
                        lambda: lay(outs[at + 1], to_piece - split, rest)
                    )
        at += len(parts)
        row += rows * width // BLOCK


class Bundle:
    def __init__(self, place, piece, bundle):
        self.place, self.bundle, self.piece = place, bundle, piece

    def hops_direct(self):
        place = self.place
        self.hops = [place.ring(self.piece, steps) for steps in (1, 2, 3)]

    def hops_ring(self):
        place = self.place
        self.hops = [place.ring(self.piece)]
        self.hops.append(place.ring(self.hops[0]))
        self.hops.append(place.ring(self.hops[1]))

    def first_links(self, *waits):
        place = self.place
        held = after(jnp.stack(self.hops), *waits)
        self.own = [held, place.swap_one(held), place.swap_two(held)]

    def second_link(self, *waits):
        place = self.place
        if waits:
            gated = lax.optimization_barrier(tuple(self.own) + waits)
            self.own = list(gated[:3])
        self.own.append(place.swap_two(self.own[1]))

    def cores(self):
        self.far = [self.place.swap_core(item) for item in self.own]

    def lay(self):
        place, bundle = self.place, self.bundle
        sizes = [unit_sizes(unit) for unit in bundle]
        weights = [item for unit in bundle for item in unit]
        index = jnp.stack(
            [place.ns]
            + [(place.ns + place.n_ns - hop) % place.n_ns for hop in (1, 2, 3)]
            + place.spread_pieces()
        ).astype(jnp.int32)
        out_shape = []
        for rows, width, split, rest in sizes:
            out_shape.append(shaped((place.n_ns, split, rows, width), LOW))
            if split < 8:
                out_shape.append(shaped((place.n_ns, 8 - split, rest, width), LOW))
        whole = call(
            lambda *refs: lay_kernel(sizes, *refs),
            out_shape,
            [IN_SMEM] + [IN_VMEM] * (len(weights) + 8),
            5,
            60,
            name="lay_weights",
        )(index, *weights, *self.own, *self.far)
        return [item.reshape(-1, item.shape[-1]) for item in whole]


class RowSum:
    def __init__(self, place, near, far):
        for mask in place.extra:
            near = near + place.swap_mask(near, mask)
            far = far + place.swap_mask(far, mask)
        self.place, self.near = place, near
        self.got = place.swap_core(far)

    def halve(self, left, right, bit):
        count, rows, width = left.shape
        shape = (count, 2, rows // 2, width)
        left, right = left.reshape(shape), right.reshape(shape)
        self.kept = pick(left, bit, 1) + pick(right, bit, 1)
        self.sent = pick(left, 1 - bit, 1) + pick(right, 1 - bit, 1)

    def step_one(self, send=True):
        self.halve(self.near, self.got, self.place.bit_one)
        if send:
            self.got = self.place.swap_one(self.sent)

    def step_two(self, send=True):
        self.halve(self.kept, self.got, self.place.bit_two)
        if send:
            self.got = self.place.swap_two(self.sent)

    def step_three(self, send=True):
        place = self.place
        odd = place.ns & 1
        pairs = (2, 2) + self.kept.shape[1:]
        kept, got = self.kept.reshape(pairs), self.got.reshape(pairs)
        self.sent = pick(kept, 1 - odd, 1) + pick(got, 1 - odd, 1)
        self.kept = pick(kept, odd, 1) + pick(got, odd, 1)
        if send:
            self.got = place.swap_ns(self.sent, 1)

    def step_four(self):
        high = (self.place.ns >> 1) & 1
        self.sent = pick(self.kept, 1 - high, 0) + pick(self.got, 1 - high, 0)
        self.kept = pick(self.kept, high, 0) + pick(self.got, high, 0)


def in_step(swap, sums):
    got = swap(jnp.stack([item.sent for item in sums]))
    for at, item in enumerate(sums):
        item.got = got[at]
    return got


def last_step(place, sums):
    kept = jnp.stack([item.kept for item in sums])
    return kept, place.swap_ns(jnp.stack([item.sent for item in sums]), 2)


def over_ns(place, parts):
    return [parts[0]] + [place.swap_ns(part, mask) for mask, part in enumerate(parts) if mask]


def total_of(place, parts):
    total = parts[0].astype(WIDE)
    for part in parts[1:]:
        total = total + part.astype(WIDE)
    return [total.astype(LOW)] * place.n_ns


def place_kernel(index_ref, *refs):
    out_ref = refs[8]
    for at, source in enumerate(refs[:8]):
        out_ref[index_ref[at], index_ref[8 + at]] = source[...]


def lay_spread(place, sources, name):
    core = place.core
    index = jnp.stack(place.spread_owners() + [core] * 4 + [1 - core] * 4).astype(jnp.int32)
    return call(
        place_kernel,
        shaped((4, 2) + sources[0].shape, sources[0].dtype),
        [IN_SMEM] + [IN_VMEM] * 8,
        1,
        32,
        name=name,
    )(index, *sources)


def spread_numbers(place):
    core = place.core
    chips = place.chip ^ jnp.array([0, 1, 2, 3] * 2, jnp.int32)
    cores = jnp.stack([core] * 4 + [1 - core] * 4)
    base = place.dp - (place.dp & 7)
    over_dp = base + chips * 2 + cores
    numbers = (over_dp[:, None] * place.n_ns + place.blocks_at[None, :]).reshape(-1)
    for mask in place.extra:
        numbers = jnp.concatenate([numbers, numbers ^ (mask * place.n_ns)])
    return numbers


def gather_units(place, units):
    parts = [units] + [place.swap_ns(units, mask) for mask in range(1, place.n_ns)]
    held = jnp.stack(parts)
    sources = [held] + [place.swap_mask(held, mask) for mask in (2, 4, 6)]
    sources = sources + [place.swap_core(item) for item in sources]
    for mask in place.extra:
        sources = sources + [place.swap_mask(item, mask) for item in sources]
    return sources


def pack_small(loss_part, image_gain, text_gain):
    width = image_gain.shape[1]
    pad = width - text_gain.shape[1]
    return jnp.concatenate(
        [
            image_gain,
            jnp.pad(text_gain, ((0, 0), (0, pad))),
            jnp.broadcast_to(loss_part, (2, width)),
        ],
        0,
    )


def rows_by(left, right):
    return lax.dot_general(left, right, (((1,), (1,)), ((), ())), preferred_element_type=WIDE)


def product(left, right):
    return jnp.dot(left, right, preferred_element_type=WIDE)


def outer(left, right):
    return lax.dot_general(left, right, (((0,), (0,)), ((), ())), preferred_element_type=WIDE)


def normalize(values):
    shifted = values - jnp.mean(values, -1, keepdims=True)
    inverse = lax.rsqrt(jnp.mean(shifted * shifted, -1, keepdims=True) + NORM_EPS)
    return shifted * inverse, inverse


def norm_back(upstream, gain, unit_rows, inverse):
    scaled = upstream * gain
    inner = (
        scaled
        - jnp.mean(scaled, -1, keepdims=True)
        - unit_rows * jnp.mean(scaled * unit_rows, -1, keepdims=True)
    )
    return inner * inverse, jnp.sum(upstream * unit_rows, 0, keepdims=True)


def gate_of(hidden):
    return 0.5 * jnp.tanh(0.851 * hidden) + 0.5


class Tower:
    def __init__(self, count, span, width, hidden, heads, joint, causal):
        self.joint = joint
        self.count, self.span, self.width, self.hidden = count, span, width, hidden
        self.heads, self.causal = heads, causal
        self.padded = -(-span // 16) * 16
        self.rows = count * self.padded

    def valid(self, length_ref):
        at = lax.broadcasted_iota(jnp.int32, (self.padded, 1), 0)
        return jnp.concatenate(
            [(at < length_ref[number]).astype(WIDE) for number in range(self.count)], 0
        )

    def quarters(self):
        lane = lax.broadcasted_iota(jnp.int32, (1, BLOCK), 1)
        return [
            ((lane >= HEAD * at) & (lane < HEAD * (at + 1))).astype(WIDE).astype(LOW)
            for at in range(BLOCK // HEAD)
        ]

    def stacked(self, value, masks):
        return jnp.concatenate([value * mask for mask in masks], 0)

    def unstacked(self, value, masks):
        total = None
        for at, mask in enumerate(masks):
            part = value[at * self.padded : (at + 1) * self.padded] * mask.astype(WIDE)
            total = part if total is None else total + part
        return total

    def probabilities(self, left, right, over):
        scores = rows_by(left, right) * HEAD ** (-0.5)
        shape = scores.shape
        key = lax.broadcasted_iota(jnp.int32, shape, over)
        if self.causal:
            query = lax.broadcasted_iota(jnp.int32, shape, 1 - over)
            within = query - (query // self.padded) * self.padded
            scores = jnp.where(key <= within, scores, MASKED)
        elif self.padded != self.span:
            scores = jnp.where(key < self.span, scores, MASKED)
        raised = jnp.exp(scores - jnp.max(scores, over, keepdims=True))
        return raised * (1.0 / jnp.sum(raised, over, keepdims=True))

    def attend_kernel(
        self, x_ref, gains_ref, wa_ref, wo_ref, normed_ref, packed_ref, attended_ref, first_ref
    ):
        width = self.width
        unit_rows, _ = normalize(x_ref[...].astype(WIDE))
        normed_ref[...] = (unit_rows * gains_ref[0:1, :]).astype(LOW)
        for at in range(0, 3 * width, width):
            packed_ref[:, at : at + width] = rows_by(
                normed_ref[...], wa_ref[at : at + width, :]
            ).astype(LOW)
        masks = self.quarters()

        def one(number, carry):
            rows = pl.ds(pl.multiple_of(number * self.padded, 16), self.padded)
            for at in range(0, width, BLOCK):
                columns = slice(at, at + BLOCK)
                queries = self.stacked(packed_ref[rows, columns], masks)
                keys = packed_ref[rows, width + at : width + at + BLOCK]
                values = packed_ref[rows, 2 * width + at : 2 * width + at + BLOCK]
                probs = self.probabilities(queries, keys, 1).astype(LOW)
                attended_ref[rows, columns] = self.unstacked(product(probs, values), masks).astype(
                    LOW
                )
            return carry

        lax.fori_loop(0, self.count, one, 0, unroll=True)
        first_ref[...] = x_ref[...].astype(WIDE) + rows_by(attended_ref[...], wo_ref[...])

    def attend(self, x, gains, wa, wo):
        rows, width = self.rows, self.width
        return call(
            self.attend_kernel,
            [
                shaped((rows, width), LOW),
                shaped((rows, 3 * width), LOW),
                shaped((rows, width), LOW),
                shaped((rows, width)),
            ],
            [IN_VMEM] * 4,
            10,
            60,
            name="attend",
        )(x, gains, wa, wo)

    def feed_kernel(self, length_ref, first_ref, gains_ref, we_ref, sums_ref, pool_ref):
        valid = self.valid(length_ref)
        first = first_ref[...]
        unit_rows, _ = normalize(first)
        second = (unit_rows * gains_ref[1:2, :]).astype(LOW)

        def pooled(value):
            shape = (self.count, self.padded, value.shape[-1])
            return jnp.sum((value * valid).reshape(shape), 1)

        pool_ref[...] = pooled(first)
        step = self.hidden // 4
        for at in range(0, self.hidden, step):
            hidden = rows_by(second, we_ref[at : at + step, :])
            activated = (hidden * gate_of(hidden)).astype(LOW)
            sums_ref[:, at : at + step] = pooled(activated.astype(WIDE))

    def feed(self, lengths, first, gains, we):
        return call(
            self.feed_kernel,
            [shaped((self.count, self.hidden)), shaped((self.count, self.width))],
            [IN_SMEM] + [IN_VMEM] * 3,
            3,
            48,
            name="feed",
        )(lengths, first, gains, we)

    def head_kernel(
        self,
        sums_ref,
        pool_ref,
        counts_ref,
        ws_ref,
        gains_ref,
        wm_ref,
        pooled_ref,
        embedded_ref,
        unit_ref,
    ):
        sums = sums_ref[...]
        high = sums.astype(LOW)
        rest = (sums - high.astype(WIDE)).astype(LOW)
        total = pool_ref[...] + product(high, ws_ref[...]) + product(rest, ws_ref[...])
        pooled = total / counts_ref[...]
        unit_rows, _ = normalize(pooled)
        embedded = product((unit_rows * gains_ref[2:3, :]).astype(LOW), wm_ref[...])
        pooled_ref[...] = pooled
        embedded_ref[...] = embedded
        unit_ref[...] = embedded * lax.rsqrt(
            jnp.sum(embedded * embedded, -1, keepdims=True) + UNIT_EPS
        )

    def head(self, sums, pool, counts, ws, gains, wm):
        joint = wm.shape[1]
        return call(
            self.head_kernel,
            [
                shaped((self.count, self.width)),
                shaped((self.count, joint)),
                shaped((self.count, joint)),
            ],
            [IN_VMEM] * 6,
            1.5,
            32,
            name="head",
        )(sums, pool, counts, ws, gains, wm)

    def head_back_kernel(
        self,
        grad,
        pooled_ref,
        embedded_ref,
        counts_ref,
        ws_ref,
        gains_ref,
        wm_ref,
        embed_grad_ref,
        final_ref,
        branch_ref,
        pushed_ref,
        gain_ref,
    ):
        embedded = embedded_ref[...]
        inverse_norm = lax.rsqrt(jnp.sum(embedded * embedded, -1, keepdims=True) + UNIT_EPS)
        unit = embedded * inverse_norm
        along = jnp.sum(grad * unit, -1, keepdims=True)
        embed_grad = (inverse_norm * (grad - unit * along)).astype(LOW)
        embed_grad_ref[...] = embed_grad
        unit_rows, inverse = normalize(pooled_ref[...])
        gain = gains_ref[2:3, :]
        final_ref[...] = (unit_rows * gain).astype(LOW)
        pooled_grad, gain_grad = norm_back(
            rows_by(embed_grad, wm_ref[...]), gain, unit_rows, inverse
        )
        gain_ref[...] = gain_grad
        branch = pooled_grad / counts_ref[...]
        branch_ref[...] = branch
        pushed_ref[...] = rows_by(branch.astype(LOW), ws_ref[...])

    def head_back_shapes(self):
        count = self.count
        return [
            shaped((count, self.joint), LOW),
            shaped((count, self.width), LOW),
            shaped((count, self.width)),
            shaped((count, self.hidden)),
            shaped((1, self.width)),
        ]

    def head_back(self, grad, pooled, embedded, counts, ws, gains, wm):
        return call(
            lambda grad_ref, *refs: self.head_back_kernel(grad_ref[...], *refs),
            self.head_back_shapes(),
            [IN_VMEM] * 7,
            1.5,
            32,
            name="head_back",
        )(grad, pooled, embedded, counts, ws, gains, wm)

    def factor_cuts(self, blocks):
        cuts = [0]
        for size in (self.hidden // blocks, self.width, self.width // blocks, self.joint):
            cuts.append(cuts[-1] + size)
        return cuts

    def factor_rows(self, block, blocks, sums, branch, final, embed_grad):
        hidden, width = self.hidden // blocks, self.width // blocks
        return jnp.concatenate(
            [
                sums[:, block * hidden : (block + 1) * hidden],
                branch,
                final[:, block * width : (block + 1) * width].astype(WIDE),
                embed_grad.astype(WIDE),
            ],
            1,
        )

    def over_tokens(self, value):
        shape = (self.count, self.padded, value.shape[-1])
        return jnp.broadcast_to(value[:, None, :], shape).reshape(self.rows, shape[-1])

    def feed_back_kernel(self, length_ref, core_ref, *refs):
        for core in range(2):
            pl.when(core_ref[0] == core)(lambda: self.feed_back_body(core, length_ref, *refs))

    def feed_back_body(
        self,
        core,
        length_ref,
        first_ref,
        gains_ref,
        we_ref,
        pushed_ref,
        branch_ref,
        first_grad_ref,
        near_ref,
        far_ref,
        gain_ref,
    ):
        valid = self.valid(length_ref)
        gain = gains_ref[1:2, :]
        unit_rows, inverse = normalize(first_ref[...])
        second = (unit_rows * gain).astype(LOW)
        blocks, step, _ = near_ref.shape
        total = None
        for block in range(blocks):
            rows = slice(2 * block * step, 2 * (block + 1) * step)
            expand = we_ref[rows, :]
            hidden = rows_by(second, expand)
            gate = gate_of(hidden)
            slope = gate + (1.702 * hidden) * (gate * (1.0 - gate))
            pushed = self.over_tokens(pushed_ref[:, rows]) * valid
            hidden_grad = (pushed * slope).astype(LOW)
            grads = outer(hidden_grad, second).astype(LOW)
            term = product(hidden_grad, expand)
            total = term if total is None else total + term
            halves = (grads[:step], grads[step:])
            near_ref[block] = halves[core]
            far_ref[block] = halves[1 - core]

        second_grad, gain_grad = norm_back(total, gain, unit_rows, inverse)
        gain_ref[...] = gain_grad
        first_grad_ref[...] = self.over_tokens(branch_ref[...]) * valid + second_grad

    def feed_back(self, blocks, lengths, core, first, gains, we, pushed, branch):
        part = (blocks, self.hidden // (2 * blocks), self.width)
        return call(
            self.feed_back_kernel,
            [
                shaped((self.rows, self.width)),
                shaped(part, LOW),
                shaped(part, LOW),
                shaped((1, self.width)),
            ],
            [IN_SMEM] * 2 + [IN_VMEM] * 5,
            13,
            56,
            name="feed_back",
        )(lengths, core, first, gains, we, pushed, branch)

    def attend_back_kernel(
        self,
        core_ref,
        first_grad_ref,
        x_ref,
        normed_ref,
        packed_ref,
        attended_ref,
        gains_ref,
        wa_ref,
        wo_ref,
        token_ref,
        near_ref,
        far_ref,
        gain_ref,
        packed_grad_ref,
        attended_grad_ref,
    ):
        width = self.width
        first_low = first_grad_ref[...].astype(LOW)
        attended_grad_ref[...] = product(first_low, wo_ref[...]).astype(LOW)
        masks = self.quarters()

        def one(number, carry):
            rows = pl.ds(pl.multiple_of(number * self.padded, 16), self.padded)
            for at in range(0, width, BLOCK):
                spots = [slice(at + part * width, at + part * width + BLOCK) for part in range(3)]
                queries = self.stacked(packed_ref[rows, spots[0]], masks)
                keys, values = packed_ref[rows, spots[1]], packed_ref[rows, spots[2]]
                upstream = self.stacked(attended_grad_ref[rows, spots[0]], masks)
                probs = self.probabilities(keys, queries, 0)
                prob_grad = rows_by(values, upstream)
                score_grad = (
                    probs * (prob_grad - jnp.sum(prob_grad * probs, 0, keepdims=True))
                ).astype(LOW)
                scale = HEAD ** (-0.5)
                query_grad = self.unstacked(outer(score_grad, keys), masks) * scale
                packed_grad_ref[rows, spots[0]] = query_grad.astype(LOW)
                packed_grad_ref[rows, spots[1]] = (product(score_grad, queries) * scale).astype(
                    LOW
                )
                packed_grad_ref[rows, spots[2]] = product(probs.astype(LOW), upstream).astype(LOW)
            return carry

        lax.fori_loop(0, self.count, one, 0, unroll=True)
        blocks, half_rows, _ = near_ref.shape
        main_rows = 3 * width // blocks
        rest_rows = width // blocks

        def weights(core):
            def put(block, half, at, value):
                (near_ref if half == core else far_ref)[block, at : at + value.shape[0]] = value

            for block in range(blocks):
                start = block * main_rows
                grads = outer(packed_grad_ref[:, start : start + main_rows], normed_ref[...])
                grads = grads.astype(LOW)
                put(block, 0, 0, grads[:half_rows])
                put(block, 1, 0, grads[half_rows:])
                start = block * rest_rows
                grads = outer(first_low[:, start : start + rest_rows], attended_ref[...])
                put(block, 1, half_rows - rest_rows, grads.astype(LOW))

        pl.when(core_ref[0] == 0)(lambda: weights(0))
        pl.when(core_ref[0] == 1)(lambda: weights(1))
        unit_rows, inverse = normalize(x_ref[...].astype(WIDE))
        input_grad, gain_grad = norm_back(
            product(packed_grad_ref[...], wa_ref[...]), gains_ref[0:1, :], unit_rows, inverse
        )
        gain_ref[...] = gain_grad
        token_ref[...] = (first_grad_ref[...] + input_grad).astype(LOW)

    def attend_back(
        self, blocks, core, first_grad, x, normed, packed, attended, gains, wa, wo
    ):
        rows, width = self.rows, self.width
        part = (blocks, 2 * width // blocks, width)
        return call(
            self.attend_back_kernel,
            [
                shaped((rows, width), LOW),
                shaped(part, LOW),
                shaped(part, LOW),
                shaped((1, width)),
            ],
            [IN_SMEM] + [IN_VMEM] * 8,
            18,
            56,
            [pltpu.VMEM((rows, 3 * width), LOW), pltpu.VMEM((rows, width), LOW)],
            "attend_back",
        )(core, first_grad, x, normed, packed, attended, gains, wa, wo)

    def pad(self, tokens):
        extra = self.padded - self.span
        return jnp.pad(tokens, ((0, 0), (0, extra), (0, 0))).reshape(self.rows, self.width)

    def unpad(self, rows):
        return rows.reshape(self.count, self.padded, self.width)[:, : self.span]


SLOTS = 16


def contrast_kernel(
    images, captions, side, image, row_ref, column_ref, *refs
):
    sources, refs = refs[:8], refs[8:]
    head_refs, outs, (ws_ref, wm_ref, sems) = refs[:6], refs[6:-3], refs[-3:]
    copies = [
        pltpu.make_async_copy(source, target, sems.at[at])
        for at, (source, target) in enumerate(((head_refs[3], ws_ref), (head_refs[5], wm_ref)))
    ]
    for copy in copies:
        copy.start()
    every = jnp.concatenate(
        [ref[...].reshape(-1, ref.shape[-1]) for ref in sources], 0
    )
    sims = rows_by(every, every) * SIM_SCALE
    row_label, column_label = row_ref[...], column_ref[...]
    valid = (row_label >= 0) & (column_label >= 0)
    match = jnp.where(valid & (row_label == column_label), 1.0, 0.0)
    counts = jnp.maximum(jnp.sum(match, 1, keepdims=True), 1.0)
    masked = jnp.where(valid, sims, -1e30)
    row_top = jnp.max(masked, 1, keepdims=True)
    row_raised = jnp.where(valid, jnp.exp(masked - row_top), 0.0)
    row_total = jnp.maximum(jnp.sum(row_raised, 1, keepdims=True), 1e-30)
    column_top = jnp.max(masked, 0, keepdims=True)
    column_raised = jnp.where(valid, jnp.exp(masked - column_top), 0.0)
    column_total = jnp.maximum(jnp.sum(column_raised, 0, keepdims=True), 1e-30)
    picked = sims * match
    image_terms = row_top + jnp.log(row_total) - jnp.sum(picked, 1, keepdims=True) / counts
    caption_terms = column_top + jnp.log(column_total) - jnp.sum(picked, 0, keepdims=True)
    row_at = lax.broadcasted_iota(jnp.int32, image_terms.shape, 0)
    column_at = lax.broadcasted_iota(jnp.int32, caption_terms.shape, 1)
    own_caption = (column_at >= images) & (column_at < images + captions)
    loss = 0.5 * jnp.sum(
        jnp.where(row_at < images, image_terms, 0.0), keepdims=True
    ) + side * jnp.sum(jnp.where(own_caption, caption_terms, 0.0), keepdims=True)
    outs[1][...] = jnp.broadcast_to(loss, outs[1].shape)
    grad = 0.5 * (row_raised / row_total - match / counts) + side * (
        column_raised / column_total - match
    )
    wide = every.astype(WIDE)
    image_grad = jnp.dot(
        grad[:SLOTS], wide, precision=HIGH, preferred_element_type=WIDE
    )
    text_grad = lax.dot_general(
        grad[:, :128],
        wide,
        (((0,), (0,)), ((), ())),
        precision=HIGH,
        preferred_element_type=WIDE,
    )
    outs[0][...] = SIM_SCALE * text_grad[images : images + captions]
    for copy in copies:
        copy.wait()
    pooled_ref, embedded_ref, counts_ref, _, gains_ref, _ = head_refs
    image.head_back_kernel(
        SIM_SCALE * image_grad[:images],
        pooled_ref,
        embedded_ref,
        counts_ref,
        ws_ref,
        gains_ref,
        wm_ref,
        *outs[2:],
    )


def contrast_whole(images, captions, side, row_label, column_label, sources):
    every = jnp.concatenate([item.reshape(-1, item.shape[-1]) for item in sources], 0)
    joint = every.shape[-1]
    slots = every.reshape(-1, SLOTS, joint)
    every_image = slots[:, :images].reshape(-1, joint)
    every_text = slots[:, images : images + captions].reshape(-1, joint)
    image_ids = row_label.reshape(-1, SLOTS)[:, :images].reshape(-1)
    named = column_label.reshape(-1, SLOTS)[:, images : images + captions].reshape(-1)
    match = (named[None, :] == image_ids[:, None]).astype(WIDE)
    counts = jnp.sum(match, 1, keepdims=True)
    sims = rows_by(every_image, every_text) * SIM_SCALE
    row_log = jax.scipy.special.logsumexp(sims, axis=1, keepdims=True)
    col_log = jax.scipy.special.logsumexp(sims, axis=0, keepdims=True)
    image_terms = row_log - jnp.sum(sims * match, 1, keepdims=True) / counts
    caption_terms = col_log - jnp.sum(sims * match, 0, keepdims=True)
    loss_part = 0.5 * jnp.sum(image_terms[:images]) + side * jnp.sum(caption_terms[:, :captions])
    grad = 0.5 * (jnp.exp(sims - row_log) - match / counts) + side * (
        jnp.exp(sims - col_log) - match
    )
    image_unit_grad = SIM_SCALE * jnp.dot(
        grad[:images], every_text.astype(WIDE), precision=HIGH
    )
    text_unit_grad = SIM_SCALE * lax.dot_general(
        grad[:, :captions],
        every_image.astype(WIDE),
        (((0,), (0,)), ((), ())),
        precision=HIGH,
        preferred_element_type=WIDE,
    )
    return image_unit_grad, text_unit_grad, jnp.broadcast_to(loss_part, (1, 128))


def contrast_labels(place, images, captions, caption_image):
    numbers = spread_numbers(place)
    at = jnp.arange(SLOTS, dtype=jnp.int32)[None, :]
    image_ids = jnp.where(at < images, numbers[:, None] * images + at, -1)
    named = jnp.take(caption_image.reshape(-1, captions), numbers, axis=0)
    named = jnp.pad(
        named, ((0, 0), (images, SLOTS - images - captions)), constant_values=-1
    )
    return image_ids.reshape(-1, 1), named.reshape(1, -1)


def contrast(place, image, head, image_unit, text_unit, row_label, column_label):
    images, captions, joint = image_unit.shape[0], text_unit.shape[0], text_unit.shape[1]
    blank = jnp.zeros((SLOTS - images - captions, joint), LOW)
    units = jnp.concatenate([image_unit.astype(LOW), text_unit.astype(LOW), blank], 0)
    sources = gather_units(place, units)
    side = 0.5 * images / captions
    if len(sources) > 8:
        image_grad, text_grad, loss_part = contrast_whole(
            images, captions, side, row_label, column_label, sources
        )
        return [text_grad, loss_part] + list(image.head_back(image_grad, *head))
    return call(
        lambda *refs: contrast_kernel(images, captions, side, image, *refs),
        [shaped((captions, joint)), shaped((1, 128))] + image.head_back_shapes(),
        [IN_VMEM] * 13 + [IN_PLACE, IN_VMEM, IN_PLACE],
        5,
        56,
        [
            pltpu.VMEM(head[3].shape, LOW),
            pltpu.VMEM(head[5].shape, LOW),
            pltpu.SemaphoreType.DMA((2,)),
        ],
        name="contrast",
    )(row_label, column_label, *sources, *head)


def together(*values):
    return lax.optimization_barrier(values)


class Factors:
    def __init__(self, place, packed, image, text):
        self.place, self.towers = place, (image, text)
        self.messages = [pick(packed, place.ns ^ mask, 0) for mask in range(place.n_ns)]

    def over_ns(self):
        place = self.place
        self.messages = [
            place.swap_ns(item, mask) if mask else item for mask, item in enumerate(self.messages)
        ]

    def stack(self):
        self.blocks = jnp.stack(self.messages)

    def every(self):
        place = self.place
        sources = self.own + [self.far[at] for at in range(4)]
        every = lay_spread(place, sources, "place_factors")
        every = every.reshape((-1,) + every.shape[3:])
        for mask in place.extra:
            other = place.swap_mask(every, mask)
            every = jnp.where(
                (place.dp & mask) == 0,
                jnp.concatenate([every, other], 0),
                jnp.concatenate([other, every], 0),
            )
        return every.reshape(-1, every.shape[-1])

    def products(self, every, dot):
        image, text = self.towers
        blocks = self.place.n_ns
        slot = lax.broadcasted_iota(jnp.int32, (every.shape[0], 1), 0) % SLOTS
        outs = []
        for tower, own in ((image, slot < image.count), (text, slot >= SLOTS - text.count)):
            cuts = tower.factor_cuts(blocks)
            held = every * jnp.where(own, 1.0, 0.0).astype(LOW)
            pieces = [held[:, low:high] for low, high in zip(cuts, cuts[1:])]
            outs += [dot(pieces[0], pieces[1]), dot(pieces[2], pieces[3])]
        return outs

    def kernel(self, index_ref, *refs):
        own_refs, far_ref, outs, every_ref = refs[:4], refs[4], refs[5:9], refs[9]
        rows = every_ref.shape[0] // 8
        for at in range(8):
            to = pl.ds(pl.multiple_of(index_ref[at] * rows, rows), rows)
            source = own_refs[at][...] if at < 4 else far_ref[at - 4]
            every_ref[to] = source.reshape(rows, source.shape[-1])
        for out_ref, value in zip(outs, self.products(every_ref[...], outer)):
            out_ref[...] = value

    def gradients(self):
        place = self.place
        if place.extra:
            return self.products(self.every(), outer)
        image, text = self.towers
        blocks, core = place.n_ns, place.core
        index = jnp.stack(
            [
                chip * 2 + (core if at < 4 else 1 - core)
                for at, chip in enumerate(place.spread_owners())
            ]
        ).astype(jnp.int32)
        columns = self.own[0].shape[-1]
        out_shape = []
        for tower in (image, text):
            out_shape.append(shaped((tower.hidden // blocks, tower.width)))
            out_shape.append(shaped((tower.width // blocks, tower.joint)))
        return call(
            self.kernel,
            out_shape,
            [IN_SMEM] + [IN_VMEM] * 5,
            4,
            48,
            [pltpu.VMEM((8 * blocks * SLOTS, columns), LOW)],
            name="factor_grads",
        )(index, *self.own, self.far)


def pack_factors(blocks, image, text, image_parts, text_parts):
    columns = max(image.factor_cuts(blocks)[-1], text.factor_cuts(blocks)[-1])

    def body(*refs):
        out_ref = refs[8]
        first, second = [ref[...] for ref in refs[:4]], [ref[...] for ref in refs[4:8]]
        out_ref[...] = jnp.zeros(out_ref.shape, LOW)
        for block in range(blocks):
            rows = image.factor_rows(block, blocks, *first)
            lower = jnp.zeros((SLOTS - text.count - image.count, rows.shape[1]), WIDE)
            rows = jnp.concatenate([rows, lower], 0)
            more = text.factor_rows(block, blocks, *second)
            blank = jnp.zeros((text.count, columns - more.shape[1]), WIDE)
            more = jnp.concatenate([more, blank], 1)
            out_ref[block] = jnp.concatenate([rows, more], 0).astype(LOW)

    return call(
        body,
        shaped((blocks, SLOTS, columns), LOW),
        [IN_VMEM] * 8,
        1,
        32,
        name="pack_factors",
    )(*image_parts, *text_parts)


class Fresh:
    def __init__(self, place, units, others, owners, per_chip):
        self.place, self.units, self.others = place, units, others
        self.owners, self.per_chip = owners, per_chip
        self.width = units[0][0].shape[1]
        self.rows = sum(item.shape[0] for item in units[0])
        self.pairs = TRI3 if per_chip else TRI2

        self.moments = [item for unit in units for item in unit] + list(others)
        owner = place.chip if per_chip else place.chip * 2 + place.core
        self.info = jnp.concatenate(
            [
                jnp.stack([owner, place.core]).astype(jnp.int32),
                place.blocks_at,
                jnp.stack(place.spread_pieces()).astype(jnp.int32),
            ]
        )

    def spots(self):
        out = []
        for unit_at, unit in enumerate(self.units):
            split = unit[0].shape[0] * 8 // self.rows
            out.append((unit_at, 0, split))
            if len(unit) > 1:
                out.append((unit_at, split, 8))
        return out

    def lay(self, info_ref, sources, at, put):
        unit_at, low, high = self.spots()[at]
        size = self.rows // 8
        for number, source in enumerate(sources):
            piece = info_ref[6 + number]

            def one():
                put(pl.ds(pl.multiple_of((piece - low) * size, size), size), source[unit_at])

            if (low, high) == (0, 8):
                one()
            else:
                pl.when((piece >= low) & (piece < high))(one)

    def gram_kernel(self, info_ref, *refs):
        gathered = len(self.spots())
        sources, refs = refs[:8], refs[8:]
        grads, refs = refs[: len(self.others)], refs[len(self.others) :]
        moments, refs = refs[: len(self.moments)], refs[len(self.moments) :]
        part_refs, (moment_ref, grad_ref, chosen_ref, gram_ref, sems) = refs[:-5], refs[-5:]
        for owner, at in enumerate(self.owners):

            @pl.when(info_ref[0] == owner)
            def _():
                rows = self.moments[at].shape[0]
                copies = [
                    pltpu.make_async_copy(moments[at], moment_ref.at[:rows], sems.at[0])
                ]
                if at >= gathered:
                    copies.append(
                        pltpu.make_async_copy(
                            grads[at - gathered], grad_ref.at[:rows], sems.at[1]
                        )
                    )
                for copy in copies:
                    copy.start()
                if rows < self.rows:
                    chosen_ref[rows:] = jnp.zeros((self.rows - rows, self.width), LOW)
                for copy in copies:
                    copy.wait()

                def put(where, gradient):
                    chosen_ref[where] = (
                        MOMENTUM * moment_ref[where] + gradient.astype(WIDE)
                    ).astype(LOW)

                if at < gathered:
                    self.lay(info_ref, sources, at, put)
                else:
                    put(slice(0, rows), grad_ref[:rows])

        @pl.when(info_ref[0] >= len(self.owners))
        def _():
            chosen_ref[...] = jnp.zeros((self.rows, self.width), LOW)

        def blocks(pairs):
            for number, (i, j) in enumerate(pairs):
                left = chosen_ref[:, i * BLOCK : (i + 1) * BLOCK]
                right = chosen_ref[:, j * BLOCK : (j + 1) * BLOCK]
                gram_ref[number * BLOCK : (number + 1) * BLOCK] = outer(left, right).astype(LOW)

        if self.per_chip:
            pl.when(info_ref[1] == 0)(lambda: blocks(self.pairs[:3]))
            pl.when(info_ref[1] == 1)(lambda: blocks(self.pairs[3:]))
        else:
            blocks(self.pairs)
        size = gram_ref.shape[0] // len(part_refs)
        for number, part_ref in enumerate(part_refs):
            at = info_ref[2 + number]
            part_ref[...] = gram_ref[pl.ds(pl.multiple_of(at * size, size), size)]

    def gram(self, sources, grads):
        count = self.place.n_ns
        return call(
            self.gram_kernel,
            [shaped((3 * BLOCK // count, BLOCK), LOW)] * count,
            [IN_SMEM] + [IN_VMEM] * 8 + [IN_PLACE] * (len(grads) + len(self.moments)),
            3,
            56,
            [
                pltpu.VMEM((self.rows, self.width), WIDE),
                pltpu.VMEM((self.rows, self.width), WIDE),
                pltpu.VMEM((self.rows, self.width), LOW),
                pltpu.VMEM((3 * BLOCK, BLOCK), LOW),
                pltpu.SemaphoreType.DMA((2,)),
            ],
            "gram",
        )(self.info, *sources, *grads, *self.moments)

    def fresh_kernel(self, info_ref, *refs):
        gathered, total = len(self.spots()), len(self.moments)
        sources, refs = refs[:8], refs[8:]
        grads, refs = refs[: len(self.others)], refs[len(self.others) :]
        moments, fresh = refs[:total], refs[total:]
        for at in range(total):

            def put(where, gradient):
                fresh[at][where] = MOMENTUM * moments[at][where] + gradient.astype(WIDE)

            if at < gathered:
                self.lay(info_ref, sources, at, put)
            else:
                put(slice(None), grads[at - gathered][...])

    def make(self, sources, grads):
        return call(
            self.fresh_kernel,
            [shaped(item.shape) for item in self.moments],
            [IN_SMEM] + [IN_VMEM] * (8 + len(grads) + len(self.moments)),
            5,
            60,
            name="freshen",
        )(self.info, *sources, *grads, *self.moments)


def polynomial_kernel(side, pairs, info_ref, *refs):
    count = info_ref.shape[0] - 1
    parts, out_ref, gram_ref = list(refs[:count]), refs[-2], refs[-1]
    if len(refs) > count + 2:
        parts += [refs[count].at[at] for at in range(count)]
    size = parts[0].shape[0]
    core = info_ref[count]
    for number, part in enumerate(parts):
        at = info_ref[number % count]
        half = 0 if side == 2 else (core if number < count else 1 - core)
        gram_ref[half, pl.ds(pl.multiple_of(at * size, size), size)] = part[...]
    blocks = {
        pair: gram_ref[at // 3, at % 3 * BLOCK : (at % 3 + 1) * BLOCK].astype(WIDE)
        for at, pair in enumerate(pairs)
    }
    rows = [
        jnp.concatenate(
            [blocks[(i, j)] if i <= j else blocks[(j, i)].T for j in range(side)], 1
        )
        for i in range(side)
    ]
    square = jnp.concatenate(rows, 0)
    span = side * BLOCK
    same = lax.broadcasted_iota(jnp.int32, (span, span), 0) == lax.broadcasted_iota(
        jnp.int32, (span, span), 1
    )
    factor = 1.0 / (jnp.sqrt(jnp.sum(jnp.where(same, square, 0.0))) + 1e-07)
    square = square * (factor * factor)

    def mm(left, right):
        return product(left.astype(LOW), right.astype(LOW))

    def terms(value):
        return COEF_B * value + COEF_C * mm(value, value)

    def following(value, term):
        half = COEF_A * value + mm(value, term)
        return COEF_A * half + mm(half, term)

    term_zero = terms(square)
    square = following(square, term_zero)
    term_one = terms(square)
    square = following(square, term_one)
    term_two = terms(square)
    both = COEF_A * (term_zero + term_one) + mm(term_zero, term_one)
    both_low, two_low = both.astype(LOW), term_two.astype(LOW)

    def give(chosen):
        top, left = min(i for i, _ in chosen) * BLOCK, min(j for _, j in chosen) * BLOCK
        bottom = (max(i for i, _ in chosen) + 1) * BLOCK
        rows, columns = slice(top, bottom), slice(left, span)
        whole = (
            COEF_A**2 * term_two[rows, columns]
            + COEF_A * both[rows, columns]
            + product(both_low[rows, :], two_low[:, columns])
        )
        whole = factor * (whole + jnp.where(same[rows, columns], COEF_A**3, 0.0))
        for at, (i, j) in enumerate(chosen):
            out_ref[at] = whole[
                i * BLOCK - top : (i + 1) * BLOCK - top, j * BLOCK - left : (j + 1) * BLOCK - left
            ].astype(LOW)

    if side == 2:
        give(pairs)
    else:
        pl.when(core == 0)(lambda: give(pairs[:3]))
        pl.when(core == 1)(lambda: give(pairs[3:]))


def polynomial(place, parts, side, pairs):
    return call(
        lambda *refs: polynomial_kernel(side, pairs, *refs),
        shaped((3, BLOCK, BLOCK), LOW),
        [IN_SMEM] + [IN_VMEM] * len(parts),
        4 if side == 2 else 10,
        60,
        [pltpu.VMEM((len(pairs) // 3, 3 * BLOCK, BLOCK), LOW)],
        name="polynomial",
    )(jnp.concatenate([place.blocks_at, place.core_at]), *parts)


def apply_kernel(weights, per_chip, info_ref, *refs):
    count = len(weights)
    sources, refs, held_ref = refs[:8], refs[8:-1], refs[-1]
    masters, fresh, outs = refs[:count], refs[count : 2 * count], refs[2 * count :]
    for at, source in enumerate(sources):
        held_ref[info_ref[at]] = source[...]
    for at, (owner, scale) in enumerate(weights):
        rows, width = outs[at].shape
        side = width // BLOCK
        pairs = TRI3 if per_chip else TRI2

        def block(i, j):
            number = pairs.index((min(i, j), max(i, j)))
            if per_chip:
                return held_ref[2 * owner + number // 3, number % 3]
            return held_ref[owner, number]

        for start in range(0, rows, BLOCK):
            spot = slice(start, min(start + BLOCK, rows))
            left = fresh[at][spot].astype(LOW)
            for j in range(side):
                total = None
                for i in range(side):
                    part = left[:, i * BLOCK : (i + 1) * BLOCK]
                    term = product(part, block(i, j)) if i <= j else rows_by(part, block(i, j))
                    total = term if total is None else total + term
                columns = slice(j * BLOCK, (j + 1) * BLOCK)
                outs[at][spot, columns] = masters[at][spot, columns] - scale * total


def apply_polynomials(place, sources, masters, fresh, owners, per_chip):
    core = place.core
    info = jnp.stack(
        [
            chip * 2 + (core if at < 4 else 1 - core)
            for at, chip in enumerate(place.spread_owners())
        ]
    ).astype(jnp.int32)
    weights = [
        (owner, RATE * math.sqrt(item.shape[0] * place.n_ns / item.shape[1]))
        for owner, item in zip(owners, masters)
    ]
    return call(
        lambda *refs: apply_kernel(weights, per_chip, *refs),
        [shaped(item.shape) for item in masters],
        [IN_SMEM] + [IN_VMEM] * (8 + 2 * len(masters)),
        6,
        60 if per_chip else 40,
        [pltpu.VMEM((8,) + sources[0].shape, LOW)],
        "apply_polynomials",
    )(info, *sources, *masters, *fresh)


def per_device(
    image_tokens,
    text_tokens,
    caption_image,
    caption_length,
    image_attention,
    image_output,
    image_expand,
    image_shrink,
    image_embedding,
    text_attention,
    text_output,
    text_expand,
    text_shrink,
    text_embedding,
    image_gains,
    text_gains,
    image_attention_momentum,
    image_output_momentum,
    image_expand_momentum,
    image_shrink_momentum,
    image_embedding_momentum,
    text_attention_momentum,
    text_output_momentum,
    text_expand_momentum,
    text_shrink_momentum,
    text_embedding_momentum,
    image_gains_momentum,
    text_gains_momentum,
):
    place = Place()
    count = place.n_ns
    joint = text_embedding.shape[1]
    bundles = (
        ((text_attention, text_output),),
        ((text_expand,), (text_shrink,)),
        ((image_attention, image_output), (image_embedding, text_embedding)),
        ((image_expand,), (image_shrink,)),
    )
    pieces = cut_pieces(place, bundles)
    one = Bundle(place, pieces[0], bundles[0])
    one.hops_direct()
    two = Bundle(place, after(pieces[1], *one.hops), bundles[1])
    two.hops_direct()
    three = Bundle(place, after(pieces[2], *two.hops), bundles[2])
    three.hops_direct()
    one.first_links()
    one.second_link()
    one.cores()
    two.first_links()
    three.first_links(*two.own[1:])

    images, image_span, image_width = image_tokens.shape
    captions, text_span, text_width = text_tokens.shape
    image = Tower(images, image_span, image_width, image_expand.shape[0] * count, HI, joint, False)
    text = Tower(captions, text_span, text_width, text_expand.shape[0] * count, HT, joint, True)
    image_lengths = jnp.full((images,), image_span, jnp.int32)
    image_counts = jnp.full((images, 1), image_span, WIDE)
    text_counts = caption_length.astype(WIDE).reshape(captions, 1)
    core = place.core.astype(jnp.int32).reshape(1)

    ta_low, to_low = one.lay()
    row_label, column_label = contrast_labels(place, images, captions, caption_image)
    tx = text.pad(text_tokens)
    t_normed, t_packed, t_attended, t_first = text.attend(
        after(tx, row_label, column_label), text_gains, ta_low, to_low
    )
    four = Bundle(place, after(pieces[3], t_attended), bundles[3])
    four.hops_ring()
    four.first_links(*three.own[1:])
    two.second_link(t_attended)
    two.cores()
    te_low, ts_low = two.lay()
    t_sums, t_pool = text.feed(caption_length, t_first, text_gains, te_low)
    three.second_link(t_sums)
    three.cores()
    ia_low, io_low, im_low, tm_low = three.lay()
    t_pooled, t_embedded, t_unit = text.head(
        t_sums, t_pool, text_counts, ts_low, text_gains, tm_low
    )
    ix = image.pad(image_tokens)
    i_normed, i_packed, i_attended, i_first = image.attend(ix, image_gains, ia_low, io_low)
    four.second_link(i_attended)
    four.own[3], t_pooled, t_embedded, t_unit = together(
        four.own[3], t_pooled, t_embedded, t_unit
    )
    four.cores()
    ie_low, is_low = four.lay()
    i_sums, i_pool = image.feed(image_lengths, i_first, image_gains, ie_low)
    i_pooled, i_embedded, i_unit = image.head(
        i_sums, i_pool, image_counts, is_low, image_gains, im_low
    )

    (
        text_unit_grad,
        loss_part,
        i_embed_grad,
        i_final,
        i_branch,
        i_pushed,
        i_gain_final,
    ) = contrast(
        place,
        image,
        (i_pooled, i_embedded, image_counts, is_low, image_gains, im_low),
        i_unit,
        t_unit,
        row_label,
        column_label,
    )
    i_first_grad, i_near, i_far, i_gain_second = image.feed_back(
        count, image_lengths, core, i_first, image_gains, ie_low, i_pushed, i_branch
    )
    sum_ie = RowSum(place, i_near, i_far)
    t_embed_grad, t_final, t_branch, t_pushed, t_gain_final = text.head_back(
        after(text_unit_grad, i_first_grad),
        t_pooled,
        t_embedded,
        text_counts,
        ts_low,
        text_gains,
        tm_low,
    )
    packed = pack_factors(
        count,
        image,
        text,
        (i_sums, i_branch, i_final, i_embed_grad),
        (t_sums, t_branch, t_final, t_embed_grad),
    )
    sum_ie.got, packed, t_pushed = together(sum_ie.got, packed, t_pushed)
    factors = Factors(place, packed, image, text)
    sum_ie.step_one()
    factors.over_ns()
    i_back = image.attend_back(
        count,
        core,
        after(i_first_grad, sum_ie.sent, packed),
        ix,
        i_normed,
        i_packed,
        i_attended,
        image_gains,
        ia_low,
        io_low,
    )
    i_back, sum_ie.got, factors.messages = together(i_back, sum_ie.got, factors.messages)
    i_token_grad, i_near, i_far, i_gain_first = i_back
    factors.stack()
    sum_iao = RowSum(place, i_near, i_far)
    sum_ie.step_two()
    factors.spread = Spread(place, factors.blocks)
    t_back = text.feed_back(
        count,
        caption_length,
        core,
        after(t_first, sum_ie.sent, i_far, factors.blocks),
        text_gains,
        te_low,
        t_pushed,
        t_branch,
    )
    t_back, sum_ie.got, sum_iao.got, flown = together(
        t_back, sum_ie.got, sum_iao.got, factors.spread.flying()
    )
    factors.spread.landed(flown)
    t_first_grad, t_near, t_far, t_gain_second = t_back
    sum_te = RowSum(place, t_near, t_far)
    sum_ie.step_three()
    sum_iao.step_one()
    factors.spread.more()
    t_back = text.attend_back(
        count,
        core,
        after(t_first_grad, sum_ie.sent, sum_iao.sent, t_far),
        tx,
        t_normed,
        t_packed,
        t_attended,
        text_gains,
        ta_low,
        to_low,
    )
    t_back, sum_ie.got, sum_iao.got, sum_te.got, factors.spread.own = together(
        t_back, sum_ie.got, sum_iao.got, sum_te.got, factors.spread.own
    )
    t_token_grad, t_near, t_far, t_gain_first = t_back

    sum_tao = RowSum(place, t_near, t_far)
    sum_iao.step_two()
    far = place.swap_core(jnp.stack(factors.spread.own))
    sum_iao.got, sum_tao.got, far = together(sum_iao.got, sum_tao.got, far)
    factors.own, factors.far = factors.spread.own, far

    text_sums = (sum_te, sum_tao)
    for item in text_sums:
        item.step_one(False)
    in_step(place.swap_one, text_sums)
    sum_iao.step_three()
    grad_is, grad_im, grad_ts, grad_tm = factors.gradients()
    sum_iao.got, sum_te.got, sum_tao.got, grad_is, grad_im, grad_ts, grad_tm = together(
        sum_iao.got, sum_te.got, sum_tao.got, grad_is, grad_im, grad_ts, grad_tm
    )

    sum_ie.step_four()
    sum_iao.step_four()
    kept, got = last_step(place, (sum_ie, sum_iao))
    for item in text_sums:
        item.step_two(False)
    in_step(place.swap_two, text_sums)
    kept, got, sum_te.got, sum_tao.got = together(kept, got, sum_te.got, sum_tao.got)

    image_spread = Spread(place, kept + got)
    for item in text_sums:
        item.step_three(False)
    in_step(lambda value: place.swap_ns(value, 1), text_sums)
    flown, sum_te.got, sum_tao.got = together(
        image_spread.flying(), sum_te.got, sum_tao.got
    )
    image_spread.landed(flown)

    more = image_spread.more()
    sum_te.step_four()
    sum_tao.step_four()
    kept, got = last_step(place, (sum_te, sum_tao))
    image_spread.own[3], kept, got, image_token_grad, text_token_grad = together(
        more, kept, got, image.unpad(i_token_grad), text.unpad(t_token_grad)
    )
    image_sources = image_spread.finish()

    fresh_image = Fresh(
        place,
        ((image_expand_momentum,), (image_attention_momentum, image_output_momentum)),
        (image_shrink_momentum,),
        (0, 3, 1, 2),
        True,
    )
    fresh_text = Fresh(
        place,
        ((text_expand_momentum,), (text_attention_momentum, text_output_momentum)),
        (text_shrink_momentum, image_embedding_momentum, text_embedding_momentum),
        (0, 3, 1, 2, 4, 5),
        False,
    )
    text_spread = Spread(place, kept + got)
    image_sources, held = together(image_sources, text_spread.own[0])
    parts = fresh_image.gram(image_sources, [grad_is])
    small = pack_small(
        loss_part[0, 0],
        jnp.concatenate([i_gain_first, i_gain_second, i_gain_final], 0),
        jnp.concatenate([t_gain_first, t_gain_second, t_gain_final], 0),
    )
    other = place.swap_mask(after(small, held), 1)
    parts, flown, other = together(parts, text_spread.flying(), other)
    small = small + other
    text_spread.landed(flown)

    made = fresh_image.make([after(image_sources[0], parts[0])] + image_sources[1:], [grad_is])
    parts = over_ns(place, parts)
    more = text_spread.more()
    parts, text_spread.own[3], made = together(parts, more, made)
    fresh_ie, fresh_ia, fresh_io, fresh_is = made
    text_sources = text_spread.finish()

    parts = total_of(place, parts)
    text_sources, parts = together(text_sources, parts)
    text_parts = fresh_text.gram(text_sources, [grad_ts, grad_im, grad_tm])
    parts = over_ns(place, parts)
    other = place.swap_mask(after(small, text_sources[0]), 2)
    text_parts, parts, other = together(text_parts, parts, other)
    small = small + other

    parts = parts + [place.swap_core(jnp.stack(parts))]
    text_parts = over_ns(place, text_parts)
    image_poly = polynomial(place, parts, 3, TRI3)
    other = place.swap_mask(after(small, parts[0]), 4)
    image_poly, text_parts, other = together(image_poly, text_parts, other)
    small = small + other

    image_spread = Spread(place, image_poly)
    text_parts = over_ns(place, total_of(place, text_parts))
    made = fresh_text.make(
        [after(text_sources[0], text_parts[0])] + text_sources[1:], [grad_ts, grad_im, grad_tm]
    )
    flown, text_parts, made = together(image_spread.flying(), text_parts, made)
    fresh_te, fresh_ta, fresh_to, fresh_ts, fresh_im, fresh_tm = made
    image_spread.landed(flown)

    text_poly = polynomial(place, text_parts, 2, TRI2)
    more = image_spread.more()
    text_poly, image_spread.own[3] = together(text_poly, more)
    image_sources = image_spread.finish()

    text_spread = Spread(place, text_poly)
    other = place.swap_ns(after(small, text_poly), 1)

    image_weights = apply_polynomials(
        place,
        image_sources,
        (image_expand, image_shrink, image_attention, image_output),
        (fresh_ie, fresh_is, fresh_ia, fresh_io),
        (0, 1, 2, 3),
        True,
    )
    image_weights, flown, other = together(image_weights, text_spread.flying(), other)
    small = small + other
    small = small + place.swap_ns(small, 2)
    for mask in place.extra:
        small = small + place.swap_mask(small, mask)
    next_ie, next_is, next_ia, next_io = image_weights
    text_spread.landed(flown)
    text_spread.more()
    next_te, next_ts, next_ta, next_to, next_im, next_tm = apply_polynomials(
        place,
        text_spread.finish(),
        (
            text_expand,
            text_shrink,
            text_attention,
            text_output,
            image_embedding,
            text_embedding,
        ),
        (fresh_te, fresh_ts, fresh_ta, fresh_to, fresh_im, fresh_tm),
        (0, 1, 2, 3, 4, 5),
        False,
    )
    loss_total, image_gain_sum = small[6, 0], small[:3]
    text_gain_sum = small[3:6, : text_gains.shape[1]]
    image_gain_next = MOMENTUM * image_gains_momentum + image_gain_sum
    text_gain_next = MOMENTUM * text_gains_momentum + text_gain_sum
    loss = jnp.reshape(loss_total / (images * place.n_dp * count), (1,))
    return (
        loss,
        image_token_grad,
        text_token_grad,
        fresh_ia,
        fresh_io,
        fresh_ie,
        fresh_is,
        fresh_im,
        fresh_ta,
        fresh_to,
        fresh_te,
        fresh_ts,
        fresh_tm,
        next_ia,
        next_io,
        next_ie,
        next_is,
        next_im,
        next_ta,
        next_to,
        next_te,
        next_ts,
        next_tm,
        image_gain_next,
        text_gain_next,
        image_gains - GAIN_RATE * image_gain_next,
        text_gains - GAIN_RATE * text_gain_next,
    )


def solution(mesh):
    placed = (
        P(("dp", "ns"), None, None),
        P(("dp", "ns"), None, None),
        P(),
        P(("dp", "ns")),
        P("ns", None),
        P("ns", None),
        P("ns", None),
        P("ns", None),
        P("ns", None),
        P("ns", None),
        P("ns", None),
        P("ns", None),
        P("ns", None),
        P("ns", None),
        P(),
        P(),
        P("ns", None),
        P("ns", None),
        P("ns", None),
        P("ns", None),
        P("ns", None),
        P("ns", None),
        P("ns", None),
        P("ns", None),
        P("ns", None),
        P("ns", None),
        P(),
        P(),
    )
    return jax.shard_map(
        per_device,
        mesh=mesh,
        in_specs=placed,
        out_specs=(
            P(),
            P(("dp", "ns"), None, None),
            P(("dp", "ns"), None, None),
            P("ns", None),
            P("ns", None),
            P("ns", None),
            P("ns", None),
            P("ns", None),
            P("ns", None),
            P("ns", None),
            P("ns", None),
            P("ns", None),
            P("ns", None),
            P("ns", None),
            P("ns", None),
            P("ns", None),
            P("ns", None),
            P("ns", None),
            P("ns", None),
            P("ns", None),
            P("ns", None),
            P("ns", None),
            P("ns", None),
            P(),
            P(),
            P(),
            P(),
        ),
        check_vma=False,
    )
```
